512 devices in a mesh: gx: 4 (over z_hi, core), gy: 4 (over x), gz: 32 (over y, z_lo).
Axes of the slice: x: 4, y: 4, z: 16 (z_hi: 2, z_lo: 8; z = z_hi * 8 + z_lo), core: 2. Of those that a mesh axis runs over, the one named last changes fastest.
Arguments:
- positions: float32 [3, 4, 4, 32, 8192], P(None, 'gx', 'gy', 'gz'), may hold values from 0 to 8
- charges: float32 [4, 4, 32, 8192], P('gx', 'gy', 'gz'), may hold values from -4 to 4
- cluster_tile: int32 [4, 4, 32, 128], P('gx', 'gy', 'gz'), may hold values from 0 to 215
- live_clusters: int32 [4, 4, 32], P('gx', 'gy', 'gz'), may hold values from 42 to 128, as said below
- kernel_blocks: bfloat16 [4, 512, 512], replicated, may hold values from -0.09375 to 0.09375
- restrict_weights: float32 [512], replicated, may hold values from -4 to 4
- top_kernel: float32 [4096, 4096], P('gz', ('gx', 'gy')), may hold values from -0.09375 to 0.09375
Outputs:
- forces: float32 [3, 4, 4, 32, 8192], P(None, 'gx', 'gy', 'gz')
- virial: float32 [6, 4, 4, 32, 8192], P(None, 'gx', 'gy', 'gz')
The draws below stay inside these ranges and needn't reach their ends.
Inputs may be any that keep to these rules, and one draw needn't show every extreme that they name: `cluster_tile`: tiles are numbered (tx 6 + ty) * 6 + tz within a brick. `live_clusters`: some brick has all 128 slots live.
All inputs are finite; a program needn't handle non-finite values.
Results may differ from the reference program's by a relative error of at most 0.0023.
Values may be sent and summed in bfloat16 or wider, within the bound.
No kernel may reach another device: no remote copies, remote signals or barrier semaphores. Data moves between devices by JAX's collectives and lax.ppermute only.
A program may use at most 64 MiB of HBM per device.

```python
import math
import jax
import jax.numpy as jnp
import numpy as np
from jax import lax

TL = 8
TP = 512
CS = 64
TD = 6
CL_DEV = 128
ATOMS_DEV = 8192
G2 = 4096
N_GX = 4
N_GY = 4
N_GZ = 32


def draw_live_clusters(key, part):
    counts = jax.random.randint(key, (N_GX, N_GY, N_GZ), CL_DEV // 3, CL_DEV + 1)
    return counts.at[0, 0, 0].set(CL_DEV).astype(jnp.int32)


def set_ends(drawn, stream_key, smallest, top_value):
    dims = drawn.shape
    place = [jax.random.randint(jax.random.fold_in(stream_key, axis), (), 0, dims[axis]) for axis in range(len(dims))]
    drawn = drawn.at[tuple(place)].set(smallest)
    longest = dims.index(max(dims))
    place[longest] = (place[longest] + 1) % dims[longest]
    return drawn.at[tuple(place)].set(top_value)


def block_levels(key, shape, shards, low, largest):
    level, own = 1.0, jax.random.fold_in(key, 6)
    for axis_at, shards_of in shards:
        draws = jnp.exp(jax.random.uniform(jax.random.fold_in(own, axis_at), (shards_of,), jnp.float32, low / len(shards), largest / len(shards)))
        level = level * jnp.repeat(draws, shape[axis_at] // shards_of).reshape([-1 if axis == axis_at else 1 for axis in range(len(shape))])
    return level


def cumulative_ranks(number_of, slope):
    weights = [(1 << 20) // math.isqrt(grade ** slope) + 1 for grade in range(1, number_of + 1)]
    width = 1 + sum(weights) // (1 << 30)
    return np.cumsum(np.array([max(1, weight // width) for weight in weights]))


def ranked(rng, shape, number_of, lean):
    table = cumulative_ranks(number_of, lean)
    pick = jax.random.randint(jax.random.fold_in(rng, 1), shape, 0, int(table[number_of - 1]))
    grade = jnp.searchsorted(jnp.asarray(table, jnp.int32), pick, side="right")
    return jax.random.permutation(jax.random.fold_in(rng, 2), number_of)[grade].astype(jnp.int32)


def scatter_about(own_key, extent, scale, bound, split=(), held_as=jnp.bfloat16):
    drawn = jax.random.normal(own_key, extent, jnp.float32) * scale
    if len(split) > 0:
        drawn = block_levels(own_key, extent, split, -0.22, 0.18) * drawn
    return jnp.clip(drawn, min=-bound, max=bound).astype(held_as)


def setup_inputs(seed: int = 0) -> dict:
    streams_of = jax.random.split(jax.random.key(seed), 8)
    return {
        "positions": jnp.clip(8.0 * jax.random.uniform(streams_of[0], (3, N_GX, N_GY, N_GZ, ATOMS_DEV), jnp.float32) ** block_levels(streams_of[0], (3, N_GX, N_GY, N_GZ, ATOMS_DEV), ((1, 4), (2, 4), (3, 32)), -0.2, 0.2), 0.0, 8.0),
        "charges": scatter_about(streams_of[1], (N_GX, N_GY, N_GZ, ATOMS_DEV), 1.0, 4.0, ((0, 4), (1, 4), (2, 32)), jnp.float32),
        "cluster_tile": set_ends(ranked(streams_of[2], (N_GX, N_GY, N_GZ, CL_DEV), TD ** 3, 1), jax.random.fold_in(streams_of[2], 3), 0, (TD ** 3) - 1).astype(jnp.int32),
        "live_clusters": draw_live_clusters(jax.random.fold_in(streams_of[7], 71), 0),
        "kernel_blocks": scatter_about(streams_of[4], (4, TP, TP), (7 * TL ** 3) ** -0.5, 0.09375),
        "restrict_weights": scatter_about(streams_of[5], (TP,), 1.0, 4.0, (), jnp.float32),
        "top_kernel": scatter_about(streams_of[6], (G2, G2), G2 ** -0.5, 0.09375, ((0, 32), (1, 16)), jnp.float32),
    }


HIGHEST_PRECISION = lax.Precision.HIGHEST

def bump_weights(coord, tile_edge):
    grid_nodes = jnp.arange(tile_edge, dtype=jnp.float32).reshape((tile_edge,) + (1,) * coord.ndim)
    offset = coord[None] - grid_nodes
    weight = jnp.exp(-0.5 * offset * offset)
    return (weight, -offset * weight)

def spread(coords, charge_live, onehot, tile_edge):
    weight_x = bump_weights(coords[0], tile_edge)[0]
    weight_y = bump_weights(coords[1], tile_edge)[0]
    weight_z = bump_weights(coords[2], tile_edge)[0]
    plane_weights = (charge_live[None] * weight_x)[:, None] * weight_y[None]
    cluster_cells = jnp.einsum('ijcn,kcn->cijk', plane_weights, weight_z, precision=HIGHEST_PRECISION)
    cluster_cells = cluster_cells.reshape(cluster_cells.shape[0], -1)
    return jnp.einsum('ct,cp->tp', onehot, cluster_cells, precision=HIGHEST_PRECISION)

def prolong(potential, coarse_pot, restrict_weights, tile_count):
    half_tiles = tile_count // 2
    spread_pot = jnp.broadcast_to(coarse_pot.reshape(2, 1, 2, 1, 2, 1, 1), (2, half_tiles, 2, half_tiles, 2, half_tiles, 1))
    return potential + spread_pot.reshape(-1, 1) * restrict_weights[None]

def forces_virial(full_field, tile_ids, coords, charge_live, tile_edge, tile_count):
    weight_x, slope_x = bump_weights(coords[0], tile_edge)
    weight_y, slope_y = bump_weights(coords[1], tile_edge)
    weight_z, slope_z = bump_weights(coords[2], tile_edge)
    cluster_field = jnp.take(full_field, tile_ids, axis=0).reshape(-1, tile_edge, tile_edge, tile_edge)
    field_z = jnp.einsum('cijk,kcn->ijcn', cluster_field, weight_z, precision=HIGHEST_PRECISION)
    field_dz = jnp.einsum('cijk,kcn->ijcn', cluster_field, slope_z, precision=HIGHEST_PRECISION)
    grad_x = lax.optimization_barrier(jnp.sum(slope_x[:, None] * weight_y[None] * field_z, axis=(0, 1)))
    grad_y = lax.optimization_barrier(jnp.sum(weight_x[:, None] * slope_y[None] * field_z, axis=(0, 1)))
    grad_z = lax.optimization_barrier(jnp.sum(weight_x[:, None] * weight_y[None] * field_dz, axis=(0, 1)))
    forces = -charge_live[None] * jnp.stack([grad_x, grad_y, grad_z])
    tile_x = tile_ids // (tile_count * tile_count)
    tile_y = tile_ids // tile_count % tile_count
    tile_z = tile_ids % tile_count
    anchor = jnp.stack([tile_x, tile_y, tile_z]).astype(coords.dtype)[:, :, None] * tile_edge
    brick_frac = (anchor + coords) / (tile_edge * tile_count)
    virial = jnp.stack([brick_frac[0] * forces[0], brick_frac[1] * forces[1], brick_frac[2] * forces[2], brick_frac[0] * forces[1], brick_frac[0] * forces[2], brick_frac[1] * forces[2]])
    return (forces, virial)

def apply_exact(rows, block, flipped):
    contract_dims = ((1,), (0,)) if flipped else ((1,), (1,))
    return lax.dot_general(rows, block, (contract_dims, ((), ())), precision=HIGHEST_PRECISION)

def reference(positions, charges, cluster_tile, live_clusters, kernel_blocks, restrict_weights, top_kernel):
    bricks = N_GX * N_GY * N_GZ
    tile_points = TL ** 3
    cubes = TD ** 3
    half_tiles = TD // 2
    brick_coords = jnp.moveaxis(positions, 0, 3).reshape(bricks, 3, CL_DEV, CS)
    brick_charges = charges.reshape(bricks, CL_DEV, CS)
    brick_tiles = cluster_tile.reshape(bricks, CL_DEV)
    brick_live = live_clusters.reshape(bricks)
    tile_range = jnp.arange(cubes, dtype=jnp.int32)
    cluster_range = jnp.arange(CL_DEV, dtype=jnp.int32)

    def charge_brick(item):
        coords, charge_rows, tile_ids, live_count = item
        alive_mask = cluster_range < live_count
        onehot = ((tile_ids[:, None] == tile_range[None]) & alive_mask[:, None]).astype(jnp.float32)
        charge_live = charge_rows * alive_mask[:, None].astype(jnp.float32)
        return spread(coords, charge_live, onehot, TL)
    fine_charge = lax.map(charge_brick, (brick_coords, brick_charges, brick_tiles, brick_live))
    moments = jnp.einsum('btp,p->bt', fine_charge, restrict_weights, precision=HIGHEST_PRECISION)
    coarse = moments.reshape(bricks, 2, half_tiles, 2, half_tiles, 2, half_tiles).sum(axis=(2, 4, 6))
    coarse = coarse.reshape(bricks * 8) / math.sqrt(tile_points * half_tiles ** 3)
    coarse_rows = jnp.dot(top_kernel, coarse, precision=HIGHEST_PRECISION)
    coarse_pot = coarse_rows.reshape(N_GZ, N_GX, N_GY, 8).transpose(1, 2, 0, 3).reshape(bricks, 8)
    grid_bf = fine_charge.astype(jnp.bfloat16).reshape(N_GX, N_GY, N_GZ, TD, TD, TD, tile_points)
    grid_bf = grid_bf.transpose(0, 3, 1, 4, 2, 5, 6).reshape(N_GX * TD, N_GY * TD, N_GZ * TD, tile_points)
    kernel_full = kernel_blocks.astype(jnp.float32)
    span_x = N_GX * TD

    def as_rows(view):
        return view.reshape(-1, tile_points).astype(jnp.float32)

    def slab_field(slab_index):
        centre_slab = lax.dynamic_index_in_dim(grid_bf, slab_index, 0, keepdims=False)
        upper_slab = lax.dynamic_index_in_dim(grid_bf, (slab_index + 1) % span_x, 0, keepdims=False)
        lower_slab = lax.dynamic_index_in_dim(grid_bf, (slab_index + span_x - 1) % span_x, 0, keepdims=False)
        potential = apply_exact(as_rows(centre_slab), kernel_full[0], False)
        potential = potential + apply_exact(as_rows(upper_slab), kernel_full[1], False)
        potential = potential + apply_exact(as_rows(lower_slab), kernel_full[1], True)
        potential = potential + apply_exact(as_rows(jnp.roll(centre_slab, -1, axis=0)), kernel_full[2], False)
        potential = potential + apply_exact(as_rows(jnp.roll(centre_slab, 1, axis=0)), kernel_full[2], True)
        potential = potential + apply_exact(as_rows(jnp.roll(centre_slab, -1, axis=1)), kernel_full[3], False)
        potential = potential + apply_exact(as_rows(jnp.roll(centre_slab, 1, axis=1)), kernel_full[3], True)
        return potential.reshape(N_GY * TD, N_GZ * TD, tile_points)
    near_pot = lax.map(slab_field, jnp.arange(span_x, dtype=jnp.int32))
    near_pot = near_pot.reshape(N_GX, TD, N_GY, TD, N_GZ, TD, tile_points).transpose(0, 2, 4, 1, 3, 5, 6)
    near_pot = near_pot.reshape(bricks, cubes, tile_points)

    def atom_brick(item):
        coords, charge_rows, tile_ids, live_count, near_field, coarse_row = item
        alive_mask = cluster_range < live_count
        charge_live = charge_rows * alive_mask[:, None].astype(jnp.float32)
        full_field = prolong(near_field, coarse_row, restrict_weights, TD)
        return forces_virial(full_field, tile_ids, coords, charge_live, TL, TD)
    forces, virial = lax.map(atom_brick, (brick_coords, brick_charges, brick_tiles, brick_live, near_pot, coarse_pot))
    forces = jnp.moveaxis(forces.reshape(N_GX, N_GY, N_GZ, 3, CL_DEV * CS), 3, 0)
    virial = jnp.moveaxis(virial.reshape(N_GX, N_GY, N_GZ, 6, CL_DEV * CS), 3, 0)
    return (forces, virial)
```

```python
import math

import jax
import jax.numpy as jnp
from jax import lax
from jax.sharding import PartitionSpec as P

TL = 8
CS = 64
TD = 6
CL_DEV = 128


HIGHEST_PRECISION = lax.Precision.HIGHEST


def shifted(value, axis, steps):
    count = lax.axis_size(axis)
    pairs = [(source, (source + steps) % count) for source in range(count)]
    return lax.ppermute(value, axis, pairs)


def bump_weights(coord, tile_edge):
    grid_nodes = jnp.arange(tile_edge, dtype=jnp.float32).reshape((tile_edge,) + (1,) * coord.ndim)
    offset = coord[None] - grid_nodes
    weight = jnp.exp(-0.5 * offset * offset)
    return (weight, -offset * weight)


def spread(coords, charge_live, onehot, tile_edge):
    weight_x = bump_weights(coords[0], tile_edge)[0]
    weight_y = bump_weights(coords[1], tile_edge)[0]
    weight_z = bump_weights(coords[2], tile_edge)[0]
    plane_weights = (charge_live[None] * weight_x)[:, None] * weight_y[None]
    cluster_cells = jnp.einsum(
        "ijcn,kcn->cijk", plane_weights, weight_z, precision=HIGHEST_PRECISION
    )
    cluster_cells = cluster_cells.reshape(cluster_cells.shape[0], -1)
    return jnp.einsum("ct,cp->tp", onehot, cluster_cells, precision=HIGHEST_PRECISION)


def prolong(potential, coarse_pot, restrict_weights, tile_count):
    half_tiles = tile_count // 2
    spread_pot = jnp.broadcast_to(
        coarse_pot.reshape(2, 1, 2, 1, 2, 1, 1), (2, half_tiles, 2, half_tiles, 2, half_tiles, 1)
    )
    return potential + spread_pot.reshape(-1, 1) * restrict_weights[None]


def forces_virial(full_field, tile_ids, coords, charge_live, tile_edge, tile_count):
    weight_x, slope_x = bump_weights(coords[0], tile_edge)
    weight_y, slope_y = bump_weights(coords[1], tile_edge)
    weight_z, slope_z = bump_weights(coords[2], tile_edge)
    cluster_field = jnp.take(full_field, tile_ids, axis=0).reshape(
        -1, tile_edge, tile_edge, tile_edge
    )
    field_z = jnp.einsum("cijk,kcn->ijcn", cluster_field, weight_z, precision=HIGHEST_PRECISION)
    field_dz = jnp.einsum("cijk,kcn->ijcn", cluster_field, slope_z, precision=HIGHEST_PRECISION)
    grad_x = jnp.sum(slope_x[:, None] * weight_y[None] * field_z, axis=(0, 1))
    grad_y = jnp.sum(weight_x[:, None] * slope_y[None] * field_z, axis=(0, 1))
    grad_z = jnp.sum(weight_x[:, None] * weight_y[None] * field_dz, axis=(0, 1))
    forces = -charge_live[None] * jnp.stack([grad_x, grad_y, grad_z])
    tile_x = tile_ids // (tile_count * tile_count)
    tile_y = tile_ids // tile_count % tile_count
    tile_z = tile_ids % tile_count
    anchor = jnp.stack([tile_x, tile_y, tile_z]).astype(coords.dtype)[:, :, None] * tile_edge
    brick_frac = (anchor + coords) / (tile_edge * tile_count)
    virial = jnp.stack(
        [
            brick_frac[0] * forces[0],
            brick_frac[1] * forces[1],
            brick_frac[2] * forces[2],
            brick_frac[0] * forces[1],
            brick_frac[0] * forces[2],
            brick_frac[1] * forces[2],
        ]
    )
    return (forces, virial)


def apply_block(rows, block, flipped):
    contract_dims = ((1,), (0,)) if flipped else ((1,), (1,))
    return lax.dot_general(
        rows, block, (contract_dims, ((), ())), preferred_element_type=jnp.float32
    )


def as_rows(view):
    return view.reshape(-1, view.shape[-1])


def face_field(grid_bf, kernel_blocks):
    upper_x = shifted(grid_bf[0], "gx", -1)
    lower_x = shifted(grid_bf[-1], "gx", 1)
    upper_y = shifted(grid_bf[:, 0], "gy", -1)
    lower_y = shifted(grid_bf[:, -1], "gy", 1)
    upper_z = shifted(grid_bf[:, :, 0], "gz", -1)
    lower_z = shifted(grid_bf[:, :, -1], "gz", 1)
    next_x = jnp.concatenate([grid_bf[1:], upper_x[None]], axis=0)
    prev_x = jnp.concatenate([lower_x[None], grid_bf[:-1]], axis=0)
    next_y = jnp.concatenate([grid_bf[:, 1:], upper_y[:, None]], axis=1)
    prev_y = jnp.concatenate([lower_y[:, None], grid_bf[:, :-1]], axis=1)
    next_z = jnp.concatenate([grid_bf[:, :, 1:], upper_z[:, :, None]], axis=2)
    prev_z = jnp.concatenate([lower_z[:, :, None], grid_bf[:, :, :-1]], axis=2)
    potential = apply_block(as_rows(grid_bf), kernel_blocks[0], False)
    potential = potential + apply_block(as_rows(next_x), kernel_blocks[1], False)
    potential = potential + apply_block(as_rows(prev_x), kernel_blocks[1], True)
    potential = potential + apply_block(as_rows(next_y), kernel_blocks[2], False)
    potential = potential + apply_block(as_rows(prev_y), kernel_blocks[2], True)
    potential = potential + apply_block(as_rows(next_z), kernel_blocks[3], False)
    potential = potential + apply_block(as_rows(prev_z), kernel_blocks[3], True)
    return potential


def level_one(grid_bf, kernel_blocks):
    return face_field(grid_bf, kernel_blocks)


def coarse_field(fine_charge, restrict_weights, top_kernel):
    half_tiles = TD // 2
    tile_points = restrict_weights.shape[0]
    moments = jnp.dot(fine_charge, restrict_weights, precision=HIGHEST_PRECISION)
    coarse = (
        moments.reshape(2, half_tiles, 2, half_tiles, 2, half_tiles).sum(axis=(1, 3, 5)).reshape(8)
    )
    coarse = coarse / math.sqrt(tile_points * half_tiles**3)
    lines = lax.axis_size("gz")
    column = lax.all_to_all(jnp.broadcast_to(coarse[None], (lines, 8)), "gz", 0, 0, tiled=True)
    column = column.reshape(lines * 8)
    partial_value = jnp.dot(top_kernel, column, precision=HIGHEST_PRECISION)
    parts = lax.all_to_all(partial_value.reshape(-1, 8), ("gx", "gy"), 0, 0, tiled=True)
    return parts.sum(axis=0)


def shards(
    positions, charges, cluster_tile, live_clusters, kernel_blocks, restrict_weights, top_kernel
):
    tile_points = TL**3
    cubes = TD**3
    coords = positions.reshape(3, CL_DEV, CS)
    charge_rows = charges.reshape(CL_DEV, CS)
    tile_ids = cluster_tile.reshape(CL_DEV)
    alive_mask = jnp.arange(CL_DEV, dtype=jnp.int32) < live_clusters.reshape(())
    onehot = (
        (tile_ids[:, None] == jnp.arange(cubes, dtype=jnp.int32)[None]) & alive_mask[:, None]
    ).astype(jnp.float32)
    charge_live = charge_rows * alive_mask[:, None].astype(jnp.float32)
    fine_charge = spread(coords, charge_live, onehot, TL)
    grid_bf = fine_charge.astype(jnp.bfloat16).reshape(TD, TD, TD, tile_points)
    near_pot = level_one(grid_bf, kernel_blocks)
    coarse_pot = coarse_field(fine_charge, restrict_weights, top_kernel)
    full_field = prolong(near_pot, coarse_pot, restrict_weights, TD)
    forces, virial = forces_virial(full_field, tile_ids, coords, charge_live, TL, TD)
    return (forces.reshape(3, 1, 1, 1, -1), virial.reshape(6, 1, 1, 1, -1))


def solution(mesh):
    placed = (
        P(None, "gx", "gy", "gz", None),
        P("gx", "gy", "gz", None),
        P("gx", "gy", "gz", None),
        P("gx", "gy", "gz"),
        P(),
        P(),
        P("gz", ("gx", "gy")),
    )
    return jax.shard_map(
        shards,
        mesh=mesh,
        in_specs=placed,
        out_specs=(P(None, "gx", "gy", "gz", None), P(None, "gx", "gy", "gz", None)),
        check_vma=False,
    )
```

```python
import math

import jax
import jax.numpy as jnp
from jax import lax
from jax.experimental import pallas as pl
from jax.experimental.pallas import tpu as pltpu
from jax.sharding import PartitionSpec as P

TL = 8
TP = 512
CS = 64
TD = 6
CUBES = TD**3
FACE = 48
GRID_ROWS = 256
EXT_ROWS = 640
HALF = CS
LANES = 128


def iota(shape, axis):
    return lax.broadcasted_iota(jnp.int32, shape, axis)


def tile_coords(tile):
    plane = (tile * 10923) >> 16
    tx = (tile * 1821) >> 16
    return tx, plane - tx * TD, tile - plane * TD


def to_clusters(upper, lower):
    both = jnp.concatenate([upper, lower], axis=0).T
    even, odd = both[:HALF], both[HALF:]
    left = iota((HALF, LANES), 1) < HALF
    return (
        jnp.where(left, even, pltpu.roll(odd, HALF, 1)),
        jnp.where(left, pltpu.roll(even, HALF, 1), odd),
    )


def to_atoms(upper, lower):
    left = iota((HALF, LANES), 1) < HALF
    even = jnp.where(left, upper, pltpu.roll(lower, HALF, 1))
    odd = jnp.where(left, pltpu.roll(upper, HALF, 1), lower)
    both = jnp.concatenate([even, odd], axis=0).T
    return both[:HALF], both[HALF:]


def bump(offset):
    return jnp.exp(-0.5 * offset * offset)


def face_tile(face, row):
    if face < 2:
        tile = row + face * 180
    elif face < 4:
        line = (row * 10923) >> 16
        tile = line * 36 + (row - line * TD) + (face - 2) * 30
    else:
        tile = row * TD + (face - 4) * 5
    return jnp.where(row < TD * TD, tile, -1)


def spread_kernel(
    live_ref, pos_ref, charge_ref, tile_ref, weights_ref,
    grid_ref, face_x_ref, face_y_ref, low_z_ref, high_z_ref, coarse_ref, coord_ref, tiles_ref, charge_out_ref,
    wx_ref, wy_ref, wz_ref, cell_ref,
):
    cluster = 2 * iota((HALF, LANES), 0) + (iota((HALF, LANES), 1) >> 6)
    charge = charge_ref[...] * (cluster < live_ref[0, 0]).astype(jnp.float32)
    charge_out_ref[...] = charge
    x, y = to_clusters(pos_ref[0], pos_ref[1])
    z, q = to_clusters(pos_ref[2], charge)
    coord_ref[0], coord_ref[1], coord_ref[2] = x, y, z
    for node in range(TL):
        wx_ref[node] = q * bump(x - node)
        wy_ref[node] = bump(y - node)
    nodes = iota((TL, LANES), 0).astype(jnp.float32)
    for atom in range(CS):
        wz_ref[atom] = bump(z[atom : atom + 1] - nodes)

    own = iota((LANES, LANES), 0)
    at = iota((LANES, LANES), 1)
    order = (own == jnp.where(at < HALF, 2 * at, 2 * at - 127)).astype(jnp.bfloat16)
    ids = jnp.broadcast_to(tile_ref[...].astype(jnp.float32), (8, LANES)).astype(jnp.bfloat16)
    tiles = jnp.dot(ids, order, preferred_element_type=jnp.float32)
    tiles_ref[...] = tiles
    tiles = tiles[:1].astype(jnp.int32)

    for half in range(2):

        def step(atom, total, half=half):
            row = pl.ds(atom, 1)
            wz = wz_ref[atom]
            line = [wy_ref[j, row, :] * wz for j in range(TL)]
            new = []
            for i in range(4):
                wx = jnp.broadcast_to(wx_ref[4 * half + i, row, :], (TL, LANES))
                new += [total[8 * i + j] + wx * line[j] for j in range(TL)]
            return tuple(new)

        start = tuple(jnp.zeros((TL, LANES), jnp.float32) for _ in range(32))
        total = lax.fori_loop(0, CS, step, start, unroll=4)
        for slot in range(32):
            cell_ref[pl.ds((32 * half + slot) * TL, TL), :] = total[slot]

    cell = cell_ref[...]
    high = cell.astype(jnp.bfloat16)
    low = (cell - high.astype(jnp.float32)).astype(jnp.bfloat16)
    cells = jnp.concatenate([high, low], axis=1)

    def gathered(rows_tile):
        hot = (rows_tile == tiles).astype(jnp.bfloat16)
        return lax.dot_general(
            jnp.concatenate([hot, hot], axis=1), cells, (((1,), (1,)), ((), ())), preferred_element_type=jnp.float32
        )

    fine = gathered(iota((GRID_ROWS, LANES), 0))
    grid_ref[...] = fine.astype(jnp.bfloat16)
    faces = gathered(jnp.concatenate([face_tile(f, iota((FACE, LANES), 0)) for f in range(6)], axis=0))
    faces = faces.astype(jnp.bfloat16)
    low_z_ref[...] = faces[4 * FACE : 5 * FACE]
    high_z_ref[...] = faces[5 * FACE :]
    for ref, axis, first in ((face_x_ref, "gx", 0), (face_y_ref, "gy", 2)):
        me, count = lax.axis_index(axis), lax.axis_size(axis)
        ref[lax.rem(me + count - 1, count)] = faces[first * FACE : (first + 1) * FACE]
        ref[lax.rem(me + 1, count)] = faces[(first + 1) * FACE : (first + 2) * FACE]

    moments = jnp.sum(fine * weights_ref[...], axis=1, keepdims=True)
    tx, ty, tz = tile_coords(iota((GRID_ROWS, LANES), 0))
    corner = ((tx >= 3).astype(jnp.int32) * 2 + (ty >= 3).astype(jnp.int32)) * 2 + (tz >= 3).astype(jnp.int32)
    mine = corner == (iota((GRID_ROWS, LANES), 1) & 7)
    coarse = jnp.sum(jnp.where(mine, moments, 0.0), axis=0, keepdims=True)
    coarse = coarse * (1.0 / math.sqrt(TP * 27))
    for line in range(coarse_ref.shape[0]):
        coarse_ref[line] = coarse


def coarse_kernel(column_ref, top_ref, out_ref):
    lines = column_ref.shape[0]
    column = column_ref[...].reshape(lines, LANES)
    column = jnp.concatenate([column] * (lines * 8 // LANES), axis=1)
    shape = column.shape
    column = jnp.sum(jnp.where((iota(shape, 1) >> 3) == iota(shape, 0), column, 0.0), axis=0, keepdims=True)
    partial_value = jnp.sum(top_ref[...] * column, axis=1, keepdims=True)
    rows = partial_value.shape[0]
    lanes = jnp.where((iota((rows, LANES), 1) & 7) == (iota((rows, LANES), 0) & 7), partial_value, 0.0)
    lanes = jnp.sum(lanes.reshape(rows // 8, 8, LANES), axis=1)
    for brick in range(rows // 8):
        out_ref[brick] = lanes[brick : brick + 1]


ATOM_ROWS = 16


def gradients(field_ref, wx, wy, wz, x, y, z):
    sums = [None] * 4
    for i in reversed(range(TL)):
        a = b = c = None
        for j in reversed(range(TL)):
            run = mean = None
            for k in reversed(range(TL)):
                term = wz[k] * field_ref[(i * TL + j) * TL + k : (i * TL + j) * TL + k + 1, :]
                run = term if run is None else run + term
                if k:
                    mean = run if mean is None else mean + run
            part = wy[j] * run
            cross = wy[j] * mean
            a = part if a is None else a + part
            c = cross if c is None else c + cross
            if j:
                b = a if b is None else b + a
        for at, value in enumerate((a, b, c)):
            term = wx[i] * value
            sums[at] = term if sums[at] is None else sums[at] + term
        if i:
            sums[3] = sums[0] if sums[3] is None else sums[3] + sums[0]
    total, with_y, with_z, with_x = sums
    return with_x - x * total, with_y - y * total, with_z - z * total


def near_kernel(
    tiles_ref, grid_ref, face_x_ref, face_y_ref, up_z_ref, down_z_ref, blocks_ref, coord_ref, weights_ref,
    near_ref, unit_ref,
    ext_ref, field_ref, flat_ref, grad_ref,
):
    ext_ref[0:GRID_ROWS] = grid_ref[...]
    faces = []
    for ref, axis in ((face_x_ref, "gx"), (face_y_ref, "gy")):
        me, count = lax.axis_index(axis), lax.axis_size(axis)
        faces += [ref[lax.rem(me + 1, count)], ref[lax.rem(me + count - 1, count)]]
    faces += [up_z_ref[...], down_z_ref[...]]
    for at, face in enumerate(faces):
        ext_ref[GRID_ROWS + at * FACE : GRID_ROWS + (at + 1) * FACE] = face
    ext_ref[GRID_ROWS + 6 * FACE :] = jnp.zeros((EXT_ROWS - GRID_ROWS - 6 * FACE, TP), jnp.bfloat16)

    tile = jnp.broadcast_to(tiles_ref[:1], (LANES, LANES)).T[:, :1].astype(jnp.int32)
    tx, ty, tz = tile_coords(tile)
    edges = ((tx, 36, ty * TD + tz), (ty, TD, tx * TD + tz), (tz, 1, tx * TD + ty))
    targets = [tile]
    for at, (place, stride, row) in enumerate(edges):
        base = GRID_ROWS + 2 * at * FACE
        targets.append(jnp.where(place < TD - 1, tile + stride, base + row))
        targets.append(jnp.where(place > 0, tile - stride, base + FACE + row))
    at_row = iota((LANES, EXT_ROWS), 1)
    field = None
    for at, target in enumerate(targets):
        hot = (at_row == target).astype(jnp.bfloat16)
        rows = jnp.dot(hot, ext_ref[...], preferred_element_type=jnp.float32).astype(jnp.bfloat16)
        flipped = at > 0 and at % 2 == 0
        term = lax.dot_general(
            rows, blocks_ref[(at + 1) // 2], (((1,), (0 if flipped else 1,)), ((), ())), preferred_element_type=jnp.float32
        )
        field = term if field is None else field + term
    for part in range(TP // LANES):
        field_ref[part * LANES : (part + 1) * LANES, :] = field[:, part * LANES : (part + 1) * LANES].T
        flat_ref[part * LANES : (part + 1) * LANES, :] = jnp.broadcast_to(
            weights_ref[:, part * LANES : (part + 1) * LANES], (LANES, LANES)
        ).T

    @pl.loop(0, CS // ATOM_ROWS)
    def _(group):
        rows = pl.ds(pl.multiple_of(group * ATOM_ROWS, ATOM_ROWS), ATOM_ROWS)
        x, y, z = coord_ref[0, rows, :], coord_ref[1, rows, :], coord_ref[2, rows, :]
        wx, wy, wz = ([bump(u - node) for node in range(TL)] for u in (x, y, z))
        for which, ref in enumerate((field_ref, flat_ref)):
            for axis, value in enumerate(gradients(ref, wx, wy, wz, x, y, z)):
                grad_ref[3 * which + axis, rows, :] = value

    near_ref[0], near_ref[1] = to_atoms(grad_ref[0], grad_ref[1])
    near_ref[2], unit_ref[0] = to_atoms(grad_ref[2], grad_ref[3])
    unit_ref[1], unit_ref[2] = to_atoms(grad_ref[4], grad_ref[5])


def final_kernel(parts_ref, tile_ref, near_ref, unit_ref, pos_ref, charge_ref, force_ref, virial_ref):
    bricks = parts_ref.shape[0]
    coarse = jnp.sum(parts_ref[...].reshape(bricks, LANES), axis=0, keepdims=True)
    tile_row = tile_ref[...].astype(jnp.float32)
    mine = ((iota((HALF, LANES), 1) >> 1) == iota((HALF, LANES), 0))
    rows = jnp.where(mine, tile_row, 0.0).astype(jnp.bfloat16)
    side = ((iota((LANES, LANES), 0) & 1) == (iota((LANES, LANES), 1) >> 6)).astype(jnp.bfloat16)
    tile = jnp.dot(rows, side, preferred_element_type=jnp.float32).astype(jnp.int32)
    coords = tile_coords(tile)
    corner = jnp.zeros((HALF, LANES), jnp.int32)
    for place in coords:
        corner = corner * 2 + (place >= 3).astype(jnp.int32)
    pot = jnp.zeros((HALF, LANES), jnp.float32)
    for at in range(8):
        pot = jnp.where(corner == at, coarse[:, at : at + 1], pot)
    charge = charge_ref[...]
    forces, fracs = [], []
    for axis in range(3):
        forces.append(-charge * (near_ref[axis] + pot * unit_ref[axis]))
        fracs.append((coords[axis].astype(jnp.float32) * TL + pos_ref[axis]) * (1.0 / (TL * TD)))
        force_ref[axis] = forces[axis]
        virial_ref[axis] = fracs[axis] * forces[axis]
    virial_ref[3] = fracs[0] * forces[1]
    virial_ref[4] = fracs[0] * forces[2]
    virial_ref[5] = fracs[1] * forces[2]


VMEM = pl.BlockSpec(memory_space=pltpu.VMEM)
SMEM = pl.BlockSpec(memory_space=pltpu.SMEM)


def f32(*shape):
    return jax.ShapeDtypeStruct(shape, jnp.float32)


def bf16(*shape):
    return jax.ShapeDtypeStruct(shape, jnp.bfloat16)


def shifted(value, axis, steps):
    count = lax.axis_size(axis)
    return lax.ppermute(value, axis, [(source, (source + steps) % count) for source in range(count)])


def shards(positions, charges, cluster_tile, live_clusters, kernel_blocks, restrict_weights, top_kernel):
    pos = positions.reshape(3, HALF, LANES)
    charge = charges.reshape(HALF, LANES)
    tile = cluster_tile.reshape(1, LANES)
    live = live_clusters.reshape(1, 1)
    weights = restrict_weights.reshape(1, TP)
    lines, wide, high = lax.axis_size("gz"), lax.axis_size("gx"), lax.axis_size("gy")

    grid, face_x, face_y, low_z, high_z, coarse, coords, tiles, charge = pl.pallas_call(
        spread_kernel,
        out_shape=(
            bf16(GRID_ROWS, TP), bf16(wide, FACE, TP), bf16(high, FACE, TP), bf16(FACE, TP), bf16(FACE, TP),
            f32(lines, 1, LANES), f32(3, CS, LANES), f32(8, LANES), f32(HALF, LANES),
        ),
        in_specs=[SMEM] + [VMEM] * 4,
        out_specs=[VMEM] * 9,
        scratch_shapes=[
            pltpu.VMEM((TL, CS, LANES), jnp.float32), pltpu.VMEM((TL, CS, LANES), jnp.float32),
            pltpu.VMEM((CS, TL, LANES), jnp.float32), pltpu.VMEM((TP, LANES), jnp.float32),
        ],
        compiler_params=pltpu.CompilerParams(vmem_limit_bytes=16 << 20),
        cost_estimate=pl.CostEstimate(flops=10_000_000, bytes_accessed=1_000_000, transcendentals=200_000),
        name="spread",
    )(live, pos, charge, tile, weights)

    column = lax.all_to_all(coarse, "gz", 0, 0, tiled=True)
    face_x = lax.all_to_all(face_x, "gx", 0, 0, tiled=True)
    face_y = lax.all_to_all(face_y, "gy", 0, 0, tiled=True)
    up_z = shifted(low_z, "gz", -1)
    down_z = shifted(high_z, "gz", 1)

    parts = pl.pallas_call(
        coarse_kernel,
        out_shape=f32(wide * high, 1, LANES),
        in_specs=[VMEM] * 2,
        out_specs=VMEM,
        cost_estimate=pl.CostEstimate(flops=70_000, bytes_accessed=200_000, transcendentals=0),
        name="coarse",
    )(column, top_kernel)
    parts = lax.all_to_all(parts, ("gx", "gy"), 0, 0, tiled=True)

    near, unit = pl.pallas_call(
        near_kernel,
        out_shape=(f32(3, HALF, LANES), f32(3, HALF, LANES)),
        in_specs=[VMEM] * 9,
        out_specs=[VMEM] * 2,
        scratch_shapes=[
            pltpu.VMEM((EXT_ROWS, TP), jnp.bfloat16), pltpu.VMEM((TP, LANES), jnp.float32),
            pltpu.VMEM((TP, LANES), jnp.float32), pltpu.VMEM((6, CS, LANES), jnp.float32),
        ],
        compiler_params=pltpu.CompilerParams(vmem_limit_bytes=24 << 20),
        cost_estimate=pl.CostEstimate(flops=1_000_000_000, bytes_accessed=4_000_000, transcendentals=200_000),
        name="near",
    )(tiles, grid, face_x, face_y, up_z, down_z, kernel_blocks, coords, weights)

    forces, virial = pl.pallas_call(
        final_kernel,
        out_shape=(f32(3, HALF, LANES), f32(6, HALF, LANES)),
        in_specs=[VMEM] * 6,
        out_specs=[VMEM] * 2,
        cost_estimate=pl.CostEstimate(flops=500_000, bytes_accessed=600_000, transcendentals=0),
        name="final",
    )(parts, tile, near, unit, pos, charge)
    return forces.reshape(3, 1, 1, 1, -1), virial.reshape(6, 1, 1, 1, -1)


def solution(mesh):
    placed = (
        P(None, "gx", "gy", "gz", None),
        P("gx", "gy", "gz", None),
        P("gx", "gy", "gz", None),
        P("gx", "gy", "gz"),
        P(),
        P(),
        P("gz", ("gx", "gy")),
    )
    return jax.shard_map(
        shards,
        mesh=mesh,
        in_specs=placed,
        out_specs=(P(None, "gx", "gy", "gz", None), P(None, "gx", "gy", "gz", None)),
        check_vma=False,
    )
```

```python
import math

import jax
import jax.numpy as jnp
from jax import lax
from jax.experimental import pallas as pl
from jax.experimental.pallas import tpu as pltpu
from jax.sharding import PartitionSpec as P

TL = 8
TP = 512
CS = 64
TD = 6
CUBES = TD**3
FACE = 48
GRID_ROWS = 256
EXT_ROWS = 640
HALF = CS
LANES = 128


def iota(shape, axis):
    return lax.broadcasted_iota(jnp.int32, shape, axis)


def tile_coords(tile):
    plane = (tile * 10923) >> 16
    tx = (tile * 1821) >> 16
    return tx, plane - tx * TD, tile - plane * TD


def to_clusters(upper, lower):
    both = jnp.concatenate([upper, lower], axis=0).T
    even, odd = both[:HALF], both[HALF:]
    left = iota((HALF, LANES), 1) < HALF
    return (
        jnp.where(left, even, pltpu.roll(odd, HALF, 1)),
        jnp.where(left, pltpu.roll(even, HALF, 1), odd),
    )


def to_atoms(upper, lower):
    left = iota((HALF, LANES), 1) < HALF
    even = jnp.where(left, upper, pltpu.roll(lower, HALF, 1))
    odd = jnp.where(left, pltpu.roll(upper, HALF, 1), lower)
    both = jnp.concatenate([even, odd], axis=0).T
    return both[:HALF], both[HALF:]


def corner_of(places):
    tx, ty, tz = ((place >= TD // 2).astype(jnp.int32) for place in places)
    return (tx * 2 + ty) * 2 + tz


def bump(offset):
    return jnp.exp(-0.5 * offset * offset)


def spread_kernel(
    live_ref, pos_any, charge_any, tile_any, weights_any, blocks_any, top_any,
    grid_ref, coarse_ref, coord_ref, tiles_ref, drive_ref, frac_ref, corner_ref, weights_ref, blocks_ref, top_ref,
    pos_ref, charge_ref, tile_ref, wx_ref, wy_ref, wz_ref, cell_ref, sems,
):
    moves = [
        pltpu.make_async_copy(source, target, sems.at[at])
        for at, (source, target) in enumerate(
            (
                (pos_any, pos_ref), (charge_any, charge_ref), (tile_any, tile_ref),
                (weights_any, weights_ref), (blocks_any, blocks_ref), (top_any, top_ref),
            )
        )
    ]
    for move in moves:
        move.start()
    for move in moves[:3]:
        move.wait()
    cluster = 2 * iota((HALF, LANES), 0) + (iota((HALF, LANES), 1) >> 6)
    charge = charge_ref[...] * (cluster < live_ref[0, 0]).astype(jnp.float32)
    x, y = to_clusters(pos_ref[0], pos_ref[1])
    z, q = to_clusters(pos_ref[2], charge)
    coord_ref[0], coord_ref[1], coord_ref[2] = x, y, z
    for node in range(TL):
        wx_ref[node] = q * bump(x - node)
        wy_ref[node] = bump(y - node)
    nodes = iota((TL, LANES), 0).astype(jnp.float32)
    for atom in range(CS):
        wz_ref[atom] = bump(z[atom : atom + 1] - nodes)

    own = iota((LANES, LANES), 0)
    at = iota((LANES, LANES), 1)
    order = (own == jnp.where(at < HALF, 2 * at, 2 * at - 127)).astype(jnp.bfloat16)
    ids = jnp.broadcast_to(tile_ref[...].astype(jnp.float32), (8, LANES)).astype(jnp.bfloat16)
    tiles = jnp.dot(ids, order, preferred_element_type=jnp.float32)
    tiles_ref[...] = tiles
    tiles = tiles[:1].astype(jnp.int32)

    for half in range(2):

        def step(atom, total, half=half):
            row = pl.ds(atom, 1)
            wz = wz_ref[atom]
            line = [wy_ref[j, row, :] * wz for j in range(TL)]
            new = []
            for i in range(4):
                wx = jnp.broadcast_to(wx_ref[4 * half + i, row, :], (TL, LANES))
                new += [total[8 * i + j] + wx * line[j] for j in range(TL)]
            return tuple(new)

        start = tuple(jnp.zeros((TL, LANES), jnp.float32) for _ in range(32))
        total = lax.fori_loop(0, CS, step, start, unroll=4)
        for slot in range(32):
            cell_ref[pl.ds((32 * half + slot) * TL, TL), :] = total[slot]

    cell = cell_ref[...]
    high = cell.astype(jnp.bfloat16)
    low = (cell - high.astype(jnp.float32)).astype(jnp.bfloat16)
    hot = (iota((GRID_ROWS, LANES), 0) == tiles).astype(jnp.bfloat16)
    fine = lax.dot_general(
        jnp.concatenate([hot, hot], axis=1), jnp.concatenate([high, low], axis=1), (((1,), (1,)), ((), ())),
        preferred_element_type=jnp.float32,
    )
    grid_ref[...] = fine.astype(jnp.bfloat16)

    moves[3].wait()
    moments = jnp.sum(fine * weights_ref[...], axis=1, keepdims=True)
    tx, ty, tz = tile_coords(iota((GRID_ROWS, LANES), 0))
    mine = corner_of((tx, ty, tz)) == (iota((GRID_ROWS, LANES), 1) & 7)
    coarse = jnp.sum(jnp.where(mine, moments, 0.0), axis=0, keepdims=True)
    coarse = coarse * (1.0 / math.sqrt(TP * 27))
    for line in range(coarse_ref.shape[0]):
        coarse_ref[line] = coarse

    own_row = (iota((HALF, LANES), 1) >> 1) == iota((HALF, LANES), 0)
    rows = jnp.where(own_row, tile_ref[...].astype(jnp.float32), 0.0).astype(jnp.bfloat16)
    side = ((iota((LANES, LANES), 0) & 1) == (iota((LANES, LANES), 1) >> 6)).astype(jnp.bfloat16)
    tile = jnp.dot(rows, side, preferred_element_type=jnp.float32).astype(jnp.int32)
    places = tile_coords(tile)
    corner_ref[...] = corner_of(places)
    drive_ref[...] = -charge
    for axis in range(3):
        frac_ref[axis] = (places[axis].astype(jnp.float32) * TL + pos_ref[axis]) * (1.0 / (TL * TD))
    for move in moves[4:]:
        move.wait()


def odd(axis):
    return lax.axis_index(axis) & 1


def face_kernel(grid_ref, near_x_ref, far_x_ref, near_y_ref, far_y_ref, near_z_ref, far_z_ref):
    row = iota((FACE, GRID_ROWS), 0)
    line = (row * 10923) >> 16
    ids = []
    for axis, (first, step) in zip(
        ("gx", "gy", "gz"), ((row, 180), (line * 36 + (row - line * TD), 30), (row * TD, 5)), strict=True
    ):
        side = odd(axis)
        ids += [first + step * (1 - side), first + step * side]
    tile = jnp.where(jnp.concatenate([row] * 6, axis=0) < TD * TD, jnp.concatenate(ids, axis=0), -1)
    hot = (iota((6 * FACE, GRID_ROWS), 1) == tile).astype(jnp.bfloat16)
    faces = jnp.dot(hot, grid_ref[...], preferred_element_type=jnp.float32).astype(jnp.bfloat16)
    for at, ref in enumerate((near_x_ref, far_x_ref, near_y_ref, far_y_ref, near_z_ref, far_z_ref)):
        ref[...] = faces[at * FACE : (at + 1) * FACE]


def coarse_kernel(column_ref, top_ref, out_ref):
    lines = column_ref.shape[0]
    column = column_ref[...].reshape(lines, LANES)
    column = jnp.concatenate([column] * (lines * 8 // LANES), axis=1)
    shape = column.shape
    column = jnp.sum(jnp.where((iota(shape, 1) >> 3) == iota(shape, 0), column, 0.0), axis=0, keepdims=True)
    partial_value = jnp.sum(top_ref[...] * column, axis=1, keepdims=True)
    rows = partial_value.shape[0]
    lanes = jnp.where((iota((rows, LANES), 1) & 7) == (iota((rows, LANES), 0) & 7), partial_value, 0.0)
    lanes = jnp.sum(lanes.reshape(rows // 8, 8, LANES), axis=1)
    for brick in range(rows // 8):
        out_ref[brick] = lanes[brick : brick + 1]


ATOM_ROWS = 16


def gradients(field_ref, wx, wy, wz, x, y, z):
    sums = [None] * 4
    for i in reversed(range(TL)):
        a = b = c = None
        for j in reversed(range(TL)):
            run = mean = None
            for k in reversed(range(TL)):
                term = wz[k] * field_ref[(i * TL + j) * TL + k : (i * TL + j) * TL + k + 1, :]
                run = term if run is None else run + term
                if k:
                    mean = run if mean is None else mean + run
            part = wy[j] * run
            cross = wy[j] * mean
            a = part if a is None else a + part
            c = cross if c is None else c + cross
            if j:
                b = a if b is None else b + a
        for at, value in enumerate((a, b, c)):
            term = wx[i] * value
            sums[at] = term if sums[at] is None else sums[at] + term
        if i:
            sums[3] = sums[0] if sums[3] is None else sums[3] + sums[0]
    total, with_y, with_z, with_x = sums
    return with_x - x * total, with_y - y * total, with_z - z * total


def near_kernel(
    tiles_ref, grid_ref, near_x_ref, far_x_ref, near_y_ref, far_y_ref, near_z_ref, far_z_ref, blocks_ref, coord_ref, weights_ref,
    near_ref, unit_ref,
    ext_ref, field_ref, flat_ref, grad_ref,
):
    ext_ref[0:GRID_ROWS] = grid_ref[...]
    for at, ref in enumerate((near_x_ref, far_x_ref, near_y_ref, far_y_ref, near_z_ref, far_z_ref)):
        ext_ref[GRID_ROWS + at * FACE : GRID_ROWS + (at + 1) * FACE] = ref[...]
    ext_ref[GRID_ROWS + 6 * FACE :] = jnp.zeros((EXT_ROWS - GRID_ROWS - 6 * FACE, TP), jnp.bfloat16)

    tile = jnp.broadcast_to(tiles_ref[:1], (LANES, LANES)).T[:, :1].astype(jnp.int32)
    tx, ty, tz = tile_coords(tile)
    edges = ((tx, 36, ty * TD + tz), (ty, TD, tx * TD + tz), (tz, 1, tx * TD + ty))
    targets = [tile]
    for at, (place, stride, row) in enumerate(edges):
        base = GRID_ROWS + 2 * at * FACE + row
        side = odd(("gx", "gy", "gz")[at])
        targets.append(jnp.where(place < TD - 1, tile + stride, base + side * FACE))
        targets.append(jnp.where(place > 0, tile - stride, base + (1 - side) * FACE))
    at_row = iota((LANES, EXT_ROWS), 1)
    field = None
    for at, target in enumerate(targets):
        hot = (at_row == target).astype(jnp.bfloat16)
        rows = jnp.dot(hot, ext_ref[...], preferred_element_type=jnp.float32).astype(jnp.bfloat16)
        flipped = at > 0 and at % 2 == 0
        term = lax.dot_general(
            rows, blocks_ref[(at + 1) // 2], (((1,), (0 if flipped else 1,)), ((), ())), preferred_element_type=jnp.float32
        )
        field = term if field is None else field + term
    for part in range(TP // LANES):
        field_ref[part * LANES : (part + 1) * LANES, :] = field[:, part * LANES : (part + 1) * LANES].T
        flat_ref[part * LANES : (part + 1) * LANES, :] = jnp.broadcast_to(
            weights_ref[:, part * LANES : (part + 1) * LANES], (LANES, LANES)
        ).T

    @pl.loop(0, CS // ATOM_ROWS)
    def _(group):
        rows = pl.ds(pl.multiple_of(group * ATOM_ROWS, ATOM_ROWS), ATOM_ROWS)
        x, y, z = coord_ref[0, rows, :], coord_ref[1, rows, :], coord_ref[2, rows, :]
        wx, wy, wz = ([bump(u - node) for node in range(TL)] for u in (x, y, z))
        for which, ref in enumerate((field_ref, flat_ref)):
            for axis, value in enumerate(gradients(ref, wx, wy, wz, x, y, z)):
                grad_ref[3 * which + axis, rows, :] = value

    near_ref[0], near_ref[1] = to_atoms(grad_ref[0], grad_ref[1])
    near_ref[2], unit_ref[0] = to_atoms(grad_ref[2], grad_ref[3])
    unit_ref[1], unit_ref[2] = to_atoms(grad_ref[4], grad_ref[5])


def final_kernel(parts_ref, corner_ref, near_ref, unit_ref, frac_ref, drive_ref, force_ref, virial_ref):
    coarse = jnp.sum(parts_ref[...].reshape(parts_ref.shape[0], LANES), axis=0, keepdims=True)
    corner = corner_ref[...]
    pot = jnp.zeros((HALF, LANES), jnp.float32)
    for at in range(8):
        pot = jnp.where(corner == at, coarse[:, at : at + 1], pot)
    drive = drive_ref[...]
    forces = [drive * (near_ref[axis] + pot * unit_ref[axis]) for axis in range(3)]
    for axis in range(3):
        force_ref[axis] = forces[axis]
        virial_ref[axis] = frac_ref[axis] * forces[axis]
    virial_ref[3] = frac_ref[0] * forces[1]
    virial_ref[4] = frac_ref[0] * forces[2]
    virial_ref[5] = frac_ref[1] * forces[2]


VMEM = pl.BlockSpec(memory_space=pltpu.VMEM)
SMEM = pl.BlockSpec(memory_space=pltpu.SMEM)
ANY = pl.BlockSpec(memory_space=pltpu.HBM)


def f32(*shape):
    return jax.ShapeDtypeStruct(shape, jnp.float32)


def bf16(*shape):
    return jax.ShapeDtypeStruct(shape, jnp.bfloat16)


def exchanged(value, axis, far):
    count = lax.axis_size(axis)
    return lax.ppermute(value, axis, [(i, (i + (1 if (i + far) % 2 == 0 else -1)) % count) for i in range(count)])


def shards(positions, charges, cluster_tile, live_clusters, kernel_blocks, restrict_weights, top_kernel):
    pos = positions.reshape(3, HALF, LANES)
    charge = charges.reshape(HALF, LANES)
    tile = cluster_tile.reshape(1, LANES)
    live = live_clusters.reshape(1, 1)
    weights = restrict_weights.reshape(1, TP)
    lines, bricks = lax.axis_size("gz"), lax.axis_size(("gx", "gy"))

    grid, coarse, coords, tiles, drive, frac, corner, weights, blocks, top = pl.pallas_call(
        spread_kernel,
        out_shape=(
            bf16(GRID_ROWS, TP), f32(lines, 1, LANES), f32(3, CS, LANES), f32(8, LANES), f32(HALF, LANES),
            f32(3, HALF, LANES), jax.ShapeDtypeStruct((HALF, LANES), jnp.int32), f32(1, TP),
            bf16(*kernel_blocks.shape), f32(*top_kernel.shape),
        ),
        in_specs=[SMEM] + [ANY] * 6,
        out_specs=[VMEM] * 10,
        scratch_shapes=[
            pltpu.VMEM((3, HALF, LANES), jnp.float32), pltpu.VMEM((HALF, LANES), jnp.float32),
            pltpu.VMEM((1, LANES), jnp.int32),
            pltpu.VMEM((TL, CS, LANES), jnp.float32), pltpu.VMEM((TL, CS, LANES), jnp.float32),
            pltpu.VMEM((CS, TL, LANES), jnp.float32), pltpu.VMEM((TP, LANES), jnp.float32),
            pltpu.SemaphoreType.DMA((6,)),
        ],
        compiler_params=pltpu.CompilerParams(vmem_limit_bytes=12 << 20),
        cost_estimate=pl.CostEstimate(flops=10_000_000, bytes_accessed=1_000_000, transcendentals=200_000),
        name="spread",
    )(live, *(pltpu.with_memory_space_constraint(a, pltpu.HBM) for a in (pos, charge, tile, weights, kernel_blocks, top_kernel)))
    column = lax.all_to_all(coarse, "gz", 0, 0, tiled=True)

    faces = pl.pallas_call(
        face_kernel,
        out_shape=(bf16(FACE, TP),) * 6,
        in_specs=[VMEM],
        out_specs=[VMEM] * 6,
        compiler_params=pltpu.CompilerParams(vmem_limit_bytes=8 << 20),
        cost_estimate=pl.CostEstimate(flops=80_000_000, bytes_accessed=600_000, transcendentals=0),
        name="faces",
    )(grid)
    faces = [exchanged(face, ("gx", "gy", "gz")[at // 2], at % 2) for at, face in enumerate(faces)]

    parts = pl.pallas_call(
        coarse_kernel,
        out_shape=f32(bricks, 1, LANES),
        in_specs=[VMEM] * 2,
        out_specs=VMEM,
        compiler_params=pltpu.CompilerParams(vmem_limit_bytes=8 << 20),
        cost_estimate=pl.CostEstimate(flops=70_000, bytes_accessed=200_000, transcendentals=0),
        name="coarse",
    )(column, top)
    parts = lax.all_to_all(parts, ("gx", "gy"), 0, 0, tiled=True)

    near, unit = pl.pallas_call(
        near_kernel,
        out_shape=(f32(3, HALF, LANES), f32(3, HALF, LANES)),
        in_specs=[VMEM] * 11,
        out_specs=[VMEM] * 2,
        scratch_shapes=[
            pltpu.VMEM((EXT_ROWS, TP), jnp.bfloat16), pltpu.VMEM((TP, LANES), jnp.float32),
            pltpu.VMEM((TP, LANES), jnp.float32), pltpu.VMEM((6, CS, LANES), jnp.float32),
        ],
        compiler_params=pltpu.CompilerParams(vmem_limit_bytes=16 << 20),
        cost_estimate=pl.CostEstimate(flops=1_000_000_000, bytes_accessed=4_000_000, transcendentals=200_000),
        name="near",
    )(tiles, grid, *faces, blocks, coords, weights)

    forces, virial = pl.pallas_call(
        final_kernel,
        out_shape=(f32(3, HALF, LANES), f32(6, HALF, LANES)),
        in_specs=[VMEM] * 6,
        out_specs=[VMEM] * 2,
        compiler_params=pltpu.CompilerParams(vmem_limit_bytes=8 << 20),
        cost_estimate=pl.CostEstimate(flops=500_000, bytes_accessed=600_000, transcendentals=0),
        name="final",
    )(parts, corner, near, unit, frac, drive)
    return forces.reshape(3, 1, 1, 1, -1), virial.reshape(6, 1, 1, 1, -1)


def solution(mesh):
    placed = (
        P(None, "gx", "gy", "gz", None),
        P("gx", "gy", "gz", None),
        P("gx", "gy", "gz", None),
        P("gx", "gy", "gz"),
        P(),
        P(),
        P("gz", ("gx", "gy")),
    )
    return jax.shard_map(
        shards,
        mesh=mesh,
        in_specs=placed,
        out_specs=(P(None, "gx", "gy", "gz", None), P(None, "gx", "gy", "gz", None)),
        check_vma=False,
    )
```

```python
import itertools
import math

import jax
import jax.numpy as jnp
from jax import lax
from jax.experimental import pallas as pl
from jax.experimental.pallas import tpu as pltpu
from jax.sharding import PartitionSpec as P

TL = 8
TP = 512
CS = 64
TD = 6
CUBES = TD**3
FACE = 48
GRID_ROWS = 256
EXT_ROWS = 768
HALF = CS
LANES = 128


def iota(shape, axis):
    return lax.broadcasted_iota(jnp.int32, shape, axis)


def tile_coords(tile):
    plane = (tile * 10923) >> 16
    tx = (tile * 1821) >> 16
    return tx, plane - tx * TD, tile - plane * TD


def to_clusters(upper, lower):
    both = jnp.concatenate([upper, lower], axis=0).T
    even, odd = both[:HALF], both[HALF:]
    left = iota((HALF, LANES), 1) < HALF
    return (
        jnp.where(left, even, pltpu.roll(odd, HALF, 1)),
        jnp.where(left, pltpu.roll(even, HALF, 1), odd),
    )


def to_atoms(upper, lower):
    left = iota((HALF, LANES), 1) < HALF
    even = jnp.where(left, upper, pltpu.roll(lower, HALF, 1))
    odd = jnp.where(left, pltpu.roll(upper, HALF, 1), lower)
    both = jnp.concatenate([even, odd], axis=0).T
    return both[:HALF], both[HALF:]


def corner_of(places):
    tx, ty, tz = ((place >= TD // 2).astype(jnp.int32) for place in places)
    return (tx * 2 + ty) * 2 + tz


def bump(offset):
    return jnp.exp(-0.5 * offset * offset)


def spread_kernel(
    live_ref, pos_any, charge_any, tile_any, weights_any, blocks_any, top_any,
    grid_ref, coarse_ref, coord_ref, tiles_ref, frac_ref, drive_ref, corner_ref, weights_ref, blocks_ref, top_ref,
    pos_ref, charge_ref, tile_ref, wx_ref, wy_ref, wz_ref, cell_ref, sems,
):
    moves = [
        pltpu.make_async_copy(source, target, sems.at[at])
        for at, (source, target) in enumerate(
            (
                (pos_any, pos_ref), (charge_any, charge_ref), (tile_any, tile_ref),
                (weights_any, weights_ref), (blocks_any, blocks_ref), (top_any, top_ref),
            )
        )
    ]
    for move in moves[:4]:
        move.start()
    for move in moves[:3]:
        move.wait()
    for move in moves[4:]:
        move.start()
    cluster = 2 * iota((HALF, LANES), 0) + (iota((HALF, LANES), 1) >> 6)
    charge = charge_ref[...] * (cluster < live_ref[0, 0]).astype(jnp.float32)
    x, y = to_clusters(pos_ref[0], pos_ref[1])
    z, q = to_clusters(pos_ref[2], charge)
    coord_ref[0], coord_ref[1], coord_ref[2] = x, y, z
    for node in range(TL):
        wx_ref[node] = q * bump(x - node)
        wy_ref[node] = bump(y - node)
    nodes = iota((TL, LANES), 0).astype(jnp.float32)
    for atom in range(CS):
        wz_ref[atom] = bump(z[atom : atom + 1] - nodes)

    own = iota((LANES, LANES), 0)
    at = iota((LANES, LANES), 1)
    order = (own == jnp.where(at < HALF, 2 * at, 2 * at - 127)).astype(jnp.bfloat16)
    ids = jnp.broadcast_to(tile_ref[...].astype(jnp.float32), (8, LANES)).astype(jnp.bfloat16)
    tiles = jnp.dot(ids, order, preferred_element_type=jnp.float32)
    tiles_ref[...] = tiles
    tiles = tiles[:1].astype(jnp.int32)

    for half in range(2):

        def step(atom, total, half=half):
            row = pl.ds(atom, 1)
            wz = wz_ref[atom]
            line = [wy_ref[j, row, :] * wz for j in range(TL)]
            new = []
            for i in range(4):
                wx = jnp.broadcast_to(wx_ref[4 * half + i, row, :], (TL, LANES))
                new += [total[8 * i + j] + wx * line[j] for j in range(TL)]
            return tuple(new)

        start = tuple(jnp.zeros((TL, LANES), jnp.float32) for _ in range(32))
        total = lax.fori_loop(0, CS, step, start, unroll=4)
        for slot in range(32):
            cell_ref[pl.ds((32 * half + slot) * TL, TL), :] = total[slot]

    cell = cell_ref[...]
    high = cell.astype(jnp.bfloat16)
    low = (cell - high.astype(jnp.float32)).astype(jnp.bfloat16)
    hot = (iota((GRID_ROWS, LANES), 0) == tiles).astype(jnp.bfloat16)
    fine = lax.dot_general(
        jnp.concatenate([hot, hot], axis=1), jnp.concatenate([high, low], axis=1), (((1,), (1,)), ((), ())),
        preferred_element_type=jnp.float32,
    )
    grid_ref[...] = fine.astype(jnp.bfloat16)

    moves[3].wait()
    moments = jnp.sum(fine * weights_ref[...], axis=1, keepdims=True)
    tx, ty, tz = tile_coords(iota((GRID_ROWS, LANES), 0))
    mine = corner_of((tx, ty, tz)) == (iota((GRID_ROWS, LANES), 1) & 7)
    coarse = jnp.sum(jnp.where(mine, moments, 0.0), axis=0, keepdims=True)
    coarse = coarse * (1.0 / math.sqrt(TP * 27))
    for line in range(coarse_ref.shape[0]):
        coarse_ref[line] = coarse

    own_row = (iota((HALF, LANES), 1) >> 1) == iota((HALF, LANES), 0)
    rows = jnp.where(own_row, tile_ref[...].astype(jnp.float32), 0.0).astype(jnp.bfloat16)
    side = ((iota((LANES, LANES), 0) & 1) == (iota((LANES, LANES), 1) >> 6)).astype(jnp.bfloat16)
    tile = jnp.dot(rows, side, preferred_element_type=jnp.float32).astype(jnp.int32)
    places = tile_coords(tile)
    corner_ref[...] = corner_of(places)
    drive_ref[...] = -charge
    for axis in range(3):
        frac_ref[axis] = (places[axis].astype(jnp.float32) * TL + pos_ref[axis]) * (1.0 / (TL * TD))
    for move in moves[4:]:
        move.wait()


def odd(axis):
    return lax.axis_index(axis) & 1


def face_kernel(grid_ref, pre_ref, keep_ref):
    row = iota((FACE, GRID_ROWS), 0)
    line = (row * 10923) >> 16
    core, side_y, side_z = odd("gx"), odd("gy"), odd("gz")
    low_y, low_z = line * 36 + (row - line * TD), row * TD
    near_x, far_x = row + 180 * (1 - core), row + 180 * core
    own_y, own_z = core ^ side_y ^ 1, core ^ side_z ^ 1
    ids = [
        near_x, low_y + 30 * (1 - own_y), low_z + 5 * (1 - own_z), far_x,
        low_y + 30 * own_y, low_z + 5 * own_z, far_x,
    ]
    tile = jnp.where(jnp.concatenate([row] * 7, axis=0) < TD * TD, jnp.concatenate(ids, axis=0), -1)
    hot = (iota((7 * FACE, GRID_ROWS), 1) == tile).astype(jnp.bfloat16)
    faces = jnp.dot(hot, grid_ref[...], preferred_element_type=jnp.float32).astype(jnp.bfloat16)
    for at in range(4):
        pre_ref[at] = faces[at * FACE : (at + 1) * FACE]
    for at in range(3):
        keep_ref[at] = faces[(at + 4) * FACE : (at + 5) * FACE]


def relay_kernel(keep_ref, got_ref, first_ref, second_ref, third_ref):
    core = odd("gx")
    first_ref[0], first_ref[1] = keep_ref[2 - core], got_ref[3 - core]
    second_ref[0], second_ref[1] = keep_ref[0], got_ref[1]
    third_ref[0], third_ref[1] = keep_ref[1], got_ref[2]


def return_kernel(first_ref, second_ref, third_ref, post_ref):
    post_ref[0] = first_ref[odd("gx")]
    post_ref[1] = second_ref[1]
    post_ref[2] = third_ref[1]


def coarse_kernel(column_ref, top_ref, out_ref):
    lines = column_ref.shape[0]
    column = column_ref[...].reshape(lines, LANES)
    column = jnp.concatenate([column] * (lines * 8 // LANES), axis=1)
    shape = column.shape
    column = jnp.sum(jnp.where((iota(shape, 1) >> 3) == iota(shape, 0), column, 0.0), axis=0, keepdims=True)
    partial_value = jnp.sum(top_ref[...] * column, axis=1, keepdims=True)
    rows = partial_value.shape[0]
    lanes = jnp.where((iota((rows, LANES), 1) & 7) == (iota((rows, LANES), 0) & 7), partial_value, 0.0)
    lanes = jnp.sum(lanes.reshape(rows // 8, 8, LANES), axis=1)
    for brick in range(rows // 8):
        out_ref[brick] = lanes[brick : brick + 1]


ATOM_ROWS = 16


def gradients(field_ref, wx, wy, wz, x, y, z):
    sums = [None] * 4
    for i in reversed(range(TL)):
        a = b = c = None
        for j in reversed(range(TL)):
            run = mean = None
            for k in reversed(range(TL)):
                term = wz[k] * field_ref[(i * TL + j) * TL + k : (i * TL + j) * TL + k + 1, :]
                run = term if run is None else run + term
                if k:
                    mean = run if mean is None else mean + run
            weight = wy(j)
            part = weight * run
            cross = weight * mean
            a = part if a is None else a + part
            c = cross if c is None else c + cross
            if j:
                b = a if b is None else b + a
        weight = wx(i)
        for at, value in enumerate((a, b, c)):
            term = weight * value
            sums[at] = term if sums[at] is None else sums[at] + term
        if i:
            sums[3] = sums[0] if sums[3] is None else sums[3] + sums[0]
    total, with_y, with_z, with_x = sums
    return with_x - x * total, with_y - y * total, with_z - z * total


def near_kernel(
    tiles_ref, grid_ref, got_ref, first_ref, second_ref, third_ref, post_ref, blocks_ref, coord_any, weights_ref,
    near_ref, unit_ref,
    ext_ref, field_ref, flat_ref, grad_ref, coord_ref, sem,
):
    move = pltpu.make_async_copy(coord_any, coord_ref, sem)
    move.start()
    ext_ref[0:GRID_ROWS] = grid_ref[...]
    base = GRID_ROWS
    for ref, count in ((got_ref, 1), (first_ref, 2), (second_ref, 2), (third_ref, 2), (post_ref, 3)):
        for at in range(count):
            ext_ref[base : base + FACE] = ref[at]
            base += FACE
    ext_ref[base:] = jnp.zeros((EXT_ROWS - base, TP), jnp.bfloat16)

    core = odd("gx")

    def at_row_of(on_core_0, on_core_1):
        return GRID_ROWS + FACE * (on_core_0 + (on_core_1 - on_core_0) * core)

    tile = jnp.broadcast_to(tiles_ref[:1], (LANES, LANES)).T[:, :1].astype(jnp.int32)
    tx, ty, tz = tile_coords(tile)
    edges = (
        ("gx", tx, 36, ty * TD + tz, at_row_of(0, 0), at_row_of(2, 7)),
        ("gy", ty, TD, tx * TD + tz, at_row_of(3, 8), at_row_of(8, 3)),
        ("gz", tz, 1, tx * TD + ty, at_row_of(5, 9), at_row_of(7, 1)),
    )
    targets = [tile]
    for axis, place, stride, row, near, far in edges:
        side = odd(axis)
        targets.append(jnp.where(place < TD - 1, tile + stride, row + near + (far - near) * side))
        targets.append(jnp.where(place > 0, tile - stride, row + far + (near - far) * side))
    at_row = iota((LANES, EXT_ROWS), 1)
    field = None
    for at, target in enumerate(targets):
        hot = (at_row == target).astype(jnp.bfloat16)
        rows = jnp.dot(hot, ext_ref[...], preferred_element_type=jnp.float32).astype(jnp.bfloat16)
        flipped = at > 0 and at % 2 == 0
        term = lax.dot_general(
            rows, blocks_ref[(at + 1) // 2], (((1,), (0 if flipped else 1,)), ((), ())), preferred_element_type=jnp.float32
        )
        field = term if field is None else field + term
    for part in range(TP // LANES):
        field_ref[part * LANES : (part + 1) * LANES, :] = field[:, part * LANES : (part + 1) * LANES].T
        flat_ref[part * LANES : (part + 1) * LANES, :] = jnp.broadcast_to(
            weights_ref[:, part * LANES : (part + 1) * LANES], (LANES, LANES)
        ).T

    move.wait()

    @pl.loop(0, CS // ATOM_ROWS)
    def _(group):
        rows = pl.ds(pl.multiple_of(group * ATOM_ROWS, ATOM_ROWS), ATOM_ROWS)
        x, y, z = coord_ref[0, rows, :], coord_ref[1, rows, :], coord_ref[2, rows, :]
        wx, wy, wz = ([bump(u - node) for node in range(TL)] for u in (x, y, z))
        for which, ref in enumerate((field_ref, flat_ref)):
            sums = gradients(ref, wx.__getitem__, wy.__getitem__, wz, x, y, z)
            for axis, value in enumerate(sums):
                grad_ref[3 * which + axis, rows, :] = value

    near_ref[0], near_ref[1] = to_atoms(grad_ref[0], grad_ref[1])
    near_ref[2], unit_ref[0] = to_atoms(grad_ref[2], grad_ref[3])
    unit_ref[1], unit_ref[2] = to_atoms(grad_ref[4], grad_ref[5])


def final_kernel(parts_ref, corner_ref, near_ref, unit_ref, frac_ref, drive_ref, force_ref, virial_ref):
    coarse = jnp.sum(parts_ref[...].reshape(parts_ref.shape[0], LANES), axis=0, keepdims=True)
    corner = corner_ref[...]
    pot = jnp.zeros((HALF, LANES), jnp.float32)
    for at in range(8):
        pot = jnp.where(corner == at, coarse[:, at : at + 1], pot)
    drive = drive_ref[...]
    forces = [drive * (near_ref[axis] + pot * unit_ref[axis]) for axis in range(3)]
    for axis in range(3):
        force_ref[axis] = forces[axis]
        virial_ref[axis] = frac_ref[axis] * forces[axis]
    virial_ref[3] = frac_ref[0] * forces[1]
    virial_ref[4] = frac_ref[0] * forces[2]
    virial_ref[5] = frac_ref[1] * forces[2]


VMEM = pl.BlockSpec(memory_space=pltpu.VMEM)
SMEM = pl.BlockSpec(memory_space=pltpu.SMEM)
ANY = pl.BlockSpec(memory_space=pltpu.HBM)


def f32(*shape):
    return jax.ShapeDtypeStruct(shape, jnp.float32)


def bf16(*shape):
    return jax.ShapeDtypeStruct(shape, jnp.bfloat16)


def exchanged(value, partner):
    wide, high, deep = (lax.axis_size(axis) for axis in ("gx", "gy", "gz"))
    pairs = []
    for x, y, z in itertools.product(range(wide), range(high), range(deep)):
        to = partner(x, y, z)
        if to is not None:
            pairs.append(((x * high + y) * deep + z, ((to[0] % wide) * high + to[1] % high) * deep + to[2] % deep))
    return lax.ppermute(value, ("gx", "gy", "gz"), pairs)


def far(i):
    return i + (1 if i % 2 else -1)


def shards(positions, charges, cluster_tile, live_clusters, kernel_blocks, restrict_weights, top_kernel):
    pos = positions.reshape(3, HALF, LANES)
    charge = charges.reshape(HALF, LANES)
    tile = cluster_tile.reshape(1, LANES)
    live = live_clusters.reshape(1, 1)
    weights = restrict_weights.reshape(1, TP)
    lines, bricks = lax.axis_size("gz"), lax.axis_size(("gx", "gy"))

    grid, coarse, coords, tiles, frac, drive, corner, weights, blocks, top = pl.pallas_call(
        spread_kernel,
        out_shape=(
            bf16(GRID_ROWS, TP), f32(lines, 1, LANES), f32(3, CS, LANES), f32(8, LANES),
            f32(3, HALF, LANES), f32(HALF, LANES), jax.ShapeDtypeStruct((HALF, LANES), jnp.int32), f32(1, TP),
            bf16(*kernel_blocks.shape), f32(*top_kernel.shape),
        ),
        in_specs=[SMEM] + [ANY] * 6,
        out_specs=[VMEM] * 10,
        scratch_shapes=[
            pltpu.VMEM((3, HALF, LANES), jnp.float32), pltpu.VMEM((HALF, LANES), jnp.float32),
            pltpu.VMEM((1, LANES), jnp.int32),
            pltpu.VMEM((TL, CS, LANES), jnp.float32), pltpu.VMEM((TL, CS, LANES), jnp.float32),
            pltpu.VMEM((CS, TL, LANES), jnp.float32), pltpu.VMEM((TP, LANES), jnp.float32),
            pltpu.SemaphoreType.DMA((6,)),
        ],
        compiler_params=pltpu.CompilerParams(vmem_limit_bytes=12 << 20),
        cost_estimate=pl.CostEstimate(flops=10_000_000, bytes_accessed=1_000_000, transcendentals=200_000),
        name="spread",
    )(live, *(pltpu.with_memory_space_constraint(a, pltpu.HBM) for a in (pos, charge, tile, weights, kernel_blocks, top_kernel)))
    column = lax.all_to_all(coarse, "gz", 0, 0, tiled=True)

    pre, keep = pl.pallas_call(
        face_kernel,
        out_shape=(bf16(4, FACE, TP), bf16(3, FACE, TP)),
        in_specs=[VMEM],
        out_specs=[VMEM] * 2,
        compiler_params=pltpu.CompilerParams(vmem_limit_bytes=8 << 20),
        cost_estimate=pl.CostEstimate(flops=80_000_000, bytes_accessed=600_000, transcendentals=0),
        name="faces",
    )(grid)
    got = exchanged(pre, lambda x, y, z: (x ^ 1, y, z))
    first, second, third = pl.pallas_call(
        relay_kernel,
        out_shape=(bf16(2, FACE, TP),) * 3,
        in_specs=[VMEM] * 2,
        out_specs=[VMEM] * 3,
        compiler_params=pltpu.CompilerParams(vmem_limit_bytes=4 << 20),
        cost_estimate=pl.CostEstimate(flops=100_000, bytes_accessed=600_000, transcendentals=0),
        name="relay",
    )(keep, got)
    first = exchanged(first, lambda x, y, z: (x, y, far(z)) if x % 2 else (x + 2, y, z))
    second = exchanged(second, lambda x, y, z: (x, far(y), z) if x % 2 else (x, y ^ 1, z))
    third = exchanged(third, lambda x, y, z: None if x % 2 else (x, y, z ^ 1))
    post = pl.pallas_call(
        return_kernel,
        out_shape=bf16(3, FACE, TP),
        in_specs=[VMEM] * 3,
        out_specs=VMEM,
        compiler_params=pltpu.CompilerParams(vmem_limit_bytes=4 << 20),
        cost_estimate=pl.CostEstimate(flops=100_000, bytes_accessed=300_000, transcendentals=0),
        name="back",
    )(first, second, third)
    post = exchanged(post, lambda x, y, z: (x ^ 1, y, z))

    parts = pl.pallas_call(
        coarse_kernel,
        out_shape=f32(bricks, 1, LANES),
        in_specs=[VMEM] * 2,
        out_specs=VMEM,
        compiler_params=pltpu.CompilerParams(vmem_limit_bytes=8 << 20),
        cost_estimate=pl.CostEstimate(flops=3_000_000_000, bytes_accessed=200_000, transcendentals=0),
        name="coarse",
    )(column, top)
    parts = lax.all_to_all(parts, ("gx", "gy"), 0, 0, tiled=True)

    near, unit = pl.pallas_call(
        near_kernel,
        out_shape=(f32(3, HALF, LANES), f32(3, HALF, LANES)),
        in_specs=[VMEM] * 8 + [ANY, VMEM],
        out_specs=[VMEM] * 2,
        scratch_shapes=[
            pltpu.VMEM((EXT_ROWS, TP), jnp.bfloat16), pltpu.VMEM((TP, LANES), jnp.float32),
            pltpu.VMEM((TP, LANES), jnp.float32), pltpu.VMEM((6, CS, LANES), jnp.float32),
            pltpu.VMEM((3, CS, LANES), jnp.float32), pltpu.SemaphoreType.DMA,
        ],
        compiler_params=pltpu.CompilerParams(vmem_limit_bytes=16 << 20),
        cost_estimate=pl.CostEstimate(flops=1_000_000_000, bytes_accessed=4_000_000, transcendentals=200_000),
        name="near",
    )(tiles, grid, got, first, second, third, post, blocks, pltpu.with_memory_space_constraint(coords, pltpu.HBM), weights)

    forces, virial = pl.pallas_call(
        final_kernel,
        out_shape=(f32(3, HALF, LANES), f32(6, HALF, LANES)),
        in_specs=[VMEM] * 6,
        out_specs=[VMEM] * 2,
        compiler_params=pltpu.CompilerParams(vmem_limit_bytes=8 << 20),
        cost_estimate=pl.CostEstimate(flops=500_000, bytes_accessed=600_000, transcendentals=0),
        name="final",
    )(parts, corner, near, unit, frac, drive)
    return forces.reshape(3, 1, 1, 1, -1), virial.reshape(6, 1, 1, 1, -1)


def solution(mesh):
    placed = (
        P(None, "gx", "gy", "gz", None),
        P("gx", "gy", "gz", None),
        P("gx", "gy", "gz", None),
        P("gx", "gy", "gz"),
        P(),
        P(),
        P("gz", ("gx", "gy")),
    )
    return jax.shard_map(
        shards,
        mesh=mesh,
        in_specs=placed,
        out_specs=(P(None, "gx", "gy", "gz", None), P(None, "gx", "gy", "gz", None)),
        check_vma=False,
    )
```

```python
import math

import jax
import jax.numpy as jnp
from jax import lax
from jax.experimental import pallas as pl
from jax.experimental.pallas import tpu as pltpu
from jax.sharding import PartitionSpec as P

TL = 8
TP = 512
CS = 64
TD = 6
CUBES = TD**3
FACE = 48
GRID_ROWS = 256
EXT_ROWS = 640
HALF = CS
LANES = 128


def iota(shape, axis):
    return lax.broadcasted_iota(jnp.int32, shape, axis)


def tile_coords(tile):
    plane = (tile * 10923) >> 16
    tx = (tile * 1821) >> 16
    return tx, plane - tx * TD, tile - plane * TD


def to_clusters(upper, lower):
    both = jnp.concatenate([upper, lower], axis=0).T
    even, odd = both[:HALF], both[HALF:]
    left = iota((HALF, LANES), 1) < HALF
    return (
        jnp.where(left, even, pltpu.roll(odd, HALF, 1)),
        jnp.where(left, pltpu.roll(even, HALF, 1), odd),
    )


def to_atoms(upper, lower):
    left = iota((HALF, LANES), 1) < HALF
    even = jnp.where(left, upper, pltpu.roll(lower, HALF, 1))
    odd = jnp.where(left, pltpu.roll(upper, HALF, 1), lower)
    both = jnp.concatenate([even, odd], axis=0).T
    return both[:HALF], both[HALF:]


def corner_of(places):
    tx, ty, tz = ((place >= TD // 2).astype(jnp.int32) for place in places)
    return (tx * 2 + ty) * 2 + tz


def bump(offset):
    return jnp.exp(-0.5 * offset * offset)


def spread_kernel(
    live_ref, pos_any, charge_any, tile_any, weights_any, blocks_any, top_any,
    grid_ref, coarse_ref, coord_ref, tiles_ref, drive_ref, frac_ref, corner_ref, weights_ref, blocks_ref, top_ref,
    pos_ref, charge_ref, tile_ref, wx_ref, wy_ref, wz_ref, cell_ref, sems,
):
    moves = [
        pltpu.make_async_copy(source, target, sems.at[at])
        for at, (source, target) in enumerate(
            (
                (pos_any, pos_ref), (charge_any, charge_ref), (tile_any, tile_ref),
                (weights_any, weights_ref), (blocks_any, blocks_ref), (top_any, top_ref),
            )
        )
    ]
    for move in moves:
        move.start()
    for move in moves[:3]:
        move.wait()
    cluster = 2 * iota((HALF, LANES), 0) + (iota((HALF, LANES), 1) >> 6)
    charge = charge_ref[...] * (cluster < live_ref[0, 0]).astype(jnp.float32)
    x, y = to_clusters(pos_ref[0], pos_ref[1])
    z, q = to_clusters(pos_ref[2], charge)
    coord_ref[0], coord_ref[1], coord_ref[2] = x, y, z
    for node in range(TL):
        wx_ref[node] = q * bump(x - node)
        wy_ref[node] = bump(y - node)
    nodes = iota((TL, LANES), 0).astype(jnp.float32)
    for atom in range(CS):
        wz_ref[atom] = bump(z[atom : atom + 1] - nodes)

    own = iota((LANES, LANES), 0)
    at = iota((LANES, LANES), 1)
    order = (own == jnp.where(at < HALF, 2 * at, 2 * at - 127)).astype(jnp.bfloat16)
    ids = jnp.broadcast_to(tile_ref[...].astype(jnp.float32), (8, LANES)).astype(jnp.bfloat16)
    tiles = jnp.dot(ids, order, preferred_element_type=jnp.float32)
    tiles_ref[...] = tiles
    tiles = tiles[:1].astype(jnp.int32)

    for half in range(2):

        def step(atom, total, half=half):
            row = pl.ds(atom, 1)
            wz = wz_ref[atom]
            line = [wy_ref[j, row, :] * wz for j in range(TL)]
            new = []
            for i in range(4):
                wx = jnp.broadcast_to(wx_ref[4 * half + i, row, :], (TL, LANES))
                new += [total[8 * i + j] + wx * line[j] for j in range(TL)]
            return tuple(new)

        start = tuple(jnp.zeros((TL, LANES), jnp.float32) for _ in range(32))
        total = lax.fori_loop(0, CS, step, start, unroll=4)
        for slot in range(32):
            cell_ref[pl.ds((32 * half + slot) * TL, TL), :] = total[slot]

    cell = cell_ref[...]
    high = cell.astype(jnp.bfloat16)
    low = (cell - high.astype(jnp.float32)).astype(jnp.bfloat16)
    hot = (iota((GRID_ROWS, LANES), 0) == tiles).astype(jnp.bfloat16)
    fine = lax.dot_general(
        jnp.concatenate([hot, hot], axis=1), jnp.concatenate([high, low], axis=1), (((1,), (1,)), ((), ())),
        preferred_element_type=jnp.float32,
    )
    grid_ref[...] = fine.astype(jnp.bfloat16)

    moves[3].wait()
    moments = jnp.sum(fine * weights_ref[...], axis=1, keepdims=True)
    tx, ty, tz = tile_coords(iota((GRID_ROWS, LANES), 0))
    mine = corner_of((tx, ty, tz)) == (iota((GRID_ROWS, LANES), 1) & 7)
    coarse = jnp.sum(jnp.where(mine, moments, 0.0), axis=0, keepdims=True)
    coarse = coarse * (1.0 / math.sqrt(TP * 27))
    for line in range(coarse_ref.shape[0]):
        coarse_ref[line] = coarse

    own_row = (iota((HALF, LANES), 1) >> 1) == iota((HALF, LANES), 0)
    rows = jnp.where(own_row, tile_ref[...].astype(jnp.float32), 0.0).astype(jnp.bfloat16)
    side = ((iota((LANES, LANES), 0) & 1) == (iota((LANES, LANES), 1) >> 6)).astype(jnp.bfloat16)
    tile = jnp.dot(rows, side, preferred_element_type=jnp.float32).astype(jnp.int32)
    places = tile_coords(tile)
    corner_ref[...] = corner_of(places)
    drive_ref[...] = -charge
    for axis in range(3):
        frac_ref[axis] = (places[axis].astype(jnp.float32) * TL + pos_ref[axis]) * (1.0 / (TL * TD))
    for move in moves[4:]:
        move.wait()


def odd(axis):
    return lax.axis_index("cx" if axis == "gx" else axis) & 1


def face_kernel(grid_ref, near_x_ref, far_x_ref, near_y_ref, far_y_ref, near_z_ref, far_z_ref):
    row = iota((FACE, GRID_ROWS), 0)
    line = (row * 10923) >> 16
    ids = []
    for axis, (first, step) in zip(
        ("gx", "gy", "gz"), ((row, 180), (line * 36 + (row - line * TD), 30), (row * TD, 5)), strict=True
    ):
        side = odd(axis)
        ids += [first + step * (1 - side), first + step * side]
    tile = jnp.where(jnp.concatenate([row] * 6, axis=0) < TD * TD, jnp.concatenate(ids, axis=0), -1)
    hot = (iota((6 * FACE, GRID_ROWS), 1) == tile).astype(jnp.bfloat16)
    faces = jnp.dot(hot, grid_ref[...], preferred_element_type=jnp.float32).astype(jnp.bfloat16)
    for at, ref in enumerate((near_x_ref, far_x_ref, near_y_ref, far_y_ref, near_z_ref, far_z_ref)):
        ref[...] = faces[at * FACE : (at + 1) * FACE]


def coarse_kernel(column_ref, top_ref, face_ref, own_ref, send_ref):
    lines = column_ref.shape[0]
    column = column_ref[...].reshape(lines, LANES)
    column = jnp.concatenate([column] * (lines * 8 // LANES), axis=1)
    shape = column.shape
    column = jnp.sum(jnp.where((iota(shape, 1) >> 3) == iota(shape, 0), column, 0.0), axis=0, keepdims=True)
    partial_value = jnp.sum(top_ref[...] * column, axis=1, keepdims=True)
    rows = partial_value.shape[0]
    lanes = jnp.where((iota((rows, LANES), 1) & 7) == (iota((rows, LANES), 0) & 7), partial_value, 0.0)
    lanes = jnp.sum(lanes.reshape(rows // 8, 8, LANES), axis=1)
    half = jnp.broadcast_to(lax.axis_index("hx"), (8, LANES)) == 0
    own_ref[...] = jnp.where(half, lanes[:8], lanes[8:])
    rest = jnp.where(half, lanes[8:], lanes[:8])
    parts = []
    for _ in range(3):
        parts.append(rest.astype(jnp.bfloat16).astype(jnp.float32))
        rest = rest - parts[-1]
    tail = jnp.concatenate(parts + [jnp.zeros((8, LANES), jnp.float32)], axis=1)
    send_ref[:32] = face_ref[:32]
    send_ref[32:] = jnp.concatenate([face_ref[32:].astype(jnp.float32)[:8], tail], axis=0).astype(jnp.bfloat16)


def merge_kernel(own_ref, far_ref, field_any, out_ref):
    tail = far_ref[32:].astype(jnp.float32)[8:]
    total = own_ref[...] + ((tail[:, :LANES] + tail[:, LANES : 2 * LANES]) + tail[:, 2 * LANES : 3 * LANES])
    for brick in range(8):
        out_ref[brick] = total[brick : brick + 1]


ATOM_ROWS = 16


def gradients(field_ref, wx, wy, wz, x, y, z):
    sums = [None] * 4
    for i in reversed(range(TL)):
        a = b = c = None
        for j in reversed(range(TL)):
            run = mean = None
            for k in reversed(range(TL)):
                term = wz[k] * field_ref[(i * TL + j) * TL + k : (i * TL + j) * TL + k + 1, :]
                run = term if run is None else run + term
                if k:
                    mean = run if mean is None else mean + run
            part = wy[j] * run
            cross = wy[j] * mean
            a = part if a is None else a + part
            c = cross if c is None else c + cross
            if j:
                b = a if b is None else b + a
        for at, value in enumerate((a, b, c)):
            term = wx[i] * value
            sums[at] = term if sums[at] is None else sums[at] + term
        if i:
            sums[3] = sums[0] if sums[3] is None else sums[3] + sums[0]
    total, with_y, with_z, with_x = sums
    return with_x - x * total, with_y - y * total, with_z - z * total


def tile_column(tiles_ref):
    return jnp.broadcast_to(tiles_ref[:1], (LANES, LANES)).T[:, :1].astype(jnp.int32)


def near_kernel(
    tiles_ref, grid_ref, near_x_ref, near_y_ref, far_y_ref, near_z_ref, far_z_ref, blocks_ref, coord_ref, weights_ref,
    field_ref, unit_ref,
    ext_ref, flat_ref, grad_ref,
):
    ext_ref[0:GRID_ROWS] = grid_ref[...]
    for at, ref in enumerate((near_x_ref, near_y_ref, far_y_ref, near_z_ref, far_z_ref)):
        ext_ref[GRID_ROWS + at * FACE : GRID_ROWS + (at + 1) * FACE] = ref[...]
    nothing = GRID_ROWS + 5 * FACE
    ext_ref[nothing:] = jnp.zeros((EXT_ROWS - nothing, TP), jnp.bfloat16)

    tile = tile_column(tiles_ref)
    tx, ty, tz = tile_coords(tile)
    row_x, row_y, row_z = ty * TD + tz, tx * TD + tz, tx * TD + ty
    base = GRID_ROWS
    edges = (
        ("gx", tx, 36, base + row_x, nothing + 0 * row_x),
        ("gy", ty, TD, base + FACE + row_y, base + 2 * FACE + row_y),
        ("gz", tz, 1, base + 3 * FACE + row_z, base + 4 * FACE + row_z),
    )
    targets = [tile]
    for axis, place, stride, near, far in edges:
        side = jnp.broadcast_to(odd(axis), near.shape) == 1
        targets.append(jnp.where(place < TD - 1, tile + stride, jnp.where(side, far, near)))
        targets.append(jnp.where(place > 0, tile - stride, jnp.where(side, near, far)))
    at_row = iota((LANES, EXT_ROWS), 1)
    field = None
    for at, target in enumerate(targets):
        hot = (at_row == target).astype(jnp.bfloat16)
        rows = jnp.dot(hot, ext_ref[...], preferred_element_type=jnp.float32).astype(jnp.bfloat16)
        flipped = at > 0 and at % 2 == 0
        term = lax.dot_general(
            rows, blocks_ref[(at + 1) // 2], (((1,), (0 if flipped else 1,)), ((), ())), preferred_element_type=jnp.float32
        )
        field = term if field is None else field + term
    field_ref[...] = field
    for part in range(TP // LANES):
        flat_ref[part * LANES : (part + 1) * LANES, :] = jnp.broadcast_to(
            weights_ref[:, part * LANES : (part + 1) * LANES], (LANES, LANES)
        ).T
    all_gradients(flat_ref, coord_ref, grad_ref)
    unit_ref[0], unit_ref[1] = to_atoms(grad_ref[0], grad_ref[1])
    unit_ref[2], _ = to_atoms(grad_ref[2], grad_ref[2])


def all_gradients(field_ref, coord_ref, grad_ref):
    @pl.loop(0, CS // ATOM_ROWS)
    def _(group):
        rows = pl.ds(pl.multiple_of(group * ATOM_ROWS, ATOM_ROWS), ATOM_ROWS)
        x, y, z = coord_ref[0, rows, :], coord_ref[1, rows, :], coord_ref[2, rows, :]
        wx, wy, wz = ([bump(u - node) for node in range(TL)] for u in (x, y, z))
        for axis, value in enumerate(gradients(field_ref, wx, wy, wz, x, y, z)):
            grad_ref[axis, rows, :] = value


def far_kernel(
    tiles_ref, part_ref, far_x_ref, block_ref, coord_ref,
    near_ref,
    sum_ref, field_ref, grad_ref,
):
    tx, ty, tz = tile_coords(tile_column(tiles_ref))
    core = odd("gx")
    target = jnp.where(tx == (TD - 1) * core, ty * TD + tz, -1)
    hot = (iota((LANES, FACE), 1) == target).astype(jnp.bfloat16)
    rows = jnp.dot(hot, far_x_ref[...], preferred_element_type=jnp.float32).astype(jnp.bfloat16)
    for side in range(2):

        @pl.when(core == side)
        def _(side=side):
            sum_ref[...] = part_ref[...] + lax.dot_general(
                rows, block_ref[1], (((1,), (side,)), ((), ())), preferred_element_type=jnp.float32
            )

    for part in range(TP // LANES):
        field_ref[part * LANES : (part + 1) * LANES, :] = sum_ref[:, part * LANES : (part + 1) * LANES].T
    all_gradients(field_ref, coord_ref, grad_ref)
    near_ref[0], near_ref[1] = to_atoms(grad_ref[0], grad_ref[1])
    near_ref[2], _ = to_atoms(grad_ref[2], grad_ref[2])


def final_kernel(parts_ref, corner_ref, near_ref, unit_ref, frac_ref, drive_ref, force_ref, virial_ref):
    coarse = jnp.sum(parts_ref[...].reshape(parts_ref.shape[0], LANES), axis=0, keepdims=True)
    corner = corner_ref[...]
    pot = jnp.zeros((HALF, LANES), jnp.float32)
    for at in range(8):
        pot = jnp.where(corner == at, coarse[:, at : at + 1], pot)
    drive = drive_ref[...]
    forces = [drive * (near_ref[axis] + pot * unit_ref[axis]) for axis in range(3)]
    for axis in range(3):
        force_ref[axis] = forces[axis]
        virial_ref[axis] = frac_ref[axis] * forces[axis]
    virial_ref[3] = frac_ref[0] * forces[1]
    virial_ref[4] = frac_ref[0] * forces[2]
    virial_ref[5] = frac_ref[1] * forces[2]


VMEM = pl.BlockSpec(memory_space=pltpu.VMEM)
SMEM = pl.BlockSpec(memory_space=pltpu.SMEM)
ANY = pl.BlockSpec(memory_space=pl.ANY)


def f32(*shape):
    return jax.ShapeDtypeStruct(shape, jnp.float32)


def bf16(*shape):
    return jax.ShapeDtypeStruct(shape, jnp.bfloat16)


def exchanged(value, axis, far):
    count = lax.axis_size(axis)
    return lax.ppermute(value, axis, [(i, (i + (1 if (i + far) % 2 == 0 else -1)) % count) for i in range(count)])


def shards(positions, charges, cluster_tile, live_clusters, kernel_blocks, restrict_weights, top_kernel):
    pos = positions.reshape(3, HALF, LANES)
    charge = charges.reshape(HALF, LANES)
    tile = cluster_tile.reshape(1, LANES)
    live = live_clusters.reshape(1, 1)
    weights = restrict_weights.reshape(1, TP)
    lines = lax.axis_size("gz")

    grid, coarse, coords, tiles, drive, frac, corner, weights, blocks, top = pl.pallas_call(
        spread_kernel,
        out_shape=(
            bf16(GRID_ROWS, TP), f32(lines, 1, LANES), f32(3, CS, LANES), f32(8, LANES), f32(HALF, LANES),
            f32(3, HALF, LANES), jax.ShapeDtypeStruct((HALF, LANES), jnp.int32), f32(1, TP),
            bf16(*kernel_blocks.shape), f32(*top_kernel.shape),
        ),
        in_specs=[SMEM] + [ANY] * 6,
        out_specs=[VMEM] * 10,
        scratch_shapes=[
            pltpu.VMEM((3, HALF, LANES), jnp.float32), pltpu.VMEM((HALF, LANES), jnp.float32),
            pltpu.VMEM((1, LANES), jnp.int32),
            pltpu.VMEM((TL, CS, LANES), jnp.float32), pltpu.VMEM((TL, CS, LANES), jnp.float32),
            pltpu.VMEM((CS, TL, LANES), jnp.float32), pltpu.VMEM((TP, LANES), jnp.float32),
            pltpu.SemaphoreType.DMA((6,)),
        ],
        compiler_params=pltpu.CompilerParams(vmem_limit_bytes=12 << 20),
        cost_estimate=pl.CostEstimate(flops=10_000_000, bytes_accessed=1_000_000, transcendentals=200_000),
        name="spread",
    )(live, *(pltpu.with_memory_space_constraint(a, pltpu.HBM) for a in (pos, charge, tile, weights, kernel_blocks, top_kernel)))
    column = lax.all_to_all(coarse, "gz", 0, 0, tiled=True)

    faces = pl.pallas_call(
        face_kernel,
        out_shape=(bf16(FACE, TP),) * 6,
        in_specs=[VMEM],
        out_specs=[VMEM] * 6,
        compiler_params=pltpu.CompilerParams(vmem_limit_bytes=8 << 20),
        cost_estimate=pl.CostEstimate(flops=80_000_000, bytes_accessed=600_000, transcendentals=0),
        name="faces",
    )(grid)
    near_x, far_x, near_y, far_y, near_z, far_z = faces
    near_x = exchanged(near_x, ("hx", "cx"), 0)
    near_y, far_y = exchanged(near_y, "gy", 0), exchanged(far_y, "gy", 1)
    near_z, far_z = exchanged(near_z, "gz", 0), exchanged(far_z, "gz", 1)

    own, far_x = pl.pallas_call(
        coarse_kernel,
        out_shape=(f32(8, LANES), bf16(FACE, TP)),
        in_specs=[VMEM] * 3,
        out_specs=[VMEM] * 2,
        compiler_params=pltpu.CompilerParams(vmem_limit_bytes=8 << 20),
        cost_estimate=pl.CostEstimate(flops=70_000, bytes_accessed=200_000, transcendentals=0),
        name="coarse",
    )(column, top, far_x)
    far_x = exchanged(far_x, ("hx", "cx"), 1)

    field, unit = pl.pallas_call(
        near_kernel,
        out_shape=(f32(LANES, TP), f32(3, HALF, LANES)),
        in_specs=[VMEM] * 10,
        out_specs=[VMEM] * 2,
        scratch_shapes=[
            pltpu.VMEM((EXT_ROWS, TP), jnp.bfloat16), pltpu.VMEM((TP, LANES), jnp.float32),
            pltpu.VMEM((3, CS, LANES), jnp.float32),
        ],
        compiler_params=pltpu.CompilerParams(vmem_limit_bytes=16 << 20),
        cost_estimate=pl.CostEstimate(flops=1_000_000_000, bytes_accessed=4_000_000, transcendentals=200_000),
        name="near",
    )(tiles, grid, near_x, near_y, far_y, near_z, far_z, blocks, coords, weights)

    parts = pl.pallas_call(
        merge_kernel,
        out_shape=f32(8, 1, LANES),
        in_specs=[VMEM] * 2 + [ANY],
        out_specs=VMEM,
        compiler_params=pltpu.CompilerParams(vmem_limit_bytes=4 << 20),
        cost_estimate=pl.CostEstimate(flops=10_000, bytes_accessed=60_000, transcendentals=0),
        name="merge",
    )(own, far_x, field)
    parts = lax.all_to_all(parts, ("cx", "gy"), 0, 0, tiled=True)

    near = pl.pallas_call(
        far_kernel,
        out_shape=f32(3, HALF, LANES),
        in_specs=[VMEM] * 5,
        out_specs=VMEM,
        scratch_shapes=[
            pltpu.VMEM((LANES, TP), jnp.float32), pltpu.VMEM((TP, LANES), jnp.float32),
            pltpu.VMEM((3, CS, LANES), jnp.float32),
        ],
        compiler_params=pltpu.CompilerParams(vmem_limit_bytes=16 << 20),
        cost_estimate=pl.CostEstimate(flops=1_000_000_000, bytes_accessed=4_000_000, transcendentals=200_000),
        name="far",
    )(tiles, field, far_x, blocks, coords)

    forces, virial = pl.pallas_call(
        final_kernel,
        out_shape=(f32(3, HALF, LANES), f32(6, HALF, LANES)),
        in_specs=[VMEM] * 6,
        out_specs=[VMEM] * 2,
        compiler_params=pltpu.CompilerParams(vmem_limit_bytes=8 << 20),
        cost_estimate=pl.CostEstimate(flops=500_000, bytes_accessed=600_000, transcendentals=0),
        name="final",
    )(parts, corner, near, unit, frac, drive)
    return forces.reshape(3, 1, 1, 1, -1), virial.reshape(6, 1, 1, 1, -1)


def solution(mesh):
    wide, high, deep = (mesh.shape[axis] for axis in ("gx", "gy", "gz"))
    split = jax.sharding.Mesh(mesh.devices.reshape(wide // 2, 2, high, deep), ("hx", "cx", "gy", "gz"))
    x = ("hx", "cx")
    placed = (
        P(None, x, "gy", "gz", None),
        P(x, "gy", "gz", None),
        P(x, "gy", "gz", None),
        P(x, "gy", "gz"),
        P(),
        P(),
        P("gz", ("hx", "cx", "gy")),
    )
    return jax.shard_map(
        shards,
        mesh=split,
        in_specs=placed,
        out_specs=(P(None, x, "gy", "gz", None), P(None, x, "gy", "gz", None)),
        check_vma=False,
    )
```

```python
import math

import jax
import jax.numpy as jnp
from jax import lax
from jax.experimental import pallas as pl
from jax.experimental.pallas import tpu as pltpu
from jax.sharding import PartitionSpec as P

TL = 8
TP = 512
CS = 64
TD = 6
CUBES = TD**3
FACE = 48
GRID_ROWS = 256
FAR_ROWS = 40
EXT_ROWS = 640
HALF = CS
LANES = 128


def iota(shape, axis):
    return lax.broadcasted_iota(jnp.int32, shape, axis)


def tile_coords(tile):
    plane = (tile * 10923) >> 16
    tx = (tile * 1821) >> 16
    return tx, plane - tx * TD, tile - plane * TD


def to_clusters(upper, lower):
    both = jnp.concatenate([upper, lower], axis=0).T
    even, odd = both[:HALF], both[HALF:]
    left = iota((HALF, LANES), 1) < HALF
    return (
        jnp.where(left, even, pltpu.roll(odd, HALF, 1)),
        jnp.where(left, pltpu.roll(even, HALF, 1), odd),
    )


def to_atoms(upper, lower):
    left = iota((HALF, LANES), 1) < HALF
    even = jnp.where(left, upper, pltpu.roll(lower, HALF, 1))
    odd = jnp.where(left, pltpu.roll(upper, HALF, 1), lower)
    both = jnp.concatenate([even, odd], axis=0).T
    return both[:HALF], both[HALF:]


def corner_of(places):
    tx, ty, tz = ((place >= TD // 2).astype(jnp.int32) for place in places)
    return (tx * 2 + ty) * 2 + tz


def bump(offset):
    return jnp.exp(-0.5 * offset * offset)


def spread_kernel(
    live_ref, pos_any, charge_any, tile_any, weights_any, blocks_any, top_any,
    grid_ref, coarse_ref, coord_ref, tiles_ref, drive_ref, frac_ref, corner_ref, weights_ref, blocks_ref, top_ref,
    pos_ref, charge_ref, tile_ref, wx_ref, wy_ref, wz_ref, cell_ref, sems,
):
    moves = [
        pltpu.make_async_copy(source, target, sems.at[at])
        for at, (source, target) in enumerate(
            (
                (pos_any, pos_ref), (charge_any, charge_ref), (tile_any, tile_ref),
                (weights_any, weights_ref), (blocks_any, blocks_ref), (top_any, top_ref),
            )
        )
    ]
    for move in moves:
        move.start()
    for move in moves[:3]:
        move.wait()
    cluster = 2 * iota((HALF, LANES), 0) + (iota((HALF, LANES), 1) >> 6)
    charge = charge_ref[...] * (cluster < live_ref[0, 0]).astype(jnp.float32)
    x, y = to_clusters(pos_ref[0], pos_ref[1])
    z, q = to_clusters(pos_ref[2], charge)
    coord_ref[0], coord_ref[1], coord_ref[2] = x, y, z
    for node in range(TL):
        wx_ref[node] = q * bump(x - node)
        wy_ref[node] = bump(y - node)
    nodes = iota((TL, LANES), 0).astype(jnp.float32)
    for atom in range(CS):
        wz_ref[atom] = bump(z[atom : atom + 1] - nodes)

    own = iota((LANES, LANES), 0)
    at = iota((LANES, LANES), 1)
    order = (own == jnp.where(at < HALF, 2 * at, 2 * at - 127)).astype(jnp.bfloat16)
    ids = jnp.broadcast_to(tile_ref[...].astype(jnp.float32), (8, LANES)).astype(jnp.bfloat16)
    tiles = jnp.dot(ids, order, preferred_element_type=jnp.float32)
    tiles_ref[...] = tiles
    tiles = tiles[:1].astype(jnp.int32)

    for half in range(2):

        def step(atom, total, half=half):
            row = pl.ds(atom, 1)
            wz = wz_ref[atom]
            line = [wy_ref[j, row, :] * wz for j in range(TL)]
            new = []
            for i in range(4):
                wx = jnp.broadcast_to(wx_ref[4 * half + i, row, :], (TL, LANES))
                new += [total[8 * i + j] + wx * line[j] for j in range(TL)]
            return tuple(new)

        start = tuple(jnp.zeros((TL, LANES), jnp.float32) for _ in range(32))
        total = lax.fori_loop(0, CS, step, start, unroll=4)
        for slot in range(32):
            cell_ref[pl.ds((32 * half + slot) * TL, TL), :] = total[slot]

    cell = cell_ref[...]
    high = cell.astype(jnp.bfloat16)
    low = (cell - high.astype(jnp.float32)).astype(jnp.bfloat16)
    hot = (iota((GRID_ROWS, LANES), 0) == tiles).astype(jnp.bfloat16)
    fine = lax.dot_general(
        jnp.concatenate([hot, hot], axis=1), jnp.concatenate([high, low], axis=1), (((1,), (1,)), ((), ())),
        preferred_element_type=jnp.float32,
    )
    grid_ref[...] = fine.astype(jnp.bfloat16)

    moves[3].wait()
    moments = jnp.sum(fine * weights_ref[...], axis=1, keepdims=True)
    tx, ty, tz = tile_coords(iota((GRID_ROWS, LANES), 0))
    mine = corner_of((tx, ty, tz)) == (iota((GRID_ROWS, LANES), 1) & 7)
    coarse = jnp.sum(jnp.where(mine, moments, 0.0), axis=0, keepdims=True)
    coarse = coarse * (1.0 / math.sqrt(TP * 27))
    for line in range(coarse_ref.shape[0]):
        coarse_ref[line] = coarse

    own_row = (iota((HALF, LANES), 1) >> 1) == iota((HALF, LANES), 0)
    rows = jnp.where(own_row, tile_ref[...].astype(jnp.float32), 0.0).astype(jnp.bfloat16)
    side = ((iota((LANES, LANES), 0) & 1) == (iota((LANES, LANES), 1) >> 6)).astype(jnp.bfloat16)
    tile = jnp.dot(rows, side, preferred_element_type=jnp.float32).astype(jnp.int32)
    places = tile_coords(tile)
    corner_ref[...] = corner_of(places)
    drive_ref[...] = -charge
    for axis in range(3):
        frac_ref[axis] = (places[axis].astype(jnp.float32) * TL + pos_ref[axis]) * (1.0 / (TL * TD))
    for move in moves[4:]:
        move.wait()


def odd(axis):
    return lax.axis_index("cx" if axis == "gx" else axis) & 1


def face_kernel(grid_ref, near_x_ref, far_x_ref, near_y_ref, far_y_ref, near_z_ref, far_z_ref):
    row = iota((FACE, GRID_ROWS), 0)
    line = (row * 10923) >> 16
    ids = []
    for axis, (first, step) in zip(
        ("gx", "gy", "gz"), ((row, 180), (line * 36 + (row - line * TD), 30), (row * TD, 5)), strict=True
    ):
        side = odd(axis)
        ids += [first + step * (1 - side), first + step * side]
    tile = jnp.where(jnp.concatenate([row] * 6, axis=0) < TD * TD, jnp.concatenate(ids, axis=0), -1)
    hot = (iota((6 * FACE, GRID_ROWS), 1) == tile).astype(jnp.bfloat16)
    faces = jnp.dot(hot, grid_ref[...], preferred_element_type=jnp.float32).astype(jnp.bfloat16)
    for at, ref in enumerate((near_x_ref, far_x_ref, near_y_ref, far_y_ref, near_z_ref, far_z_ref)):
        ref[...] = faces[at * FACE : (at + 1) * FACE]


def coarse_kernel(column_ref, top_ref, face_ref, face_y_ref, own_ref, send_ref, pass_ref):
    lines = column_ref.shape[0]
    column = column_ref[...].reshape(lines, LANES)
    column = jnp.concatenate([column] * (lines * 8 // LANES), axis=1)
    shape = column.shape
    column = jnp.sum(jnp.where((iota(shape, 1) >> 3) == iota(shape, 0), column, 0.0), axis=0, keepdims=True)
    partial_value = jnp.sum(top_ref[...] * column, axis=1, keepdims=True)
    rows = partial_value.shape[0]
    lanes = jnp.where((iota((rows, LANES), 1) & 7) == (iota((rows, LANES), 0) & 7), partial_value, 0.0)
    lanes = jnp.sum(lanes.reshape(rows // 8, 8, LANES), axis=1)
    mine = iota((8, LANES), 1) >> 3 == iota((8, LANES), 0)
    lower, upper = (jnp.sum(jnp.where(mine, lanes[at : at + 8], 0.0), axis=0, keepdims=True) for at in (0, 8))
    half = jnp.broadcast_to(lax.axis_index("hx"), (1, LANES)) == 0
    own_ref[...] = jnp.where(half, lower, upper)
    rest = jnp.where(half, upper, lower)
    parts = []
    for _ in range(3):
        parts.append(rest.astype(jnp.bfloat16).astype(jnp.float32))
        rest = rest - parts[-1]
    sums = jnp.concatenate(parts + [jnp.zeros((1, LANES), jnp.float32)], axis=1)
    rows = face_ref[...].astype(jnp.float32)[:FAR_ROWS]
    send_ref[...] = jnp.where(iota((FAR_ROWS, TP), 0) == TD * TD, sums, rows).astype(jnp.bfloat16)
    pass_ref[...] = face_y_ref[...].astype(jnp.float32)[: pass_ref.shape[0]].astype(jnp.bfloat16)


def merge_kernel(own_ref, far_ref, field_any, out_ref):
    sums = far_ref[...].astype(jnp.float32)[TD * TD : TD * TD + 1]
    total = own_ref[...] + ((sums[:, :LANES] + sums[:, LANES : 2 * LANES]) + sums[:, 2 * LANES : 3 * LANES])
    for brick in range(8):
        out_ref[brick] = pltpu.roll(total, (LANES - 8 * brick) % LANES, 1) if brick else total


ATOM_ROWS = 16


def gradients(field_ref, wx, wy, wz, x, y, z):
    sums = [None] * 4
    for i in reversed(range(TL)):
        a = b = c = None
        for j in reversed(range(TL)):
            run = mean = None
            for k in reversed(range(TL)):
                term = wz[k] * field_ref[(i * TL + j) * TL + k : (i * TL + j) * TL + k + 1, :]
                run = term if run is None else run + term
                if k:
                    mean = run if mean is None else mean + run
            part = wy[j] * run
            cross = wy[j] * mean
            a = part if a is None else a + part
            c = cross if c is None else c + cross
            if j:
                b = a if b is None else b + a
        for at, value in enumerate((a, b, c)):
            term = wx[i] * value
            sums[at] = term if sums[at] is None else sums[at] + term
        if i:
            sums[3] = sums[0] if sums[3] is None else sums[3] + sums[0]
    total, with_y, with_z, with_x = sums
    return with_x - x * total, with_y - y * total, with_z - z * total


def tile_column(tiles_ref):
    return jnp.broadcast_to(tiles_ref[:1], (LANES, LANES)).T[:, :1].astype(jnp.int32)


def near_kernel(
    tiles_ref, grid_ref, near_x_ref, near_y_ref, far_y_ref, near_z_ref, far_z_ref, blocks_ref, coord_ref, weights_ref,
    field_ref, unit_ref,
    ext_ref, flat_ref, grad_ref,
):
    ext_ref[0:GRID_ROWS] = grid_ref[...]
    for at, ref in enumerate((near_x_ref, near_y_ref, far_y_ref, near_z_ref, far_z_ref)):
        face = ref[...]
        if face.shape[0] < FACE:
            rest = jnp.zeros((FACE - face.shape[0], TP), jnp.float32)
            face = jnp.concatenate([face.astype(jnp.float32), rest], axis=0).astype(jnp.bfloat16)
        ext_ref[GRID_ROWS + at * FACE : GRID_ROWS + (at + 1) * FACE] = face
    nothing = GRID_ROWS + 5 * FACE
    ext_ref[nothing:] = jnp.zeros((EXT_ROWS - nothing, TP), jnp.bfloat16)

    tile = tile_column(tiles_ref)
    tx, ty, tz = tile_coords(tile)
    row_x, row_y, row_z = ty * TD + tz, tx * TD + tz, tx * TD + ty
    base = GRID_ROWS
    edges = (
        ("gx", tx, 36, base + row_x, nothing + 0 * row_x),
        ("gy", ty, TD, base + FACE + row_y, base + 2 * FACE + row_y),
        ("gz", tz, 1, base + 3 * FACE + row_z, base + 4 * FACE + row_z),
    )
    targets = [tile]
    for axis, place, stride, near, far in edges:
        side = jnp.broadcast_to(odd(axis), near.shape) == 1
        targets.append(jnp.where(place < TD - 1, tile + stride, jnp.where(side, far, near)))
        targets.append(jnp.where(place > 0, tile - stride, jnp.where(side, near, far)))
    at_row = iota((LANES, EXT_ROWS), 1)
    field = None
    for at, target in enumerate(targets):
        hot = (at_row == target).astype(jnp.bfloat16)
        rows = jnp.dot(hot, ext_ref[...], preferred_element_type=jnp.float32).astype(jnp.bfloat16)
        flipped = at > 0 and at % 2 == 0
        term = lax.dot_general(
            rows, blocks_ref[(at + 1) // 2], (((1,), (0 if flipped else 1,)), ((), ())), preferred_element_type=jnp.float32
        )
        field = term if field is None else field + term
    field_ref[...] = field
    for part in range(TP // LANES):
        flat_ref[part * LANES : (part + 1) * LANES, :] = jnp.broadcast_to(
            weights_ref[:, part * LANES : (part + 1) * LANES], (LANES, LANES)
        ).T
    all_gradients(flat_ref, coord_ref, grad_ref)
    unit_ref[0], unit_ref[1] = to_atoms(grad_ref[0], grad_ref[1])
    unit_ref[2], _ = to_atoms(grad_ref[2], grad_ref[2])


def all_gradients(field_ref, coord_ref, grad_ref):
    @pl.loop(0, CS // ATOM_ROWS)
    def _(group):
        rows = pl.ds(pl.multiple_of(group * ATOM_ROWS, ATOM_ROWS), ATOM_ROWS)
        x, y, z = coord_ref[0, rows, :], coord_ref[1, rows, :], coord_ref[2, rows, :]
        wx, wy, wz = ([bump(u - node) for node in range(TL)] for u in (x, y, z))
        for axis, value in enumerate(gradients(field_ref, wx, wy, wz, x, y, z)):
            grad_ref[axis, rows, :] = value


def far_kernel(
    tiles_ref, part_ref, far_x_ref, block_ref, coord_ref,
    near_ref,
    sum_ref, field_ref, grad_ref,
):
    tx, ty, tz = tile_coords(tile_column(tiles_ref))
    core = odd("gx")
    target = jnp.where(tx == (TD - 1) * core, ty * TD + tz, -1)
    hot = (iota((LANES, FAR_ROWS), 1) == target).astype(jnp.bfloat16)
    rows = jnp.dot(hot, far_x_ref[...], preferred_element_type=jnp.float32).astype(jnp.bfloat16)
    for side in range(2):

        @pl.when(core == side)
        def _(side=side):
            sum_ref[...] = part_ref[...] + lax.dot_general(
                rows, block_ref[1], (((1,), (side,)), ((), ())), preferred_element_type=jnp.float32
            )

    for part in range(TP // LANES):
        field_ref[part * LANES : (part + 1) * LANES, :] = sum_ref[:, part * LANES : (part + 1) * LANES].T
    all_gradients(field_ref, coord_ref, grad_ref)
    near_ref[0], near_ref[1] = to_atoms(grad_ref[0], grad_ref[1])
    near_ref[2], _ = to_atoms(grad_ref[2], grad_ref[2])


def final_kernel(parts_ref, corner_ref, near_ref, unit_ref, frac_ref, drive_ref, force_ref, virial_ref):
    coarse = jnp.sum(parts_ref[...].reshape(parts_ref.shape[0], LANES), axis=0, keepdims=True)
    corner = corner_ref[...]
    pot = jnp.zeros((HALF, LANES), jnp.float32)
    for at in range(8):
        pot = jnp.where(corner == at, coarse[:, at : at + 1], pot)
    drive = drive_ref[...]
    forces = [drive * (near_ref[axis] + pot * unit_ref[axis]) for axis in range(3)]
    for axis in range(3):
        force_ref[axis] = forces[axis]
        virial_ref[axis] = frac_ref[axis] * forces[axis]
    virial_ref[3] = frac_ref[0] * forces[1]
    virial_ref[4] = frac_ref[0] * forces[2]
    virial_ref[5] = frac_ref[1] * forces[2]


VMEM = pl.BlockSpec(memory_space=pltpu.VMEM)
SMEM = pl.BlockSpec(memory_space=pltpu.SMEM)
ANY = pl.BlockSpec(memory_space=pl.ANY)


def f32(*shape):
    return jax.ShapeDtypeStruct(shape, jnp.float32)


def bf16(*shape):
    return jax.ShapeDtypeStruct(shape, jnp.bfloat16)


def exchanged(value, axis, far):
    count = lax.axis_size(axis)
    return lax.ppermute(value, axis, [(i, (i + (1 if (i + far) % 2 == 0 else -1)) % count) for i in range(count)])


def shards(positions, charges, cluster_tile, live_clusters, kernel_blocks, restrict_weights, top_kernel):
    pos = positions.reshape(3, HALF, LANES)
    charge = charges.reshape(HALF, LANES)
    tile = cluster_tile.reshape(1, LANES)
    live = live_clusters.reshape(1, 1)
    weights = restrict_weights.reshape(1, TP)
    lines = lax.axis_size("gz")

    grid, coarse, coords, tiles, drive, frac, corner, weights, blocks, top = pl.pallas_call(
        spread_kernel,
        out_shape=(
            bf16(GRID_ROWS, TP), f32(lines, 1, LANES), f32(3, CS, LANES), f32(8, LANES), f32(HALF, LANES),
            f32(3, HALF, LANES), jax.ShapeDtypeStruct((HALF, LANES), jnp.int32), f32(1, TP),
            bf16(*kernel_blocks.shape), f32(*top_kernel.shape),
        ),
        in_specs=[SMEM] + [ANY] * 6,
        out_specs=[VMEM] * 10,
        scratch_shapes=[
            pltpu.VMEM((3, HALF, LANES), jnp.float32), pltpu.VMEM((HALF, LANES), jnp.float32),
            pltpu.VMEM((1, LANES), jnp.int32),
            pltpu.VMEM((TL, CS, LANES), jnp.float32), pltpu.VMEM((TL, CS, LANES), jnp.float32),
            pltpu.VMEM((CS, TL, LANES), jnp.float32), pltpu.VMEM((TP, LANES), jnp.float32),
            pltpu.SemaphoreType.DMA((6,)),
        ],
        compiler_params=pltpu.CompilerParams(vmem_limit_bytes=12 << 20),
        cost_estimate=pl.CostEstimate(flops=10_000_000, bytes_accessed=1_000_000, transcendentals=200_000),
        name="spread",
    )(live, *(pltpu.with_memory_space_constraint(a, pltpu.HBM) for a in (pos, charge, tile, weights, kernel_blocks, top_kernel)))
    column = lax.all_to_all(coarse, "gz", 0, 0, tiled=True)

    faces = pl.pallas_call(
        face_kernel,
        out_shape=(bf16(FACE, TP),) * 6,
        in_specs=[VMEM],
        out_specs=[VMEM] * 6,
        compiler_params=pltpu.CompilerParams(vmem_limit_bytes=8 << 20),
        cost_estimate=pl.CostEstimate(flops=80_000_000, bytes_accessed=600_000, transcendentals=0),
        name="faces",
    )(grid)
    near_x, far_x, near_y, far_y, near_z, far_z = faces
    far_z, near_z = exchanged(far_z, "gz", 1), exchanged(near_z, "gz", 0)
    near_x = exchanged(near_x, ("hx", "cx"), 0)
    near_y = exchanged(near_y, "gy", 0)

    own, far_x, far_y = pl.pallas_call(
        coarse_kernel,
        out_shape=(f32(1, LANES), bf16(FAR_ROWS, TP), bf16(36, TP)),
        in_specs=[VMEM] * 4,
        out_specs=[VMEM] * 3,
        compiler_params=pltpu.CompilerParams(vmem_limit_bytes=8 << 20),
        cost_estimate=pl.CostEstimate(flops=70_000, bytes_accessed=200_000, transcendentals=0),
        name="coarse",
    )(column, top, far_x, far_y)
    far_x = exchanged(far_x, ("hx", "cx"), 1)
    far_y = exchanged(far_y, "gy", 1)

    field, unit = pl.pallas_call(
        near_kernel,
        out_shape=(f32(LANES, TP), f32(3, HALF, LANES)),
        in_specs=[VMEM] * 10,
        out_specs=[VMEM] * 2,
        scratch_shapes=[
            pltpu.VMEM((EXT_ROWS, TP), jnp.bfloat16), pltpu.VMEM((TP, LANES), jnp.float32),
            pltpu.VMEM((3, CS, LANES), jnp.float32),
        ],
        compiler_params=pltpu.CompilerParams(vmem_limit_bytes=16 << 20),
        cost_estimate=pl.CostEstimate(flops=1000, bytes_accessed=1000, transcendentals=0),
        name="near",
    )(tiles, grid, near_x, near_y, far_y, near_z, far_z, blocks, coords, weights)

    parts = pl.pallas_call(
        merge_kernel,
        out_shape=f32(8, 1, LANES),
        in_specs=[VMEM] * 2 + [ANY],
        out_specs=VMEM,
        compiler_params=pltpu.CompilerParams(vmem_limit_bytes=4 << 20),
        cost_estimate=pl.CostEstimate(flops=10_000, bytes_accessed=60_000, transcendentals=0),
        name="merge",
    )(own, far_x, field)
    parts = lax.all_to_all(parts, ("cx", "gy"), 0, 0, tiled=True)

    near = pl.pallas_call(
        far_kernel,
        out_shape=f32(3, HALF, LANES),
        in_specs=[VMEM] * 5,
        out_specs=VMEM,
        scratch_shapes=[
            pltpu.VMEM((LANES, TP), jnp.float32), pltpu.VMEM((TP, LANES), jnp.float32),
            pltpu.VMEM((3, CS, LANES), jnp.float32),
        ],
        compiler_params=pltpu.CompilerParams(vmem_limit_bytes=16 << 20),
        cost_estimate=pl.CostEstimate(flops=1_000_000_000, bytes_accessed=4_000_000, transcendentals=200_000),
        name="far",
    )(tiles, field, far_x, blocks, coords)

    forces, virial = pl.pallas_call(
        final_kernel,
        out_shape=(f32(3, HALF, LANES), f32(6, HALF, LANES)),
        in_specs=[VMEM] * 6,
        out_specs=[VMEM] * 2,
        compiler_params=pltpu.CompilerParams(vmem_limit_bytes=8 << 20),
        cost_estimate=pl.CostEstimate(flops=500_000, bytes_accessed=600_000, transcendentals=0),
        name="final",
    )(parts, corner, near, unit, frac, drive)
    return forces.reshape(3, 1, 1, 1, -1), virial.reshape(6, 1, 1, 1, -1)


def solution(mesh):
    wide, high, deep = (mesh.shape[axis] for axis in ("gx", "gy", "gz"))
    split = jax.sharding.Mesh(mesh.devices.reshape(wide // 2, 2, high, deep), ("hx", "cx", "gy", "gz"))
    x = ("hx", "cx")
    placed = (
        P(None, x, "gy", "gz", None),
        P(x, "gy", "gz", None),
        P(x, "gy", "gz", None),
        P(x, "gy", "gz"),
        P(),
        P(),
        P("gz", ("hx", "cx", "gy")),
    )
    return jax.shard_map(
        shards,
        mesh=split,
        in_specs=placed,
        out_specs=(P(None, x, "gy", "gz", None), P(None, x, "gy", "gz", None)),
        check_vma=False,
    )
```

```python
import math

import jax
import jax.numpy as jnp
from jax import lax
from jax.experimental import pallas as pl
from jax.experimental.pallas import tpu as pltpu
from jax.sharding import PartitionSpec as P

TL = 8
TP = 512
CS = 64
TD = 6
CUBES = TD**3
FACE = 48
GRID_ROWS = 256
FAR_ROWS = 40
EXT_ROWS = 512
HALF = CS
LANES = 128


def iota(shape, axis):
    return lax.broadcasted_iota(jnp.int32, shape, axis)


def tile_coords(tile):
    plane = (tile * 10923) >> 16
    tx = (tile * 1821) >> 16
    return tx, plane - tx * TD, tile - plane * TD


def to_clusters(upper, lower):
    both = jnp.concatenate([upper, lower], axis=0).T
    even, odd = both[:HALF], both[HALF:]
    left = iota((HALF, LANES), 1) < HALF
    return (
        jnp.where(left, even, pltpu.roll(odd, HALF, 1)),
        jnp.where(left, pltpu.roll(even, HALF, 1), odd),
    )


def to_atoms(upper, lower):
    left = iota((HALF, LANES), 1) < HALF
    even = jnp.where(left, upper, pltpu.roll(lower, HALF, 1))
    odd = jnp.where(left, pltpu.roll(upper, HALF, 1), lower)
    both = jnp.concatenate([even, odd], axis=0).T
    return both[:HALF], both[HALF:]


def corner_of(places):
    tx, ty, tz = ((place >= TD // 2).astype(jnp.int32) for place in places)
    return (tx * 2 + ty) * 2 + tz


def bump(offset):
    return jnp.exp(-0.5 * offset * offset)


def spread_kernel(
    live_ref, pos_any, charge_any, tile_any, weights_any, blocks_any, top_any,
    grid_ref, coarse_ref, coord_ref, tiles_ref, drive_ref, frac_ref, corner_ref, weights_ref, blocks_ref, top_ref,
    pos_ref, charge_ref, tile_ref, wx_ref, wy_ref, wz_ref, cell_ref, sems,
):
    moves = [
        pltpu.make_async_copy(source, target, sems.at[at])
        for at, (source, target) in enumerate(
            (
                (pos_any, pos_ref), (charge_any, charge_ref), (tile_any, tile_ref),
                (weights_any, weights_ref), (blocks_any, blocks_ref), (top_any, top_ref),
            )
        )
    ]
    for move in moves:
        move.start()
    for move in moves[:3]:
        move.wait()
    cluster = 2 * iota((HALF, LANES), 0) + (iota((HALF, LANES), 1) >> 6)
    charge = charge_ref[...] * (cluster < live_ref[0, 0]).astype(jnp.float32)
    x, y = to_clusters(pos_ref[0], pos_ref[1])
    z, q = to_clusters(pos_ref[2], charge)
    coord_ref[0], coord_ref[1], coord_ref[2] = x, y, z
    for node in range(TL):
        wx_ref[node] = q * bump(x - node)
        wy_ref[node] = bump(y - node)
    nodes = iota((TL, LANES), 0).astype(jnp.float32)
    for atom in range(CS):
        wz_ref[atom] = bump(z[atom : atom + 1] - nodes)

    own = iota((LANES, LANES), 0)
    at = iota((LANES, LANES), 1)
    order = (own == jnp.where(at < HALF, 2 * at, 2 * at - 127)).astype(jnp.bfloat16)
    ids = jnp.broadcast_to(tile_ref[...].astype(jnp.float32), (8, LANES)).astype(jnp.bfloat16)
    tiles = jnp.dot(ids, order, preferred_element_type=jnp.float32)
    tiles_ref[...] = tiles
    tiles = tiles[:1].astype(jnp.int32)

    for half in range(2):

        def step(atom, total, half=half):
            row = pl.ds(atom, 1)
            wz = wz_ref[atom]
            line = [wy_ref[j, row, :] * wz for j in range(TL)]
            new = []
            for i in range(4):
                wx = jnp.broadcast_to(wx_ref[4 * half + i, row, :], (TL, LANES))
                new += [total[8 * i + j] + wx * line[j] for j in range(TL)]
            return tuple(new)

        start = tuple(jnp.zeros((TL, LANES), jnp.float32) for _ in range(32))
        total = lax.fori_loop(0, CS, step, start, unroll=4)
        for slot in range(32):
            cell_ref[pl.ds((32 * half + slot) * TL, TL), :] = total[slot]

    cell = cell_ref[...]
    high = cell.astype(jnp.bfloat16)
    low = (cell - high.astype(jnp.float32)).astype(jnp.bfloat16)
    hot = (iota((GRID_ROWS, LANES), 0) == tiles).astype(jnp.bfloat16)
    fine = lax.dot_general(
        jnp.concatenate([hot, hot], axis=1), jnp.concatenate([high, low], axis=1), (((1,), (1,)), ((), ())),
        preferred_element_type=jnp.float32,
    )
    grid_ref[...] = fine.astype(jnp.bfloat16)

    moves[3].wait()
    moments = jnp.sum(fine * weights_ref[...], axis=1, keepdims=True)
    tx, ty, tz = tile_coords(iota((GRID_ROWS, LANES), 0))
    mine = corner_of((tx, ty, tz)) == (iota((GRID_ROWS, LANES), 1) & 7)
    coarse = jnp.sum(jnp.where(mine, moments, 0.0), axis=0, keepdims=True)
    coarse = coarse * (1.0 / math.sqrt(TP * 27))
    for line in range(coarse_ref.shape[0]):
        coarse_ref[line] = coarse

    own_row = (iota((HALF, LANES), 1) >> 1) == iota((HALF, LANES), 0)
    rows = jnp.where(own_row, tile_ref[...].astype(jnp.float32), 0.0).astype(jnp.bfloat16)
    side = ((iota((LANES, LANES), 0) & 1) == (iota((LANES, LANES), 1) >> 6)).astype(jnp.bfloat16)
    tile = jnp.dot(rows, side, preferred_element_type=jnp.float32).astype(jnp.int32)
    places = tile_coords(tile)
    corner_ref[...] = corner_of(places)
    drive_ref[...] = -charge
    for axis in range(3):
        frac_ref[axis] = (places[axis].astype(jnp.float32) * TL + pos_ref[axis]) * (1.0 / (TL * TD))
    for move in moves[4:]:
        move.wait()


def odd(axis):
    return lax.axis_index("cx" if axis == "gx" else axis) & 1


def face_kernel(grid_ref, near_x_ref, far_x_ref, near_y_ref, far_y_ref, near_z_ref, far_z_ref):
    row = iota((FACE, GRID_ROWS), 0)
    line = (row * 10923) >> 16
    ids = []
    for axis, (first, step) in zip(
        ("gx", "gy", "gz"), ((row, 180), (line * 36 + (row - line * TD), 30), (row * TD, 5)), strict=True
    ):
        side = odd(axis)
        ids += [first + step * (1 - side), first + step * side]
    tile = jnp.where(jnp.concatenate([row] * 6, axis=0) < TD * TD, jnp.concatenate(ids, axis=0), -1)
    hot = (iota((6 * FACE, GRID_ROWS), 1) == tile).astype(jnp.bfloat16)
    faces = jnp.dot(hot, grid_ref[...], preferred_element_type=jnp.float32).astype(jnp.bfloat16)
    for at, ref in enumerate((near_x_ref, far_x_ref, near_y_ref, far_y_ref, near_z_ref, far_z_ref)):
        ref[...] = faces[at * FACE : (at + 1) * FACE]


def coarse_kernel(column_ref, top_ref, face_ref, face_y_ref, own_ref, send_ref, pass_ref):
    lines = column_ref.shape[0]
    column = column_ref[...].reshape(lines, LANES)
    column = jnp.concatenate([column] * (lines * 8 // LANES), axis=1)
    shape = column.shape
    column = jnp.sum(jnp.where((iota(shape, 1) >> 3) == iota(shape, 0), column, 0.0), axis=0, keepdims=True)
    partial_value = jnp.sum(top_ref[...] * column, axis=1, keepdims=True)
    rows = partial_value.shape[0]
    lanes = jnp.where((iota((rows, LANES), 1) & 7) == (iota((rows, LANES), 0) & 7), partial_value, 0.0)
    lanes = jnp.sum(lanes.reshape(rows // 8, 8, LANES), axis=1)
    mine = iota((8, LANES), 1) >> 3 == iota((8, LANES), 0)
    lower, upper = (jnp.sum(jnp.where(mine, lanes[at : at + 8], 0.0), axis=0, keepdims=True) for at in (0, 8))
    half = jnp.broadcast_to(lax.axis_index("hx"), (1, LANES)) == 0
    own_ref[...] = jnp.where(half, lower, upper)
    rest = jnp.where(half, upper, lower)
    parts = []
    for _ in range(3):
        parts.append(rest.astype(jnp.bfloat16).astype(jnp.float32))
        rest = rest - parts[-1]
    sums = jnp.concatenate(parts + [jnp.zeros((1, LANES), jnp.float32)], axis=1)
    rows = face_ref[...].astype(jnp.float32)[:FAR_ROWS]
    send_ref[...] = jnp.where(iota((FAR_ROWS, TP), 0) == TD * TD, sums, rows).astype(jnp.bfloat16)
    pass_ref[...] = face_y_ref[...].astype(jnp.float32)[: pass_ref.shape[0]].astype(jnp.bfloat16)


def merge_kernel(own_ref, far_ref, field_any, out_ref):
    sums = far_ref[...].astype(jnp.float32)[TD * TD : TD * TD + 1]
    total = own_ref[...] + ((sums[:, :LANES] + sums[:, LANES : 2 * LANES]) + sums[:, 2 * LANES : 3 * LANES])
    for brick in range(8):
        out_ref[brick] = pltpu.roll(total, (LANES - 8 * brick) % LANES, 1) if brick else total


ATOM_ROWS = 16


def gradients(field_ref, wx, wy, wz, x, y, z):
    sums = [None] * 4
    for i in reversed(range(TL)):
        a = b = c = None
        for j in reversed(range(TL)):
            run = mean = None
            for k in reversed(range(TL)):
                term = wz[k] * field_ref[(i * TL + j) * TL + k : (i * TL + j) * TL + k + 1, :]
                run = term if run is None else run + term
                if k:
                    mean = run if mean is None else mean + run
            part = wy[j] * run
            cross = wy[j] * mean
            a = part if a is None else a + part
            c = cross if c is None else c + cross
            if j:
                b = a if b is None else b + a
        for at, value in enumerate((a, b, c)):
            term = wx[i] * value
            sums[at] = term if sums[at] is None else sums[at] + term
        if i:
            sums[3] = sums[0] if sums[3] is None else sums[3] + sums[0]
    total, with_y, with_z, with_x = sums
    return with_x - x * total, with_y - y * total, with_z - z * total


def tile_column(tiles_ref):
    return jnp.broadcast_to(tiles_ref[:1], (LANES, LANES)).T[:, :1].astype(jnp.int32)


def near_kernel(
    tiles_ref, grid_ref, near_x_ref, near_y_ref, near_z_ref, far_z_ref, blocks_ref, coord_ref, weights_ref,
    field_ref, unit_ref,
    ext_ref, flat_ref, grad_ref,
):
    ext_ref[0:GRID_ROWS] = grid_ref[...]
    for at, ref in enumerate((near_x_ref, near_y_ref, near_z_ref, far_z_ref)):
        ext_ref[GRID_ROWS + at * FACE : GRID_ROWS + (at + 1) * FACE] = ref[...]
    nothing = GRID_ROWS + 4 * FACE
    ext_ref[nothing:] = jnp.zeros((EXT_ROWS - nothing, TP), jnp.bfloat16)

    tile = tile_column(tiles_ref)
    tx, ty, tz = tile_coords(tile)
    row_x, row_y, row_z = ty * TD + tz, tx * TD + tz, tx * TD + ty
    base = GRID_ROWS
    edges = (
        ("gx", tx, 36, base + row_x, nothing + 0 * row_x),
        ("gy", ty, TD, base + FACE + row_y, nothing + 0 * row_y),
        ("gz", tz, 1, base + 2 * FACE + row_z, base + 3 * FACE + row_z),
    )
    targets = [tile]
    for axis, place, stride, near, far in edges:
        side = jnp.broadcast_to(odd(axis), near.shape) == 1
        targets.append(jnp.where(place < TD - 1, tile + stride, jnp.where(side, far, near)))
        targets.append(jnp.where(place > 0, tile - stride, jnp.where(side, near, far)))
    at_row = iota((LANES, EXT_ROWS), 1)
    field = None
    for at, target in enumerate(targets):
        hot = (at_row == target).astype(jnp.bfloat16)
        rows = jnp.dot(hot, ext_ref[...], preferred_element_type=jnp.float32).astype(jnp.bfloat16)
        flipped = at > 0 and at % 2 == 0
        term = lax.dot_general(
            rows, blocks_ref[(at + 1) // 2], (((1,), (0 if flipped else 1,)), ((), ())), preferred_element_type=jnp.float32
        )
        field = term if field is None else field + term
    field_ref[...] = field
    for part in range(TP // LANES):
        flat_ref[part * LANES : (part + 1) * LANES, :] = jnp.broadcast_to(
            weights_ref[:, part * LANES : (part + 1) * LANES], (LANES, LANES)
        ).T
    all_gradients(flat_ref, coord_ref, grad_ref)
    unit_ref[0], unit_ref[1] = to_atoms(grad_ref[0], grad_ref[1])
    unit_ref[2], _ = to_atoms(grad_ref[2], grad_ref[2])


def all_gradients(field_ref, coord_ref, grad_ref):
    @pl.loop(0, CS // ATOM_ROWS)
    def _(group):
        rows = pl.ds(pl.multiple_of(group * ATOM_ROWS, ATOM_ROWS), ATOM_ROWS)
        x, y, z = coord_ref[0, rows, :], coord_ref[1, rows, :], coord_ref[2, rows, :]
        wx, wy, wz = ([bump(u - node) for node in range(TL)] for u in (x, y, z))
        for axis, value in enumerate(gradients(field_ref, wx, wy, wz, x, y, z)):
            grad_ref[axis, rows, :] = value


def far_kernel(
    tiles_ref, part_ref, far_x_ref, far_y_ref, block_ref, coord_ref,
    near_ref,
    sum_ref, field_ref, grad_ref,
):
    tx, ty, tz = tile_coords(tile_column(tiles_ref))
    sum_ref[...] = part_ref[...]
    for axis, ref, place, row, block in (("gx", far_x_ref, tx, ty * TD + tz, 1), ("gy", far_y_ref, ty, tx * TD + tz, 2)):
        own_side = odd(axis)
        target = jnp.where(place == (TD - 1) * own_side, row, -1)
        hot = (iota((LANES, FACE), 1) == target).astype(jnp.bfloat16)
        rest = jnp.zeros((FACE - ref.shape[0], TP), jnp.float32)
        face = jnp.concatenate([ref[...].astype(jnp.float32), rest], axis=0).astype(jnp.bfloat16)
        rows = jnp.dot(hot, face, preferred_element_type=jnp.float32).astype(jnp.bfloat16)
        for side in range(2):

            @pl.when(own_side == side)
            def _(side=side, rows=rows, block=block):
                sum_ref[...] += lax.dot_general(
                    rows, block_ref[block], (((1,), (side,)), ((), ())), preferred_element_type=jnp.float32
                )

    for part in range(TP // LANES):
        field_ref[part * LANES : (part + 1) * LANES, :] = sum_ref[:, part * LANES : (part + 1) * LANES].T
    all_gradients(field_ref, coord_ref, grad_ref)
    near_ref[0], near_ref[1] = to_atoms(grad_ref[0], grad_ref[1])
    near_ref[2], _ = to_atoms(grad_ref[2], grad_ref[2])


def final_kernel(parts_ref, corner_ref, near_ref, unit_ref, frac_ref, drive_ref, force_ref, virial_ref):
    coarse = jnp.sum(parts_ref[...].reshape(parts_ref.shape[0], LANES), axis=0, keepdims=True)
    corner = corner_ref[...]
    pot = jnp.zeros((HALF, LANES), jnp.float32)
    for at in range(8):
        pot = jnp.where(corner == at, coarse[:, at : at + 1], pot)
    drive = drive_ref[...]
    forces = [drive * (near_ref[axis] + pot * unit_ref[axis]) for axis in range(3)]
    for axis in range(3):
        force_ref[axis] = forces[axis]
        virial_ref[axis] = frac_ref[axis] * forces[axis]
    virial_ref[3] = frac_ref[0] * forces[1]
    virial_ref[4] = frac_ref[0] * forces[2]
    virial_ref[5] = frac_ref[1] * forces[2]


VMEM = pl.BlockSpec(memory_space=pltpu.VMEM)
SMEM = pl.BlockSpec(memory_space=pltpu.SMEM)
ANY = pl.BlockSpec(memory_space=pl.ANY)


def f32(*shape):
    return jax.ShapeDtypeStruct(shape, jnp.float32)


def bf16(*shape):
    return jax.ShapeDtypeStruct(shape, jnp.bfloat16)


def exchanged(value, axis, far):
    count = lax.axis_size(axis)
    return lax.ppermute(value, axis, [(i, (i + (1 if (i + far) % 2 == 0 else -1)) % count) for i in range(count)])


def shards(positions, charges, cluster_tile, live_clusters, kernel_blocks, restrict_weights, top_kernel):
    pos = positions.reshape(3, HALF, LANES)
    charge = charges.reshape(HALF, LANES)
    tile = cluster_tile.reshape(1, LANES)
    live = live_clusters.reshape(1, 1)
    weights = restrict_weights.reshape(1, TP)
    lines = lax.axis_size("gz")

    grid, coarse, coords, tiles, drive, frac, corner, weights, blocks, top = pl.pallas_call(
        spread_kernel,
        out_shape=(
            bf16(GRID_ROWS, TP), f32(lines, 1, LANES), f32(3, CS, LANES), f32(8, LANES), f32(HALF, LANES),
            f32(3, HALF, LANES), jax.ShapeDtypeStruct((HALF, LANES), jnp.int32), f32(1, TP),
            bf16(*kernel_blocks.shape), f32(*top_kernel.shape),
        ),
        in_specs=[SMEM] + [ANY] * 6,
        out_specs=[VMEM] * 10,
        scratch_shapes=[
            pltpu.VMEM((3, HALF, LANES), jnp.float32), pltpu.VMEM((HALF, LANES), jnp.float32),
            pltpu.VMEM((1, LANES), jnp.int32),
            pltpu.VMEM((TL, CS, LANES), jnp.float32), pltpu.VMEM((TL, CS, LANES), jnp.float32),
            pltpu.VMEM((CS, TL, LANES), jnp.float32), pltpu.VMEM((TP, LANES), jnp.float32),
            pltpu.SemaphoreType.DMA((6,)),
        ],
        compiler_params=pltpu.CompilerParams(vmem_limit_bytes=12 << 20),
        cost_estimate=pl.CostEstimate(flops=10_000_000, bytes_accessed=1_000_000, transcendentals=200_000),
        name="spread",
    )(live, *(pltpu.with_memory_space_constraint(a, pltpu.HBM) for a in (pos, charge, tile, weights, kernel_blocks, top_kernel)))
    column = lax.all_to_all(coarse, "gz", 0, 0, tiled=True)

    faces = pl.pallas_call(
        face_kernel,
        out_shape=(bf16(FACE, TP),) * 6,
        in_specs=[VMEM],
        out_specs=[VMEM] * 6,
        compiler_params=pltpu.CompilerParams(vmem_limit_bytes=8 << 20),
        cost_estimate=pl.CostEstimate(flops=80_000_000, bytes_accessed=600_000, transcendentals=0),
        name="faces",
    )(grid)
    near_x, far_x, near_y, far_y, near_z, far_z = faces
    far_z, near_z = exchanged(far_z, "gz", 1), exchanged(near_z, "gz", 0)
    near_x = exchanged(near_x, ("hx", "cx"), 0)
    near_y = exchanged(near_y, "gy", 0)

    own, far_x, far_y = pl.pallas_call(
        coarse_kernel,
        out_shape=(f32(1, LANES), bf16(FAR_ROWS, TP), bf16(36, TP)),
        in_specs=[VMEM] * 4,
        out_specs=[VMEM] * 3,
        compiler_params=pltpu.CompilerParams(vmem_limit_bytes=8 << 20),
        cost_estimate=pl.CostEstimate(flops=70_000, bytes_accessed=200_000, transcendentals=0),
        name="coarse",
    )(column, top, far_x, far_y)
    far_x = exchanged(far_x, ("hx", "cx"), 1)
    far_y = exchanged(far_y, "gy", 1)

    field, unit = pl.pallas_call(
        near_kernel,
        out_shape=(f32(LANES, TP), f32(3, HALF, LANES)),
        in_specs=[VMEM] * 9,
        out_specs=[VMEM] * 2,
        scratch_shapes=[
            pltpu.VMEM((EXT_ROWS, TP), jnp.bfloat16), pltpu.VMEM((TP, LANES), jnp.float32),
            pltpu.VMEM((3, CS, LANES), jnp.float32),
        ],
        compiler_params=pltpu.CompilerParams(vmem_limit_bytes=16 << 20),
        cost_estimate=pl.CostEstimate(flops=1000, bytes_accessed=1000, transcendentals=0),
        name="near",
    )(tiles, grid, near_x, near_y, near_z, far_z, blocks, coords, weights)

    parts = pl.pallas_call(
        merge_kernel,
        out_shape=f32(8, 1, LANES),
        in_specs=[VMEM] * 2 + [ANY],
        out_specs=VMEM,
        compiler_params=pltpu.CompilerParams(vmem_limit_bytes=4 << 20),
        cost_estimate=pl.CostEstimate(flops=10_000, bytes_accessed=60_000, transcendentals=0),
        name="merge",
    )(own, far_x, field)
    parts = lax.all_to_all(parts, ("cx", "gy"), 0, 0, tiled=True)

    near = pl.pallas_call(
        far_kernel,
        out_shape=f32(3, HALF, LANES),
        in_specs=[VMEM] * 6,
        out_specs=VMEM,
        scratch_shapes=[
            pltpu.VMEM((LANES, TP), jnp.float32), pltpu.VMEM((TP, LANES), jnp.float32),
            pltpu.VMEM((3, CS, LANES), jnp.float32),
        ],
        compiler_params=pltpu.CompilerParams(vmem_limit_bytes=16 << 20),
        cost_estimate=pl.CostEstimate(flops=1_000_000_000, bytes_accessed=4_000_000, transcendentals=200_000),
        name="far",
    )(tiles, field, far_x, far_y, blocks, coords)

    forces, virial = pl.pallas_call(
        final_kernel,
        out_shape=(f32(3, HALF, LANES), f32(6, HALF, LANES)),
        in_specs=[VMEM] * 6,
        out_specs=[VMEM] * 2,
        compiler_params=pltpu.CompilerParams(vmem_limit_bytes=8 << 20),
        cost_estimate=pl.CostEstimate(flops=500_000, bytes_accessed=600_000, transcendentals=0),
        name="final",
    )(parts, corner, near, unit, frac, drive)
    return forces.reshape(3, 1, 1, 1, -1), virial.reshape(6, 1, 1, 1, -1)


def solution(mesh):
    wide, high, deep = (mesh.shape[axis] for axis in ("gx", "gy", "gz"))
    split = jax.sharding.Mesh(mesh.devices.reshape(wide // 2, 2, high, deep), ("hx", "cx", "gy", "gz"))
    x = ("hx", "cx")
    placed = (
        P(None, x, "gy", "gz", None),
        P(x, "gy", "gz", None),
        P(x, "gy", "gz", None),
        P(x, "gy", "gz"),
        P(),
        P(),
        P("gz", ("hx", "cx", "gy")),
    )
    return jax.shard_map(
        shards,
        mesh=split,
        in_specs=placed,
        out_specs=(P(None, x, "gy", "gz", None), P(None, x, "gy", "gz", None)),
        check_vma=False,
    )
```

```python
import math

import jax
import jax.numpy as jnp
from jax import lax
from jax.experimental import pallas as pl
from jax.experimental.pallas import tpu as pltpu
from jax.sharding import PartitionSpec as P

TL = 8
TP = 512
CS = 64
TD = 6
CUBES = TD**3
FACE = 48
GRID_ROWS = 256
FAR_ROWS = 40
HALF = CS
LANES = 128


def iota(shape, axis):
    return lax.broadcasted_iota(jnp.int32, shape, axis)


def tile_coords(tile):
    plane = (tile * 10923) >> 16
    tx = (tile * 1821) >> 16
    return tx, plane - tx * TD, tile - plane * TD


def to_clusters(upper, lower):
    both = jnp.concatenate([upper, lower], axis=0).T
    even, odd = both[:HALF], both[HALF:]
    left = iota((HALF, LANES), 1) < HALF
    return (
        jnp.where(left, even, pltpu.roll(odd, HALF, 1)),
        jnp.where(left, pltpu.roll(even, HALF, 1), odd),
    )


def to_atoms(upper, lower):
    left = iota((HALF, LANES), 1) < HALF
    even = jnp.where(left, upper, pltpu.roll(lower, HALF, 1))
    odd = jnp.where(left, pltpu.roll(upper, HALF, 1), lower)
    both = jnp.concatenate([even, odd], axis=0).T
    return both[:HALF], both[HALF:]


def corner_of(places):
    tx, ty, tz = ((place >= TD // 2).astype(jnp.int32) for place in places)
    return (tx * 2 + ty) * 2 + tz


def bump(offset):
    return jnp.exp(-0.5 * offset * offset)


def spread_kernel(
    live_ref, pos_any, charge_any, tile_any, weights_any, blocks_any, top_any,
    grid_ref, coarse_any, coord_ref, tiles_ref, frac_ref, corner_ref, weights_ref, blocks_ref, top_ref, wx_any, wy_any,
    pos_ref, charge_ref, tile_ref, wx_ref, wy_ref, wz_ref, cell_ref, coarse_ref, sems,
):
    moves = [
        pltpu.make_async_copy(source, target, sems.at[at])
        for at, (source, target) in enumerate(
            (
                (pos_any, pos_ref), (charge_any, charge_ref), (tile_any, tile_ref),
                (weights_any, weights_ref), (blocks_any, blocks_ref), (top_any, top_ref),
                (wx_ref, wx_any), (wy_ref, wy_any), (coarse_ref, coarse_any),
            )
        )
    ]
    for move in moves[:4]:
        move.start()
    for move in moves[:3]:
        move.wait()
    for move in moves[4:6]:
        move.start()
    cluster = 2 * iota((HALF, LANES), 0) + (iota((HALF, LANES), 1) >> 6)
    charge = charge_ref[...] * (cluster < live_ref[0, 0]).astype(jnp.float32)
    x, y = to_clusters(pos_ref[0], pos_ref[1])
    z, q = to_clusters(pos_ref[2], charge)
    coord_ref[0], coord_ref[1], coord_ref[2] = x, y, z
    for node in range(TL):
        wx_ref[node] = q * bump(x - node)
        wy_ref[node] = bump(y - node)
    moves[6].start()
    moves[7].start()
    nodes = iota((TL, LANES), 0).astype(jnp.float32)
    for atom in range(CS):
        wz_ref[atom] = bump(z[atom : atom + 1] - nodes)

    own = iota((LANES, LANES), 0)
    at = iota((LANES, LANES), 1)
    order = (own == jnp.where(at < HALF, 2 * at, 2 * at - 127)).astype(jnp.bfloat16)
    ids = jnp.broadcast_to(tile_ref[...].astype(jnp.float32), (8, LANES)).astype(jnp.bfloat16)
    tiles = jnp.dot(ids, order, preferred_element_type=jnp.float32)
    tiles_ref[...] = tiles
    tiles = tiles[:1].astype(jnp.int32)

    for half in range(2):

        def step(atom, total, half=half):
            row = pl.ds(atom, 1)
            wz = wz_ref[atom]
            line = [wy_ref[j, row, :] * wz for j in range(TL)]
            new = []
            for i in range(4):
                wx = jnp.broadcast_to(wx_ref[4 * half + i, row, :], (TL, LANES))
                new += [total[8 * i + j] + wx * line[j] for j in range(TL)]
            return tuple(new)

        start = tuple(jnp.zeros((TL, LANES), jnp.float32) for _ in range(32))
        total = lax.fori_loop(0, CS, step, start, unroll=4)
        for slot in range(32):
            cell_ref[pl.ds((32 * half + slot) * TL, TL), :] = total[slot]

    cell = cell_ref[...]
    high = cell.astype(jnp.bfloat16)
    low = (cell - high.astype(jnp.float32)).astype(jnp.bfloat16)
    hot = (iota((GRID_ROWS, LANES), 0) == tiles).astype(jnp.bfloat16)
    fine = lax.dot_general(
        jnp.concatenate([hot, hot], axis=1), jnp.concatenate([high, low], axis=1), (((1,), (1,)), ((), ())),
        preferred_element_type=jnp.float32,
    )
    grid_ref[...] = fine.astype(jnp.bfloat16)

    moves[3].wait()
    moments = jnp.sum(fine * weights_ref[...], axis=1, keepdims=True)
    tx, ty, tz = tile_coords(iota((GRID_ROWS, LANES), 0))
    mine = corner_of((tx, ty, tz)) == (iota((GRID_ROWS, LANES), 1) & 7)
    coarse = jnp.sum(jnp.where(mine, moments, 0.0), axis=0, keepdims=True)
    coarse = coarse * (1.0 / math.sqrt(TP * 27))
    for line in range(coarse_ref.shape[0]):
        coarse_ref[line] = coarse
    moves[8].start()

    own_row = (iota((HALF, LANES), 1) >> 1) == iota((HALF, LANES), 0)
    rows = jnp.where(own_row, tile_ref[...].astype(jnp.float32), 0.0).astype(jnp.bfloat16)
    side = ((iota((LANES, LANES), 0) & 1) == (iota((LANES, LANES), 1) >> 6)).astype(jnp.bfloat16)
    tile = jnp.dot(rows, side, preferred_element_type=jnp.float32).astype(jnp.int32)
    places = tile_coords(tile)
    corner_ref[...] = corner_of(places)
    for axis in range(3):
        frac_ref[axis] = (places[axis].astype(jnp.float32) * TL + pos_ref[axis]) * (1.0 / (TL * TD))
    for move in moves[4:]:
        move.wait()


def odd(axis):
    return lax.axis_index("cx" if axis == "gx" else axis) & 1


def face_kernel(grid_ref, near_x_ref, far_x_ref, near_y_ref, far_y_ref, near_z_ref, far_z_ref):
    row = iota((FACE, GRID_ROWS), 0)
    line = (row * 10923) >> 16
    ids = []
    for axis, (first, step) in zip(
        ("gx", "gy", "gz"), ((row, 180), (line * 36 + (row - line * TD), 30), (row * TD, 5)), strict=True
    ):
        side = odd(axis)
        ids += [first + step * (1 - side), first + step * side]
    tile = jnp.where(jnp.concatenate([row] * 6, axis=0) < TD * TD, jnp.concatenate(ids, axis=0), -1)
    hot = (iota((6 * FACE, GRID_ROWS), 1) == tile).astype(jnp.bfloat16)
    faces = jnp.dot(hot, grid_ref[...], preferred_element_type=jnp.float32).astype(jnp.bfloat16)
    for at, ref in enumerate((near_x_ref, far_x_ref, near_y_ref, far_y_ref, near_z_ref, far_z_ref)):
        ref[...] = faces[at * FACE : (at + 1) * FACE]


def coarse_kernel(column_ref, top_ref, face_ref, face_y_ref, own_ref, send_ref, pass_ref):
    lines = column_ref.shape[0]
    column = column_ref[...].reshape(lines, LANES)
    column = jnp.concatenate([column] * (lines * 8 // LANES), axis=1)
    shape = column.shape
    column = jnp.sum(jnp.where((iota(shape, 1) >> 3) == iota(shape, 0), column, 0.0), axis=0, keepdims=True)
    partial_value = jnp.sum(top_ref[...] * column, axis=1, keepdims=True)
    rows = partial_value.shape[0]
    lanes = jnp.where((iota((rows, LANES), 1) & 7) == (iota((rows, LANES), 0) & 7), partial_value, 0.0)
    lanes = jnp.sum(lanes.reshape(rows // 8, 8, LANES), axis=1)
    mine = iota((8, LANES), 1) >> 3 == iota((8, LANES), 0)
    lower, upper = (jnp.sum(jnp.where(mine, lanes[at : at + 8], 0.0), axis=0, keepdims=True) for at in (0, 8))
    half = jnp.broadcast_to(lax.axis_index("hx"), (1, LANES)) == 0
    own_ref[...] = jnp.where(half, lower, upper)
    rest = jnp.where(half, upper, lower)
    parts = []
    for _ in range(3):
        parts.append(rest.astype(jnp.bfloat16).astype(jnp.float32))
        rest = rest - parts[-1]
    sums = jnp.concatenate(parts + [jnp.zeros((1, LANES), jnp.float32)], axis=1)
    rows = face_ref[...].astype(jnp.float32)[:FAR_ROWS]
    send_ref[...] = jnp.where(iota((FAR_ROWS, TP), 0) == TD * TD, sums, rows).astype(jnp.bfloat16)
    pass_ref[...] = face_y_ref[...].astype(jnp.float32)[: pass_ref.shape[0]].astype(jnp.bfloat16)


def merge_kernel(own_ref, far_ref, field_any, out_ref):
    sums = far_ref[...].astype(jnp.float32)[TD * TD : TD * TD + 1]
    total = own_ref[...] + ((sums[:, :LANES] + sums[:, LANES : 2 * LANES]) + sums[:, 2 * LANES : 3 * LANES])
    for brick in range(8):
        out_ref[brick] = pltpu.roll(total, (LANES - 8 * brick) % LANES, 1) if brick else total


ATOM_ROWS = 16


def gradients(field_ref, wx, wy, wz, x, y, z):
    sums = [None] * 4
    for i in reversed(range(TL)):
        a = b = c = None
        for j in reversed(range(TL)):
            run = mean = None
            for k in reversed(range(TL)):
                term = wz[k] * field_ref[(i * TL + j) * TL + k : (i * TL + j) * TL + k + 1, :]
                run = term if run is None else run + term
                if k:
                    mean = run if mean is None else mean + run
            weight = wy(j)
            part = weight * run
            cross = weight * mean
            a = part if a is None else a + part
            c = cross if c is None else c + cross
            if j:
                b = a if b is None else b + a
        weight = wx(i)
        for at, value in enumerate((a, b, c)):
            term = weight * value
            sums[at] = term if sums[at] is None else sums[at] + term
        if i:
            sums[3] = sums[0] if sums[3] is None else sums[3] + sums[0]
    total, with_y, with_z, with_x = sums
    return with_x - x * total, with_y - y * total, with_z - z * total


def tile_column(tiles_ref):
    return jnp.broadcast_to(tiles_ref[:1], (LANES, LANES)).T[:, :1].astype(jnp.int32)


def near_kernel(
    tiles_ref, grid_ref, near_x_ref, near_y_ref, near_z_ref, far_z_ref, blocks_ref, coord_ref, weights_ref, wx_any, wy_any,
    field_ref, unit_ref,
    flat_ref, grad_ref, wx_ref, wy_ref, sems,
):
    moves = read_weights(wx_any, wy_any, wx_ref, wy_ref, sems)
    tile = tile_column(tiles_ref)
    tx, ty, tz = tile_coords(tile)
    row_x, row_y, row_z = ty * TD + tz, tx * TD + tz, tx * TD + ty

    def picked(ref, row):
        hot = (iota((LANES, ref.shape[0]), 1) == row).astype(jnp.bfloat16)
        return jnp.dot(hot, ref[...], preferred_element_type=jnp.float32)

    field = lax.dot_general(
        picked(grid_ref, tile).astype(jnp.bfloat16), blocks_ref[0], (((1,), (1,)), ((), ())), preferred_element_type=jnp.float32
    )
    edges = (
        ("gx", tx, 36, row_x, near_x_ref, None),
        ("gy", ty, TD, row_y, near_y_ref, None),
        ("gz", tz, 1, row_z, near_z_ref, far_z_ref),
    )
    for block, (axis, place, stride, row, near_face, far_face) in enumerate(edges, 1):
        side = jnp.broadcast_to(odd(axis), row.shape)
        for down in range(2):
            edge = place == (TD - 1) * (1 - down)
            rows = picked(grid_ref, jnp.where(edge, -1, tile + (1 - 2 * down) * stride))
            rows += picked(near_face, jnp.where(edge & (side == down), row, -1))
            if far_face is not None:
                rows += picked(far_face, jnp.where(edge & (side != down), row, -1))
            field += lax.dot_general(
                rows.astype(jnp.bfloat16), blocks_ref[block], (((1,), (1 - down,)), ((), ())),
                preferred_element_type=jnp.float32,
            )
    field_ref[...] = field
    for part in range(TP // LANES):
        flat_ref[part * LANES : (part + 1) * LANES, :] = jnp.broadcast_to(
            weights_ref[:, part * LANES : (part + 1) * LANES], (LANES, LANES)
        ).T
    for move in moves:
        move.wait()
    all_gradients(flat_ref, coord_ref, wx_ref, wy_ref, grad_ref)
    unit_ref[0], unit_ref[1] = to_atoms(grad_ref[0], grad_ref[1])
    unit_ref[2], _ = to_atoms(grad_ref[2], grad_ref[2])


def read_weights(wx_any, wy_any, wx_ref, wy_ref, sems):
    moves = [pltpu.make_async_copy(wx_any, wx_ref, sems.at[0]), pltpu.make_async_copy(wy_any, wy_ref, sems.at[1])]
    for move in moves:
        move.start()
    return moves


def all_gradients(field_ref, coord_ref, wx_ref, wy_ref, grad_ref):
    @pl.loop(0, CS // ATOM_ROWS)
    def _(group):
        rows = pl.ds(pl.multiple_of(group * ATOM_ROWS, ATOM_ROWS), ATOM_ROWS)
        x, y, z = coord_ref[0, rows, :], coord_ref[1, rows, :], coord_ref[2, rows, :]
        wz = [bump(z - node) for node in range(TL)]
        values = gradients(field_ref, lambda i: wx_ref[i, rows, :], lambda j: wy_ref[j, rows, :], wz, x, y, z)
        for axis, value in enumerate(values):
            grad_ref[axis, rows, :] = -value


def far_kernel(
    tiles_ref, part_ref, far_x_ref, far_y_ref, block_ref, coord_ref, wx_any, wy_any,
    near_ref,
    sum_ref, field_ref, grad_ref, wx_ref, wy_ref, sems,
):
    moves = read_weights(wx_any, wy_any, wx_ref, wy_ref, sems)
    tx, ty, tz = tile_coords(tile_column(tiles_ref))
    sum_ref[...] = part_ref[...]
    for axis, ref, place, row, block in (("gx", far_x_ref, tx, ty * TD + tz, 1), ("gy", far_y_ref, ty, tx * TD + tz, 2)):
        own_side = odd(axis)
        target = jnp.where(place == (TD - 1) * own_side, row, -1)
        hot = (iota((LANES, FACE), 1) == target).astype(jnp.bfloat16)
        rest = jnp.zeros((FACE - ref.shape[0], TP), jnp.float32)
        face = jnp.concatenate([ref[...].astype(jnp.float32), rest], axis=0).astype(jnp.bfloat16)
        rows = jnp.dot(hot, face, preferred_element_type=jnp.float32).astype(jnp.bfloat16)
        for side in range(2):

            @pl.when(own_side == side)
            def _(side=side, rows=rows, block=block):
                sum_ref[...] += lax.dot_general(
                    rows, block_ref[block], (((1,), (side,)), ((), ())), preferred_element_type=jnp.float32
                )

    for part in range(TP // LANES):
        field_ref[part * LANES : (part + 1) * LANES, :] = sum_ref[:, part * LANES : (part + 1) * LANES].T
    for move in moves:
        move.wait()
    all_gradients(field_ref, coord_ref, wx_ref, wy_ref, grad_ref)
    near_ref[0], near_ref[1] = to_atoms(grad_ref[0], grad_ref[1])
    near_ref[2], _ = to_atoms(grad_ref[2], grad_ref[2])


def final_kernel(parts_ref, corner_ref, near_ref, unit_ref, frac_ref, force_ref, virial_ref):
    coarse = jnp.sum(parts_ref[...].reshape(parts_ref.shape[0], LANES), axis=0, keepdims=True)
    corner = corner_ref[...]
    pot = jnp.zeros((HALF, LANES), jnp.float32)
    for at in range(8):
        pot = jnp.where(corner == at, coarse[:, at : at + 1], pot)
    forces = [near_ref[axis] + pot * unit_ref[axis] for axis in range(3)]
    for axis in range(3):
        force_ref[axis] = forces[axis]
        virial_ref[axis] = frac_ref[axis] * forces[axis]
    virial_ref[3] = frac_ref[0] * forces[1]
    virial_ref[4] = frac_ref[0] * forces[2]
    virial_ref[5] = frac_ref[1] * forces[2]


VMEM = pl.BlockSpec(memory_space=pltpu.VMEM)
SMEM = pl.BlockSpec(memory_space=pltpu.SMEM)
ANY = pl.BlockSpec(memory_space=pl.ANY)
HBM = pl.BlockSpec(memory_space=pltpu.HBM)


def f32(*shape):
    return jax.ShapeDtypeStruct(shape, jnp.float32)


def bf16(*shape):
    return jax.ShapeDtypeStruct(shape, jnp.bfloat16)


def exchanged(value, axis, far):
    count = lax.axis_size(axis)
    return lax.ppermute(value, axis, [(i, (i + (1 if (i + far) % 2 == 0 else -1)) % count) for i in range(count)])


def shards(positions, charges, cluster_tile, live_clusters, kernel_blocks, restrict_weights, top_kernel):
    pos = positions.reshape(3, HALF, LANES)
    charge = charges.reshape(HALF, LANES)
    tile = cluster_tile.reshape(1, LANES)
    live = live_clusters.reshape(1, 1)
    weights = restrict_weights.reshape(1, TP)
    lines = lax.axis_size("gz")

    grid, coarse, coords, tiles, frac, corner, weights, blocks, top, wx, wy = pl.pallas_call(
        spread_kernel,
        out_shape=(
            bf16(GRID_ROWS, TP), f32(lines, 1, LANES), f32(3, CS, LANES), f32(8, LANES),
            f32(3, HALF, LANES), jax.ShapeDtypeStruct((HALF, LANES), jnp.int32), f32(1, TP),
            bf16(*kernel_blocks.shape), f32(*top_kernel.shape), pltpu.HBM((TL, CS, LANES), jnp.float32), pltpu.HBM((TL, CS, LANES), jnp.float32),
        ),
        in_specs=[SMEM] + [ANY] * 6,
        out_specs=[VMEM, HBM] + [VMEM] * 7 + [HBM] * 2,
        scratch_shapes=[
            pltpu.VMEM((3, HALF, LANES), jnp.float32), pltpu.VMEM((HALF, LANES), jnp.float32),
            pltpu.VMEM((1, LANES), jnp.int32),
            pltpu.VMEM((TL, CS, LANES), jnp.float32), pltpu.VMEM((TL, CS, LANES), jnp.float32),
            pltpu.VMEM((CS, TL, LANES), jnp.float32), pltpu.VMEM((TP, LANES), jnp.float32),
            pltpu.VMEM((lines, 1, LANES), jnp.float32), pltpu.SemaphoreType.DMA((9,)),
        ],
        compiler_params=pltpu.CompilerParams(vmem_limit_bytes=12 << 20),
        cost_estimate=pl.CostEstimate(flops=10_000_000, bytes_accessed=1_000_000, transcendentals=200_000),
        name="spread",
    )(live, *(pltpu.with_memory_space_constraint(a, pltpu.HBM) for a in (pos, charge, tile, weights, kernel_blocks, top_kernel)))
    wx, wy = (pltpu.with_memory_space_constraint(a, pltpu.HBM) for a in (wx, wy))
    column = lax.all_to_all(coarse, "gz", 0, 0, tiled=True)

    faces = pl.pallas_call(
        face_kernel,
        out_shape=(bf16(FACE, TP),) * 6,
        in_specs=[VMEM],
        out_specs=[VMEM] * 6,
        compiler_params=pltpu.CompilerParams(vmem_limit_bytes=8 << 20),
        cost_estimate=pl.CostEstimate(flops=80_000_000, bytes_accessed=600_000, transcendentals=0),
        name="faces",
    )(grid)
    near_x, far_x, near_y, far_y, near_z, far_z = faces
    far_z, near_z = exchanged(far_z, "gz", 1), exchanged(near_z, "gz", 0)
    near_x = exchanged(near_x, ("hx", "cx"), 0)
    near_y = exchanged(near_y, "gy", 0)

    own, far_x, far_y = pl.pallas_call(
        coarse_kernel,
        out_shape=(f32(1, LANES), bf16(FAR_ROWS, TP), bf16(36, TP)),
        in_specs=[VMEM] * 4,
        out_specs=[VMEM] * 3,
        compiler_params=pltpu.CompilerParams(vmem_limit_bytes=8 << 20),
        cost_estimate=pl.CostEstimate(flops=70_000, bytes_accessed=200_000, transcendentals=0),
        name="coarse",
    )(column, top, far_x, far_y)
    far_x = exchanged(far_x, ("hx", "cx"), 1)
    far_y = exchanged(far_y, "gy", 1)

    field, unit = pl.pallas_call(
        near_kernel,
        out_shape=(f32(LANES, TP), f32(3, HALF, LANES)),
        in_specs=[VMEM] * 9 + [HBM] * 2,
        out_specs=[VMEM] * 2,
        scratch_shapes=[
            pltpu.VMEM((TP, LANES), jnp.float32), pltpu.VMEM((3, CS, LANES), jnp.float32),
            pltpu.VMEM((TL, CS, LANES), jnp.float32), pltpu.VMEM((TL, CS, LANES), jnp.float32), pltpu.SemaphoreType.DMA((2,)),
        ],
        compiler_params=pltpu.CompilerParams(vmem_limit_bytes=16 << 20),
        cost_estimate=pl.CostEstimate(flops=1000, bytes_accessed=1000, transcendentals=0),
        name="near",
    )(tiles, grid, near_x, near_y, near_z, far_z, blocks, coords, weights, wx, wy)

    parts = pl.pallas_call(
        merge_kernel,
        out_shape=f32(8, 1, LANES),
        in_specs=[VMEM] * 2 + [ANY],
        out_specs=VMEM,
        compiler_params=pltpu.CompilerParams(vmem_limit_bytes=4 << 20),
        cost_estimate=pl.CostEstimate(flops=10_000, bytes_accessed=60_000, transcendentals=0),
        name="merge",
    )(own, far_x, field)
    parts = lax.all_to_all(parts, ("cx", "gy"), 0, 0, tiled=True)

    near = pl.pallas_call(
        far_kernel,
        out_shape=f32(3, HALF, LANES),
        in_specs=[VMEM] * 6 + [HBM] * 2,
        out_specs=VMEM,
        scratch_shapes=[
            pltpu.VMEM((LANES, TP), jnp.float32), pltpu.VMEM((TP, LANES), jnp.float32),
            pltpu.VMEM((3, CS, LANES), jnp.float32),
            pltpu.VMEM((TL, CS, LANES), jnp.float32), pltpu.VMEM((TL, CS, LANES), jnp.float32), pltpu.SemaphoreType.DMA((2,)),
        ],
        compiler_params=pltpu.CompilerParams(vmem_limit_bytes=16 << 20),
        cost_estimate=pl.CostEstimate(flops=1_000_000_000, bytes_accessed=4_000_000, transcendentals=200_000),
        name="far",
    )(tiles, field, far_x, far_y, blocks, coords, wx, wy)

    forces, virial = pl.pallas_call(
        final_kernel,
        out_shape=(f32(3, HALF, LANES), f32(6, HALF, LANES)),
        in_specs=[VMEM] * 5,
        out_specs=[VMEM] * 2,
        compiler_params=pltpu.CompilerParams(vmem_limit_bytes=8 << 20),
        cost_estimate=pl.CostEstimate(flops=500_000, bytes_accessed=600_000, transcendentals=0),
        name="final",
    )(parts, corner, near, unit, frac)
    return forces.reshape(3, 1, 1, 1, -1), virial.reshape(6, 1, 1, 1, -1)


def solution(mesh):
    wide, high, deep = (mesh.shape[axis] for axis in ("gx", "gy", "gz"))
    split = jax.sharding.Mesh(mesh.devices.reshape(wide // 2, 2, high, deep), ("hx", "cx", "gy", "gz"))
    x = ("hx", "cx")
    placed = (
        P(None, x, "gy", "gz", None),
        P(x, "gy", "gz", None),
        P(x, "gy", "gz", None),
        P(x, "gy", "gz"),
        P(),
        P(),
        P("gz", ("hx", "cx", "gy")),
    )
    return jax.shard_map(
        shards,
        mesh=split,
        in_specs=placed,
        out_specs=(P(None, x, "gy", "gz", None), P(None, x, "gy", "gz", None)),
        check_vma=False,
    )
```

```python
import math

import jax
import jax.numpy as jnp
from jax import lax
from jax.experimental import pallas as pl
from jax.experimental.pallas import tpu as pltpu
from jax.sharding import PartitionSpec as P

TL = 8
TP = 512
CS = 64
TD = 6
CUBES = TD**3
FACE = 48
GRID_ROWS = 256
FAR_ROWS = 40
EXT_ROWS = 512
HALF = CS
LANES = 128


def iota(shape, axis):
    return lax.broadcasted_iota(jnp.int32, shape, axis)


def tile_coords(tile):
    plane = (tile * 10923) >> 16
    tx = (tile * 1821) >> 16
    return tx, plane - tx * TD, tile - plane * TD


def to_clusters(upper, lower):
    both = jnp.concatenate([upper, lower], axis=0).T
    even, odd = both[:HALF], both[HALF:]
    left = iota((HALF, LANES), 1) < HALF
    return (
        jnp.where(left, even, pltpu.roll(odd, HALF, 1)),
        jnp.where(left, pltpu.roll(even, HALF, 1), odd),
    )


def to_atoms(upper, lower):
    left = iota((HALF, LANES), 1) < HALF
    even = jnp.where(left, upper, pltpu.roll(lower, HALF, 1))
    odd = jnp.where(left, pltpu.roll(upper, HALF, 1), lower)
    both = jnp.concatenate([even, odd], axis=0).T
    return both[:HALF], both[HALF:]


def corner_of(places):
    tx, ty, tz = ((place >= TD // 2).astype(jnp.int32) for place in places)
    return (tx * 2 + ty) * 2 + tz


def bump(offset):
    return jnp.exp(-0.5 * offset * offset)


def spread_kernel(
    live_ref, pos_any, charge_any, tile_any, weights_any, blocks_any, top_any,
    grid_ref, coarse_ref, coord_ref, tiles_ref, drive_ref, frac_ref, corner_ref, weights_ref, blocks_ref, top_ref,
    pos_ref, charge_ref, tile_ref, wx_ref, wy_ref, wz_ref, cell_ref, sems,
):
    moves = [
        pltpu.make_async_copy(source, target, sems.at[at])
        for at, (source, target) in enumerate(
            (
                (pos_any, pos_ref), (charge_any, charge_ref), (tile_any, tile_ref),
                (weights_any, weights_ref), (blocks_any, blocks_ref), (top_any, top_ref),
            )
        )
    ]
    for move in moves:
        move.start()
    for move in moves[:3]:
        move.wait()
    cluster = 2 * iota((HALF, LANES), 0) + (iota((HALF, LANES), 1) >> 6)
    charge = charge_ref[...] * (cluster < live_ref[0, 0]).astype(jnp.float32)
    x, y = to_clusters(pos_ref[0], pos_ref[1])
    z, q = to_clusters(pos_ref[2], charge)
    coord_ref[0], coord_ref[1], coord_ref[2] = x, y, z
    for node in range(TL):
        wx_ref[node] = q * bump(x - node)
        wy_ref[node] = bump(y - node)
    nodes = iota((TL, LANES), 0).astype(jnp.float32)
    for atom in range(CS):
        wz_ref[atom] = bump(z[atom : atom + 1] - nodes)

    own = iota((LANES, LANES), 0)
    at = iota((LANES, LANES), 1)
    order = (own == jnp.where(at < HALF, 2 * at, 2 * at - 127)).astype(jnp.bfloat16)
    ids = jnp.broadcast_to(tile_ref[...].astype(jnp.float32), (8, LANES)).astype(jnp.bfloat16)
    tiles = jnp.dot(ids, order, preferred_element_type=jnp.float32)
    tiles_ref[...] = tiles
    tiles = tiles[:1].astype(jnp.int32)

    for half in range(2):

        def step(atom, total, half=half):
            row = pl.ds(atom, 1)
            wz = wz_ref[atom]
            line = [wy_ref[j, row, :] * wz for j in range(TL)]
            new = []
            for i in range(4):
                wx = jnp.broadcast_to(wx_ref[4 * half + i, row, :], (TL, LANES))
                new += [total[8 * i + j] + wx * line[j] for j in range(TL)]
            return tuple(new)

        start = tuple(jnp.zeros((TL, LANES), jnp.float32) for _ in range(32))
        total = lax.fori_loop(0, CS, step, start, unroll=4)
        for slot in range(32):
            cell_ref[pl.ds((32 * half + slot) * TL, TL), :] = total[slot]

    cell = cell_ref[...]
    high = cell.astype(jnp.bfloat16)
    low = (cell - high.astype(jnp.float32)).astype(jnp.bfloat16)
    hot = (iota((GRID_ROWS, LANES), 0) == tiles).astype(jnp.bfloat16)
    fine = lax.dot_general(
        jnp.concatenate([hot, hot], axis=1), jnp.concatenate([high, low], axis=1), (((1,), (1,)), ((), ())),
        preferred_element_type=jnp.float32,
    )
    grid_ref[...] = fine.astype(jnp.bfloat16)

    moves[3].wait()
    moments = jnp.sum(fine * weights_ref[...], axis=1, keepdims=True)
    tx, ty, tz = tile_coords(iota((GRID_ROWS, LANES), 0))
    mine = corner_of((tx, ty, tz)) == (iota((GRID_ROWS, LANES), 1) & 7)
    coarse = jnp.sum(jnp.where(mine, moments, 0.0), axis=0, keepdims=True)
    coarse = coarse * (1.0 / math.sqrt(TP * 27))
    for line in range(coarse_ref.shape[0]):
        coarse_ref[line] = coarse

    own_row = (iota((HALF, LANES), 1) >> 1) == iota((HALF, LANES), 0)
    rows = jnp.where(own_row, tile_ref[...].astype(jnp.float32), 0.0).astype(jnp.bfloat16)
    side = ((iota((LANES, LANES), 0) & 1) == (iota((LANES, LANES), 1) >> 6)).astype(jnp.bfloat16)
    tile = jnp.dot(rows, side, preferred_element_type=jnp.float32).astype(jnp.int32)
    places = tile_coords(tile)
    corner_ref[...] = corner_of(places)
    drive_ref[...] = -charge
    for axis in range(3):
        frac_ref[axis] = (places[axis].astype(jnp.float32) * TL + pos_ref[axis]) * (1.0 / (TL * TD))
    for move in moves[4:]:
        move.wait()


def odd(axis):
    return lax.axis_index("cx" if axis == "gx" else axis) & 1


def face_kernel(grid_ref, near_x_ref, far_x_ref, near_z_ref, far_z_ref, y_ref):
    row = iota((FACE, GRID_ROWS), 0)
    line = (row * 10923) >> 16
    side_x, side_z = odd("gx"), odd("gz")
    low_y = line * 36 + (row - line * TD)
    ids = [row + 180 * (1 - side_x), row + 180 * side_x, row * TD + 5 * (1 - side_z), row * TD + 5 * side_z, low_y, low_y + 30]
    tile = jnp.where(jnp.concatenate([row] * 6, axis=0) < TD * TD, jnp.concatenate(ids, axis=0), -1)
    hot = (iota((6 * FACE, GRID_ROWS), 1) == tile).astype(jnp.bfloat16)
    faces = jnp.dot(hot, grid_ref[...], preferred_element_type=jnp.float32).astype(jnp.bfloat16)
    for at, ref in enumerate((near_x_ref, far_x_ref, near_z_ref, far_z_ref)):
        ref[...] = faces[at * FACE : (at + 1) * FACE]
    me, count = lax.axis_index("gy"), lax.axis_size("gy")
    for step in range(count):
        high = step == 1
        y_ref[lax.rem(me + step, count)] = faces[(5 if high else 4) * FACE : (6 if high else 5) * FACE]


def coarse_kernel(column_ref, top_ref, face_ref, own_ref, send_ref):
    lines = column_ref.shape[0]
    column = column_ref[...].reshape(lines, LANES)
    column = jnp.concatenate([column] * (lines * 8 // LANES), axis=1)
    shape = column.shape
    column = jnp.sum(jnp.where((iota(shape, 1) >> 3) == iota(shape, 0), column, 0.0), axis=0, keepdims=True)
    partial_value = jnp.sum(top_ref[...] * column, axis=1, keepdims=True)
    rows = partial_value.shape[0]
    lanes = jnp.where((iota((rows, LANES), 1) & 7) == (iota((rows, LANES), 0) & 7), partial_value, 0.0)
    lanes = jnp.sum(lanes.reshape(rows // 8, 8, LANES), axis=1)
    mine = iota((8, LANES), 1) >> 3 == iota((8, LANES), 0)
    lower, upper = (jnp.sum(jnp.where(mine, lanes[at : at + 8], 0.0), axis=0, keepdims=True) for at in (0, 8))
    half = jnp.broadcast_to(lax.axis_index("hx"), (1, LANES)) == 0
    own_ref[...] = jnp.where(half, lower, upper)
    rest = jnp.where(half, upper, lower)
    parts = []
    for _ in range(3):
        parts.append(rest.astype(jnp.bfloat16).astype(jnp.float32))
        rest = rest - parts[-1]
    sums = jnp.concatenate(parts + [jnp.zeros((1, LANES), jnp.float32)], axis=1)
    rows = face_ref[...].astype(jnp.float32)[:FAR_ROWS]
    send_ref[...] = jnp.where(iota((FAR_ROWS, TP), 0) == TD * TD, sums, rows).astype(jnp.bfloat16)


def gate_kernel(face_ref, *rest):
    rest[-1][...] = face_ref[...]


def merge_kernel(own_ref, far_ref, field_any, out_ref):
    sums = far_ref[...].astype(jnp.float32)[TD * TD : TD * TD + 1]
    total = own_ref[...] + ((sums[:, :LANES] + sums[:, LANES : 2 * LANES]) + sums[:, 2 * LANES : 3 * LANES])
    for brick in range(8):
        out_ref[brick] = pltpu.roll(total, (LANES - 8 * brick) % LANES, 1) if brick else total


ATOM_ROWS = 16


def gradients(field_ref, wx, wy, wz, x, y, z):
    sums = [None] * 4
    for i in reversed(range(TL)):
        a = b = c = None
        for j in reversed(range(TL)):
            run = mean = None
            for k in reversed(range(TL)):
                term = wz[k] * field_ref[(i * TL + j) * TL + k : (i * TL + j) * TL + k + 1, :]
                run = term if run is None else run + term
                if k:
                    mean = run if mean is None else mean + run
            part = wy[j] * run
            cross = wy[j] * mean
            a = part if a is None else a + part
            c = cross if c is None else c + cross
            if j:
                b = a if b is None else b + a
        for at, value in enumerate((a, b, c)):
            term = wx[i] * value
            sums[at] = term if sums[at] is None else sums[at] + term
        if i:
            sums[3] = sums[0] if sums[3] is None else sums[3] + sums[0]
    total, with_y, with_z, with_x = sums
    return with_x - x * total, with_y - y * total, with_z - z * total


def tile_column(tiles_ref):
    return jnp.broadcast_to(tiles_ref[:1], (LANES, LANES)).T[:, :1].astype(jnp.int32)


def near_kernel(
    tiles_ref, grid_ref, near_x_ref, near_z_ref, far_z_ref, blocks_ref, coord_ref, weights_ref,
    field_ref, unit_ref,
    ext_ref, flat_ref, grad_ref,
):
    ext_ref[0:GRID_ROWS] = grid_ref[...]
    for at, ref in enumerate((near_x_ref, near_z_ref, far_z_ref)):
        ext_ref[GRID_ROWS + at * FACE : GRID_ROWS + (at + 1) * FACE] = ref[...]
    nothing = GRID_ROWS + 3 * FACE
    ext_ref[nothing:] = jnp.zeros((EXT_ROWS - nothing, TP), jnp.bfloat16)

    tile = tile_column(tiles_ref)
    tx, ty, tz = tile_coords(tile)
    row_x, row_z = ty * TD + tz, tx * TD + ty
    base = GRID_ROWS
    edges = (
        ("gx", tx, 36, base + row_x, nothing + 0 * row_x),
        ("gy", ty, TD, nothing + 0 * row_x, nothing + 0 * row_x),
        ("gz", tz, 1, base + FACE + row_z, base + 2 * FACE + row_z),
    )
    targets = [tile]
    for axis, place, stride, near, far in edges:
        side = jnp.broadcast_to(odd(axis), near.shape) == 1
        targets.append(jnp.where(place < TD - 1, tile + stride, jnp.where(side, far, near)))
        targets.append(jnp.where(place > 0, tile - stride, jnp.where(side, near, far)))
    at_row = iota((LANES, EXT_ROWS), 1)
    field = None
    for at, target in enumerate(targets):
        hot = (at_row == target).astype(jnp.bfloat16)
        rows = jnp.dot(hot, ext_ref[...], preferred_element_type=jnp.float32).astype(jnp.bfloat16)
        flipped = at > 0 and at % 2 == 0
        term = lax.dot_general(
            rows, blocks_ref[(at + 1) // 2], (((1,), (0 if flipped else 1,)), ((), ())), preferred_element_type=jnp.float32
        )
        field = term if field is None else field + term
    field_ref[...] = field
    for part in range(TP // LANES):
        flat_ref[part * LANES : (part + 1) * LANES, :] = jnp.broadcast_to(
            weights_ref[:, part * LANES : (part + 1) * LANES], (LANES, LANES)
        ).T
    all_gradients(flat_ref, coord_ref, grad_ref)
    unit_ref[0], unit_ref[1] = to_atoms(grad_ref[0], grad_ref[1])
    unit_ref[2], _ = to_atoms(grad_ref[2], grad_ref[2])


def all_gradients(field_ref, coord_ref, grad_ref):
    @pl.loop(0, CS // ATOM_ROWS)
    def _(group):
        rows = pl.ds(pl.multiple_of(group * ATOM_ROWS, ATOM_ROWS), ATOM_ROWS)
        x, y, z = coord_ref[0, rows, :], coord_ref[1, rows, :], coord_ref[2, rows, :]
        wx, wy, wz = ([bump(u - node) for node in range(TL)] for u in (x, y, z))
        for axis, value in enumerate(gradients(field_ref, wx, wy, wz, x, y, z)):
            grad_ref[axis, rows, :] = value


def far_kernel(
    tiles_ref, part_ref, far_x_ref, y_ref, block_ref, coord_ref,
    near_ref,
    sum_ref, field_ref, grad_ref,
):
    tx, ty, tz = tile_coords(tile_column(tiles_ref))

    def picked(face, target):
        hot = (iota((LANES, FACE), 1) == target).astype(jnp.bfloat16)
        return jnp.dot(hot, face, preferred_element_type=jnp.float32).astype(jnp.bfloat16)

    def term(rows, block, up):
        return lax.dot_general(rows, block_ref[block], (((1,), (up,)), ((), ())), preferred_element_type=jnp.float32)

    me, count = lax.axis_index("gy"), lax.axis_size("gy")
    row = tx * TD + tz
    above = picked(y_ref[lax.rem(me + 1, count)], jnp.where(ty == TD - 1, row, -1))
    below = picked(y_ref[lax.rem(me + count - 1, count)], jnp.where(ty == 0, row, -1))
    field = part_ref[...] + term(above, 2, 1) + term(below, 2, 0)
    core = odd("gx")
    rest = jnp.zeros((FACE - FAR_ROWS, TP), jnp.float32)
    face = jnp.concatenate([far_x_ref[...].astype(jnp.float32), rest], axis=0).astype(jnp.bfloat16)
    rows = picked(face, jnp.where(tx == (TD - 1) * core, ty * TD + tz, -1))
    for side in range(2):

        @pl.when(core == side)
        def _(side=side):
            sum_ref[...] = field + term(rows, 1, side)

    for part in range(TP // LANES):
        field_ref[part * LANES : (part + 1) * LANES, :] = sum_ref[:, part * LANES : (part + 1) * LANES].T
    all_gradients(field_ref, coord_ref, grad_ref)
    near_ref[0], near_ref[1] = to_atoms(grad_ref[0], grad_ref[1])
    near_ref[2], _ = to_atoms(grad_ref[2], grad_ref[2])


def final_kernel(parts_ref, corner_ref, near_ref, unit_ref, frac_ref, drive_ref, force_ref, virial_ref):
    coarse = jnp.sum(parts_ref[...].reshape(parts_ref.shape[0], LANES), axis=0, keepdims=True)
    corner = corner_ref[...]
    pot = jnp.zeros((HALF, LANES), jnp.float32)
    for at in range(8):
        pot = jnp.where(corner == at, coarse[:, at : at + 1], pot)
    drive = drive_ref[...]
    forces = [drive * (near_ref[axis] + pot * unit_ref[axis]) for axis in range(3)]
    for axis in range(3):
        force_ref[axis] = forces[axis]
        virial_ref[axis] = frac_ref[axis] * forces[axis]
    virial_ref[3] = frac_ref[0] * forces[1]
    virial_ref[4] = frac_ref[0] * forces[2]
    virial_ref[5] = frac_ref[1] * forces[2]


VMEM = pl.BlockSpec(memory_space=pltpu.VMEM)
SMEM = pl.BlockSpec(memory_space=pltpu.SMEM)
ANY = pl.BlockSpec(memory_space=pl.ANY)


def f32(*shape):
    return jax.ShapeDtypeStruct(shape, jnp.float32)


def bf16(*shape):
    return jax.ShapeDtypeStruct(shape, jnp.bfloat16)


def exchanged(value, axis, far):
    count = lax.axis_size(axis)
    return lax.ppermute(value, axis, [(i, (i + (1 if (i + far) % 2 == 0 else -1)) % count) for i in range(count)])


def shards(positions, charges, cluster_tile, live_clusters, kernel_blocks, restrict_weights, top_kernel):
    pos = positions.reshape(3, HALF, LANES)
    charge = charges.reshape(HALF, LANES)
    tile = cluster_tile.reshape(1, LANES)
    live = live_clusters.reshape(1, 1)
    weights = restrict_weights.reshape(1, TP)
    lines = lax.axis_size("gz")

    grid, coarse, coords, tiles, drive, frac, corner, weights, blocks, top = pl.pallas_call(
        spread_kernel,
        out_shape=(
            bf16(GRID_ROWS, TP), f32(lines, 1, LANES), f32(3, CS, LANES), f32(8, LANES), f32(HALF, LANES),
            f32(3, HALF, LANES), jax.ShapeDtypeStruct((HALF, LANES), jnp.int32), f32(1, TP),
            bf16(*kernel_blocks.shape), f32(*top_kernel.shape),
        ),
        in_specs=[SMEM] + [ANY] * 6,
        out_specs=[VMEM] * 10,
        scratch_shapes=[
            pltpu.VMEM((3, HALF, LANES), jnp.float32), pltpu.VMEM((HALF, LANES), jnp.float32),
            pltpu.VMEM((1, LANES), jnp.int32),
            pltpu.VMEM((TL, CS, LANES), jnp.float32), pltpu.VMEM((TL, CS, LANES), jnp.float32),
            pltpu.VMEM((CS, TL, LANES), jnp.float32), pltpu.VMEM((TP, LANES), jnp.float32),
            pltpu.SemaphoreType.DMA((6,)),
        ],
        compiler_params=pltpu.CompilerParams(vmem_limit_bytes=12 << 20),
        cost_estimate=pl.CostEstimate(flops=10_000_000, bytes_accessed=1_000_000, transcendentals=200_000),
        name="spread",
    )(live, *(pltpu.with_memory_space_constraint(a, pltpu.HBM) for a in (pos, charge, tile, weights, kernel_blocks, top_kernel)))
    column = lax.all_to_all(coarse, "gz", 0, 0, tiled=True)

    faces = pl.pallas_call(
        face_kernel,
        out_shape=(bf16(FACE, TP),) * 4 + (bf16(lax.axis_size("gy"), FACE, TP),),
        in_specs=[VMEM],
        out_specs=[VMEM] * 5,
        compiler_params=pltpu.CompilerParams(vmem_limit_bytes=8 << 20),
        cost_estimate=pl.CostEstimate(flops=80_000_000, bytes_accessed=600_000, transcendentals=0),
        name="faces",
    )(grid)
    near_x, far_x, near_z, far_z, face_y = faces
    far_z, near_z = exchanged(far_z, "gz", 1), exchanged(near_z, "gz", 0)
    near_x = exchanged(near_x, ("hx", "cx"), 0)

    own, far_x = pl.pallas_call(
        coarse_kernel,
        out_shape=(f32(1, LANES), bf16(FAR_ROWS, TP)),
        in_specs=[VMEM] * 3,
        out_specs=[VMEM] * 2,
        compiler_params=pltpu.CompilerParams(vmem_limit_bytes=8 << 20),
        cost_estimate=pl.CostEstimate(flops=70_000, bytes_accessed=200_000, transcendentals=0),
        name="coarse",
    )(column, top, far_x)
    far_x = exchanged(far_x, ("hx", "cx"), 1)
    face_y = pl.pallas_call(
        gate_kernel,
        out_shape=bf16(*face_y.shape),
        in_specs=[VMEM] + [ANY] * 3,
        out_specs=VMEM,
        compiler_params=pltpu.CompilerParams(vmem_limit_bytes=4 << 20),
        cost_estimate=pl.CostEstimate(flops=1000, bytes_accessed=1000, transcendentals=0),
        name="gate",
    )(face_y, own, near_x, near_z)
    face_y = lax.all_to_all(face_y, "gy", 0, 0, tiled=True)

    field, unit = pl.pallas_call(
        near_kernel,
        out_shape=(f32(LANES, TP), f32(3, HALF, LANES)),
        in_specs=[VMEM] * 8,
        out_specs=[VMEM] * 2,
        scratch_shapes=[
            pltpu.VMEM((EXT_ROWS, TP), jnp.bfloat16), pltpu.VMEM((TP, LANES), jnp.float32),
            pltpu.VMEM((3, CS, LANES), jnp.float32),
        ],
        compiler_params=pltpu.CompilerParams(vmem_limit_bytes=16 << 20),
        cost_estimate=pl.CostEstimate(flops=20_000_000_000, bytes_accessed=1000, transcendentals=0),
        name="near",
    )(tiles, grid, near_x, near_z, far_z, blocks, coords, weights)

    parts = pl.pallas_call(
        merge_kernel,
        out_shape=f32(8, 1, LANES),
        in_specs=[VMEM] * 2 + [ANY],
        out_specs=VMEM,
        compiler_params=pltpu.CompilerParams(vmem_limit_bytes=4 << 20),
        cost_estimate=pl.CostEstimate(flops=10_000, bytes_accessed=60_000, transcendentals=0),
        name="merge",
    )(own, far_x, field)
    parts = lax.all_to_all(parts, ("cx", "gy"), 0, 0, tiled=True)

    near = pl.pallas_call(
        far_kernel,
        out_shape=f32(3, HALF, LANES),
        in_specs=[VMEM] * 6,
        out_specs=VMEM,
        scratch_shapes=[
            pltpu.VMEM((LANES, TP), jnp.float32), pltpu.VMEM((TP, LANES), jnp.float32),
            pltpu.VMEM((3, CS, LANES), jnp.float32),
        ],
        compiler_params=pltpu.CompilerParams(vmem_limit_bytes=16 << 20),
        cost_estimate=pl.CostEstimate(flops=1_000_000_000, bytes_accessed=4_000_000, transcendentals=200_000),
        name="far",
    )(tiles, field, far_x, face_y, blocks, coords)

    forces, virial = pl.pallas_call(
        final_kernel,
        out_shape=(f32(3, HALF, LANES), f32(6, HALF, LANES)),
        in_specs=[VMEM] * 6,
        out_specs=[VMEM] * 2,
        compiler_params=pltpu.CompilerParams(vmem_limit_bytes=8 << 20),
        cost_estimate=pl.CostEstimate(flops=500_000, bytes_accessed=600_000, transcendentals=0),
        name="final",
    )(parts, corner, near, unit, frac, drive)
    return forces.reshape(3, 1, 1, 1, -1), virial.reshape(6, 1, 1, 1, -1)


def solution(mesh):
    wide, high, deep = (mesh.shape[axis] for axis in ("gx", "gy", "gz"))
    split = jax.sharding.Mesh(mesh.devices.reshape(wide // 2, 2, high, deep), ("hx", "cx", "gy", "gz"))
    x = ("hx", "cx")
    placed = (
        P(None, x, "gy", "gz", None),
        P(x, "gy", "gz", None),
        P(x, "gy", "gz", None),
        P(x, "gy", "gz"),
        P(),
        P(),
        P("gz", ("hx", "cx", "gy")),
    )
    return jax.shard_map(
        shards,
        mesh=split,
        in_specs=placed,
        out_specs=(P(None, x, "gy", "gz", None), P(None, x, "gy", "gz", None)),
        check_vma=False,
    )
```

```python
import math

import jax
import jax.numpy as jnp
from jax import lax
from jax.experimental import pallas as pl
from jax.experimental.pallas import tpu as pltpu
from jax.sharding import PartitionSpec as P

TL = 8
TP = 512
CS = 64
TD = 6
CUBES = TD**3
FACE = 48
GRID_ROWS = 256
FAR_ROWS = 40
EXT_ROWS = 512
HALF = CS
LANES = 128


def iota(shape, axis):
    return lax.broadcasted_iota(jnp.int32, shape, axis)


def tile_coords(tile):
    plane = (tile * 10923) >> 16
    tx = (tile * 1821) >> 16
    return tx, plane - tx * TD, tile - plane * TD


def to_clusters(upper, lower):
    both = jnp.concatenate([upper, lower], axis=0).T
    even, odd = both[:HALF], both[HALF:]
    left = iota((HALF, LANES), 1) < HALF
    return (
        jnp.where(left, even, pltpu.roll(odd, HALF, 1)),
        jnp.where(left, pltpu.roll(even, HALF, 1), odd),
    )


def to_atoms(upper, lower):
    left = iota((HALF, LANES), 1) < HALF
    even = jnp.where(left, upper, pltpu.roll(lower, HALF, 1))
    odd = jnp.where(left, pltpu.roll(upper, HALF, 1), lower)
    both = jnp.concatenate([even, odd], axis=0).T
    return both[:HALF], both[HALF:]


def corner_of(places):
    tx, ty, tz = ((place >= TD // 2).astype(jnp.int32) for place in places)
    return (tx * 2 + ty) * 2 + tz


def bump(offset):
    return jnp.exp(-0.5 * offset * offset)


def spread_kernel(
    live_ref, pos_any, charge_any, tile_any, weights_any, blocks_any, top_any,
    grid_ref, coarse_ref, coord_ref, tiles_ref, drive_ref, frac_ref, corner_ref, weights_ref, blocks_ref, top_ref,
    pos_ref, charge_ref, tile_ref, wx_ref, wy_ref, wz_ref, cell_ref, sems,
):
    moves = [
        pltpu.make_async_copy(source, target, sems.at[at])
        for at, (source, target) in enumerate(
            (
                (pos_any, pos_ref), (charge_any, charge_ref), (tile_any, tile_ref),
                (weights_any, weights_ref), (blocks_any, blocks_ref), (top_any, top_ref),
            )
        )
    ]
    for move in moves:
        move.start()
    for move in moves[:3]:
        move.wait()
    cluster = 2 * iota((HALF, LANES), 0) + (iota((HALF, LANES), 1) >> 6)
    charge = charge_ref[...] * (cluster < live_ref[0, 0]).astype(jnp.float32)
    x, y = to_clusters(pos_ref[0], pos_ref[1])
    z, q = to_clusters(pos_ref[2], charge)
    coord_ref[0], coord_ref[1], coord_ref[2] = x, y, z
    for node in range(TL):
        wx_ref[node] = q * bump(x - node)
        wy_ref[node] = bump(y - node)
    nodes = iota((TL, LANES), 0).astype(jnp.float32)
    for atom in range(CS):
        wz_ref[atom] = bump(z[atom : atom + 1] - nodes)

    own = iota((LANES, LANES), 0)
    at = iota((LANES, LANES), 1)
    order = (own == jnp.where(at < HALF, 2 * at, 2 * at - 127)).astype(jnp.bfloat16)
    ids = jnp.broadcast_to(tile_ref[...].astype(jnp.float32), (8, LANES)).astype(jnp.bfloat16)
    tiles = jnp.dot(ids, order, preferred_element_type=jnp.float32)
    tiles_ref[...] = tiles
    tiles = tiles[:1].astype(jnp.int32)

    for half in range(2):

        def step(atom, total, half=half):
            row = pl.ds(atom, 1)
            wz = wz_ref[atom]
            line = [wy_ref[j, row, :] * wz for j in range(TL)]
            new = []
            for i in range(4):
                wx = jnp.broadcast_to(wx_ref[4 * half + i, row, :], (TL, LANES))
                new += [total[8 * i + j] + wx * line[j] for j in range(TL)]
            return tuple(new)

        start = tuple(jnp.zeros((TL, LANES), jnp.float32) for _ in range(32))
        total = lax.fori_loop(0, CS, step, start, unroll=4)
        for slot in range(32):
            cell_ref[pl.ds((32 * half + slot) * TL, TL), :] = total[slot]

    cell = cell_ref[...]
    high = cell.astype(jnp.bfloat16)
    low = (cell - high.astype(jnp.float32)).astype(jnp.bfloat16)
    hot = (iota((GRID_ROWS, LANES), 0) == tiles).astype(jnp.bfloat16)
    fine = lax.dot_general(
        jnp.concatenate([hot, hot], axis=1), jnp.concatenate([high, low], axis=1), (((1,), (1,)), ((), ())),
        preferred_element_type=jnp.float32,
    )
    grid_ref[...] = fine.astype(jnp.bfloat16)

    moves[3].wait()
    moments = jnp.sum(fine * weights_ref[...], axis=1, keepdims=True)
    tx, ty, tz = tile_coords(iota((GRID_ROWS, LANES), 0))
    mine = corner_of((tx, ty, tz)) == (iota((GRID_ROWS, LANES), 1) & 7)
    coarse = jnp.sum(jnp.where(mine, moments, 0.0), axis=0, keepdims=True)
    coarse = coarse * (1.0 / math.sqrt(TP * 27))
    for line in range(coarse_ref.shape[0]):
        coarse_ref[line] = coarse

    own_row = (iota((HALF, LANES), 1) >> 1) == iota((HALF, LANES), 0)
    rows = jnp.where(own_row, tile_ref[...].astype(jnp.float32), 0.0).astype(jnp.bfloat16)
    side = ((iota((LANES, LANES), 0) & 1) == (iota((LANES, LANES), 1) >> 6)).astype(jnp.bfloat16)
    tile = jnp.dot(rows, side, preferred_element_type=jnp.float32).astype(jnp.int32)
    places = tile_coords(tile)
    corner_ref[...] = corner_of(places)
    drive_ref[...] = -charge
    for axis in range(3):
        frac_ref[axis] = (places[axis].astype(jnp.float32) * TL + pos_ref[axis]) * (1.0 / (TL * TD))
    for move in moves[4:]:
        move.wait()


def odd(axis):
    return lax.axis_index("cx" if axis == "gx" else axis) & 1


def face_kernel(grid_ref, near_x_ref, far_x_ref, near_z_ref, far_z_ref, y_any, y_ref, sem):
    row = iota((FACE, GRID_ROWS), 0)
    line = (row * 10923) >> 16
    side_x, side_z = odd("gx"), odd("gz")
    low_y = line * 36 + (row - line * TD)
    ids = [row + 180 * (1 - side_x), row + 180 * side_x, row * TD + 5 * (1 - side_z), row * TD + 5 * side_z, low_y, low_y + 30]
    tile = jnp.where(jnp.concatenate([row] * 6, axis=0) < TD * TD, jnp.concatenate(ids, axis=0), -1)
    hot = (iota((6 * FACE, GRID_ROWS), 1) == tile).astype(jnp.bfloat16)
    faces = jnp.dot(hot, grid_ref[...], preferred_element_type=jnp.float32).astype(jnp.bfloat16)
    me, count = lax.axis_index("gy"), lax.axis_size("gy")
    for step in range(count):
        high = step == 1
        y_ref[lax.rem(me + step, count)] = faces[(5 if high else 4) * FACE : (6 if high else 5) * FACE]
    move = pltpu.make_async_copy(y_ref, y_any, sem)
    move.start()
    for at, ref in enumerate((near_x_ref, far_x_ref, near_z_ref, far_z_ref)):
        ref[...] = faces[at * FACE : (at + 1) * FACE]
    move.wait()


def coarse_kernel(column_ref, top_ref, face_ref, own_ref, send_ref):
    lines = column_ref.shape[0]
    column = column_ref[...].reshape(lines, LANES)
    column = jnp.concatenate([column] * (lines * 8 // LANES), axis=1)
    shape = column.shape
    column = jnp.sum(jnp.where((iota(shape, 1) >> 3) == iota(shape, 0), column, 0.0), axis=0, keepdims=True)
    partial_value = jnp.sum(top_ref[...] * column, axis=1, keepdims=True)
    rows = partial_value.shape[0]
    lanes = jnp.where((iota((rows, LANES), 1) & 7) == (iota((rows, LANES), 0) & 7), partial_value, 0.0)
    lanes = jnp.sum(lanes.reshape(rows // 8, 8, LANES), axis=1)
    mine = iota((8, LANES), 1) >> 3 == iota((8, LANES), 0)
    lower, upper = (jnp.sum(jnp.where(mine, lanes[at : at + 8], 0.0), axis=0, keepdims=True) for at in (0, 8))
    half = jnp.broadcast_to(lax.axis_index("hx"), (1, LANES)) == 0
    own_ref[...] = jnp.where(half, lower, upper)
    rest = jnp.where(half, upper, lower)
    parts = []
    for _ in range(3):
        parts.append(rest.astype(jnp.bfloat16).astype(jnp.float32))
        rest = rest - parts[-1]
    sums = jnp.concatenate(parts + [jnp.zeros((1, LANES), jnp.float32)], axis=1)
    rows = face_ref[...].astype(jnp.float32)[:FAR_ROWS]
    send_ref[...] = jnp.where(iota((FAR_ROWS, TP), 0) == TD * TD, sums, rows).astype(jnp.bfloat16)


def gate_kernel(*refs):
    pass


def merge_kernel(own_ref, far_ref, field_any, out_ref):
    sums = far_ref[...].astype(jnp.float32)[TD * TD : TD * TD + 1]
    total = own_ref[...] + ((sums[:, :LANES] + sums[:, LANES : 2 * LANES]) + sums[:, 2 * LANES : 3 * LANES])
    for brick in range(8):
        out_ref[brick] = pltpu.roll(total, (LANES - 8 * brick) % LANES, 1) if brick else total


ATOM_ROWS = 16


def gradients(field_ref, wx, wy, wz, x, y, z):
    sums = [None] * 4
    for i in reversed(range(TL)):
        a = b = c = None
        for j in reversed(range(TL)):
            run = mean = None
            for k in reversed(range(TL)):
                term = wz[k] * field_ref[(i * TL + j) * TL + k : (i * TL + j) * TL + k + 1, :]
                run = term if run is None else run + term
                if k:
                    mean = run if mean is None else mean + run
            part = wy[j] * run
            cross = wy[j] * mean
            a = part if a is None else a + part
            c = cross if c is None else c + cross
            if j:
                b = a if b is None else b + a
        for at, value in enumerate((a, b, c)):
            term = wx[i] * value
            sums[at] = term if sums[at] is None else sums[at] + term
        if i:
            sums[3] = sums[0] if sums[3] is None else sums[3] + sums[0]
    total, with_y, with_z, with_x = sums
    return with_x - x * total, with_y - y * total, with_z - z * total


def tile_column(tiles_ref):
    return jnp.broadcast_to(tiles_ref[:1], (LANES, LANES)).T[:, :1].astype(jnp.int32)


def near_kernel(
    tiles_ref, grid_ref, near_x_ref, near_z_ref, far_z_ref, blocks_ref, coord_ref, weights_ref,
    field_ref, unit_ref,
    ext_ref, flat_ref, grad_ref,
):
    ext_ref[0:GRID_ROWS] = grid_ref[...]
    for at, ref in enumerate((near_x_ref, near_z_ref, far_z_ref)):
        ext_ref[GRID_ROWS + at * FACE : GRID_ROWS + (at + 1) * FACE] = ref[...]
    nothing = GRID_ROWS + 3 * FACE
    ext_ref[nothing:] = jnp.zeros((EXT_ROWS - nothing, TP), jnp.bfloat16)

    tile = tile_column(tiles_ref)
    tx, ty, tz = tile_coords(tile)
    row_x, row_z = ty * TD + tz, tx * TD + ty
    base = GRID_ROWS
    edges = (
        ("gx", tx, 36, base + row_x, nothing + 0 * row_x),
        ("gy", ty, TD, nothing + 0 * row_x, nothing + 0 * row_x),
        ("gz", tz, 1, base + FACE + row_z, base + 2 * FACE + row_z),
    )
    targets = [tile]
    for axis, place, stride, near, far in edges:
        side = jnp.broadcast_to(odd(axis), near.shape) == 1
        targets.append(jnp.where(place < TD - 1, tile + stride, jnp.where(side, far, near)))
        targets.append(jnp.where(place > 0, tile - stride, jnp.where(side, near, far)))
    at_row = iota((LANES, EXT_ROWS), 1)
    field = None
    for at, target in enumerate(targets):
        hot = (at_row == target).astype(jnp.bfloat16)
        rows = jnp.dot(hot, ext_ref[...], preferred_element_type=jnp.float32).astype(jnp.bfloat16)
        flipped = at > 0 and at % 2 == 0
        term = lax.dot_general(
            rows, blocks_ref[(at + 1) // 2], (((1,), (0 if flipped else 1,)), ((), ())), preferred_element_type=jnp.float32
        )
        field = term if field is None else field + term
    field_ref[...] = field
    for part in range(TP // LANES):
        flat_ref[part * LANES : (part + 1) * LANES, :] = jnp.broadcast_to(
            weights_ref[:, part * LANES : (part + 1) * LANES], (LANES, LANES)
        ).T
    all_gradients(flat_ref, coord_ref, grad_ref)
    unit_ref[0], unit_ref[1] = to_atoms(grad_ref[0], grad_ref[1])
    unit_ref[2], _ = to_atoms(grad_ref[2], grad_ref[2])


def all_gradients(field_ref, coord_ref, grad_ref):
    @pl.loop(0, CS // ATOM_ROWS)
    def _(group):
        rows = pl.ds(pl.multiple_of(group * ATOM_ROWS, ATOM_ROWS), ATOM_ROWS)
        x, y, z = coord_ref[0, rows, :], coord_ref[1, rows, :], coord_ref[2, rows, :]
        wx, wy, wz = ([bump(u - node) for node in range(TL)] for u in (x, y, z))
        for axis, value in enumerate(gradients(field_ref, wx, wy, wz, x, y, z)):
            grad_ref[axis, rows, :] = value


def far_kernel(
    tiles_ref, part_ref, far_x_ref, y_ref, block_ref, coord_ref,
    near_ref,
    sum_ref, field_ref, grad_ref,
):
    tx, ty, tz = tile_coords(tile_column(tiles_ref))

    def picked(face, target):
        hot = (iota((LANES, FACE), 1) == target).astype(jnp.bfloat16)
        return jnp.dot(hot, face, preferred_element_type=jnp.float32).astype(jnp.bfloat16)

    def term(rows, block, up):
        return lax.dot_general(rows, block_ref[block], (((1,), (up,)), ((), ())), preferred_element_type=jnp.float32)

    me, count = lax.axis_index("gy"), lax.axis_size("gy")
    row = tx * TD + tz
    above = picked(y_ref[lax.rem(me + 1, count)], jnp.where(ty == TD - 1, row, -1))
    below = picked(y_ref[lax.rem(me + count - 1, count)], jnp.where(ty == 0, row, -1))
    field = part_ref[...] + term(above, 2, 1) + term(below, 2, 0)
    core = odd("gx")
    rest = jnp.zeros((FACE - FAR_ROWS, TP), jnp.float32)
    face = jnp.concatenate([far_x_ref[...].astype(jnp.float32), rest], axis=0).astype(jnp.bfloat16)
    rows = picked(face, jnp.where(tx == (TD - 1) * core, ty * TD + tz, -1))
    for side in range(2):

        @pl.when(core == side)
        def _(side=side):
            sum_ref[...] = field + term(rows, 1, side)

    for part in range(TP // LANES):
        field_ref[part * LANES : (part + 1) * LANES, :] = sum_ref[:, part * LANES : (part + 1) * LANES].T
    all_gradients(field_ref, coord_ref, grad_ref)
    near_ref[0], near_ref[1] = to_atoms(grad_ref[0], grad_ref[1])
    near_ref[2], _ = to_atoms(grad_ref[2], grad_ref[2])


def final_kernel(parts_ref, corner_ref, near_ref, unit_ref, frac_ref, drive_ref, force_ref, virial_ref):
    coarse = jnp.sum(parts_ref[...].reshape(parts_ref.shape[0], LANES), axis=0, keepdims=True)
    corner = corner_ref[...]
    pot = jnp.zeros((HALF, LANES), jnp.float32)
    for at in range(8):
        pot = jnp.where(corner == at, coarse[:, at : at + 1], pot)
    drive = drive_ref[...]
    forces = [drive * (near_ref[axis] + pot * unit_ref[axis]) for axis in range(3)]
    for axis in range(3):
        force_ref[axis] = forces[axis]
        virial_ref[axis] = frac_ref[axis] * forces[axis]
    virial_ref[3] = frac_ref[0] * forces[1]
    virial_ref[4] = frac_ref[0] * forces[2]
    virial_ref[5] = frac_ref[1] * forces[2]


VMEM = pl.BlockSpec(memory_space=pltpu.VMEM)
SMEM = pl.BlockSpec(memory_space=pltpu.SMEM)
ANY = pl.BlockSpec(memory_space=pl.ANY)
HBM = pl.BlockSpec(memory_space=pltpu.HBM)


def f32(*shape):
    return jax.ShapeDtypeStruct(shape, jnp.float32)


def bf16(*shape):
    return jax.ShapeDtypeStruct(shape, jnp.bfloat16)


def exchanged(value, axis, far):
    count = lax.axis_size(axis)
    return lax.ppermute(value, axis, [(i, (i + (1 if (i + far) % 2 == 0 else -1)) % count) for i in range(count)])


def shards(positions, charges, cluster_tile, live_clusters, kernel_blocks, restrict_weights, top_kernel):
    pos = positions.reshape(3, HALF, LANES)
    charge = charges.reshape(HALF, LANES)
    tile = cluster_tile.reshape(1, LANES)
    live = live_clusters.reshape(1, 1)
    weights = restrict_weights.reshape(1, TP)
    lines = lax.axis_size("gz")

    grid, coarse, coords, tiles, drive, frac, corner, weights, blocks, top = pl.pallas_call(
        spread_kernel,
        out_shape=(
            bf16(GRID_ROWS, TP), f32(lines, 1, LANES), f32(3, CS, LANES), f32(8, LANES), f32(HALF, LANES),
            f32(3, HALF, LANES), jax.ShapeDtypeStruct((HALF, LANES), jnp.int32), f32(1, TP),
            bf16(*kernel_blocks.shape), f32(*top_kernel.shape),
        ),
        in_specs=[SMEM] + [ANY] * 6,
        out_specs=[VMEM] * 10,
        scratch_shapes=[
            pltpu.VMEM((3, HALF, LANES), jnp.float32), pltpu.VMEM((HALF, LANES), jnp.float32),
            pltpu.VMEM((1, LANES), jnp.int32),
            pltpu.VMEM((TL, CS, LANES), jnp.float32), pltpu.VMEM((TL, CS, LANES), jnp.float32),
            pltpu.VMEM((CS, TL, LANES), jnp.float32), pltpu.VMEM((TP, LANES), jnp.float32),
            pltpu.SemaphoreType.DMA((6,)),
        ],
        compiler_params=pltpu.CompilerParams(vmem_limit_bytes=12 << 20),
        cost_estimate=pl.CostEstimate(flops=10_000_000, bytes_accessed=1_000_000, transcendentals=200_000),
        name="spread",
    )(live, *(pltpu.with_memory_space_constraint(a, pltpu.HBM) for a in (pos, charge, tile, weights, kernel_blocks, top_kernel)))
    column = lax.all_to_all(coarse, "gz", 0, 0, tiled=True)

    faces = pl.pallas_call(
        face_kernel,
        out_shape=(bf16(FACE, TP),) * 4 + (pltpu.HBM((lax.axis_size("gy"), FACE, TP), jnp.bfloat16),),
        in_specs=[VMEM],
        out_specs=[VMEM] * 4 + [HBM],
        scratch_shapes=[pltpu.VMEM((lax.axis_size("gy"), FACE, TP), jnp.bfloat16), pltpu.SemaphoreType.DMA],
        compiler_params=pltpu.CompilerParams(vmem_limit_bytes=8 << 20),
        cost_estimate=pl.CostEstimate(flops=80_000_000, bytes_accessed=600_000, transcendentals=0),
        name="faces",
    )(grid)
    near_x, far_x, near_z, far_z, face_y = faces
    far_z, near_z = exchanged(far_z, "gz", 1), exchanged(near_z, "gz", 0)
    near_x = exchanged(near_x, ("hx", "cx"), 0)

    own, far_x = pl.pallas_call(
        coarse_kernel,
        out_shape=(f32(1, LANES), bf16(FAR_ROWS, TP)),
        in_specs=[VMEM] * 3,
        out_specs=[VMEM] * 2,
        compiler_params=pltpu.CompilerParams(vmem_limit_bytes=8 << 20),
        cost_estimate=pl.CostEstimate(flops=70_000, bytes_accessed=200_000, transcendentals=0),
        name="coarse",
    )(column, top, far_x)
    far_x = exchanged(far_x, ("hx", "cx"), 1)
    face_y = pl.pallas_call(
        gate_kernel,
        out_shape=pltpu.HBM(face_y.shape, jnp.bfloat16),
        in_specs=[HBM] + [ANY] * 3,
        out_specs=HBM,
        input_output_aliases={0: 0},
        compiler_params=pltpu.CompilerParams(vmem_limit_bytes=4 << 20),
        cost_estimate=pl.CostEstimate(flops=1000, bytes_accessed=1000, transcendentals=0),
        name="gate",
    )(face_y, own, near_x, near_z)
    face_y = lax.all_to_all(face_y, "gy", 0, 0, tiled=True)

    field, unit = pl.pallas_call(
        near_kernel,
        out_shape=(f32(LANES, TP), f32(3, HALF, LANES)),
        in_specs=[VMEM] * 8,
        out_specs=[VMEM] * 2,
        scratch_shapes=[
            pltpu.VMEM((EXT_ROWS, TP), jnp.bfloat16), pltpu.VMEM((TP, LANES), jnp.float32),
            pltpu.VMEM((3, CS, LANES), jnp.float32),
        ],
        compiler_params=pltpu.CompilerParams(vmem_limit_bytes=16 << 20),
        cost_estimate=pl.CostEstimate(flops=20_000_000_000, bytes_accessed=1000, transcendentals=0),
        name="near",
    )(tiles, grid, near_x, near_z, far_z, blocks, coords, weights)

    parts = pl.pallas_call(
        merge_kernel,
        out_shape=f32(8, 1, LANES),
        in_specs=[VMEM] * 2 + [ANY],
        out_specs=VMEM,
        compiler_params=pltpu.CompilerParams(vmem_limit_bytes=4 << 20),
        cost_estimate=pl.CostEstimate(flops=10_000, bytes_accessed=60_000, transcendentals=0),
        name="merge",
    )(own, far_x, field)
    parts = lax.all_to_all(parts, ("cx", "gy"), 0, 0, tiled=True)

    near = pl.pallas_call(
        far_kernel,
        out_shape=f32(3, HALF, LANES),
        in_specs=[VMEM] * 6,
        out_specs=VMEM,
        scratch_shapes=[
            pltpu.VMEM((LANES, TP), jnp.float32), pltpu.VMEM((TP, LANES), jnp.float32),
            pltpu.VMEM((3, CS, LANES), jnp.float32),
        ],
        compiler_params=pltpu.CompilerParams(vmem_limit_bytes=16 << 20),
        cost_estimate=pl.CostEstimate(flops=1_000_000_000, bytes_accessed=4_000_000, transcendentals=200_000),
        name="far",
    )(tiles, field, far_x, face_y, blocks, coords)

    forces, virial = pl.pallas_call(
        final_kernel,
        out_shape=(f32(3, HALF, LANES), f32(6, HALF, LANES)),
        in_specs=[VMEM] * 6,
        out_specs=[VMEM] * 2,
        compiler_params=pltpu.CompilerParams(vmem_limit_bytes=8 << 20),
        cost_estimate=pl.CostEstimate(flops=500_000, bytes_accessed=600_000, transcendentals=0),
        name="final",
    )(parts, corner, near, unit, frac, drive)
    return forces.reshape(3, 1, 1, 1, -1), virial.reshape(6, 1, 1, 1, -1)


def solution(mesh):
    wide, high, deep = (mesh.shape[axis] for axis in ("gx", "gy", "gz"))
    split = jax.sharding.Mesh(mesh.devices.reshape(wide // 2, 2, high, deep), ("hx", "cx", "gy", "gz"))
    x = ("hx", "cx")
    placed = (
        P(None, x, "gy", "gz", None),
        P(x, "gy", "gz", None),
        P(x, "gy", "gz", None),
        P(x, "gy", "gz"),
        P(),
        P(),
        P("gz", ("hx", "cx", "gy")),
    )
    return jax.shard_map(
        shards,
        mesh=split,
        in_specs=placed,
        out_specs=(P(None, x, "gy", "gz", None), P(None, x, "gy", "gz", None)),
        check_vma=False,
    )
```

```python
import math

import jax
import jax.numpy as jnp
from jax import lax
from jax.experimental import pallas as pl
from jax.experimental.pallas import tpu as pltpu
from jax.sharding import PartitionSpec as P

TL = 8
TP = 512
CS = 64
TD = 6
CUBES = TD**3
FACE = 48
GRID_ROWS = 256
FAR_ROWS = 40
EXT_ROWS = 512
HALF = CS
LANES = 128


def iota(shape, axis):
    return lax.broadcasted_iota(jnp.int32, shape, axis)


def tile_coords(tile):
    plane = (tile * 10923) >> 16
    tx = (tile * 1821) >> 16
    return tx, plane - tx * TD, tile - plane * TD


def to_clusters(upper, lower):
    both = jnp.concatenate([upper, lower], axis=0).T
    even, odd = both[:HALF], both[HALF:]
    left = iota((HALF, LANES), 1) < HALF
    return (
        jnp.where(left, even, pltpu.roll(odd, HALF, 1)),
        jnp.where(left, pltpu.roll(even, HALF, 1), odd),
    )


def to_atoms(upper, lower):
    left = iota((HALF, LANES), 1) < HALF
    even = jnp.where(left, upper, pltpu.roll(lower, HALF, 1))
    odd = jnp.where(left, pltpu.roll(upper, HALF, 1), lower)
    both = jnp.concatenate([even, odd], axis=0).T
    return both[:HALF], both[HALF:]


def corner_of(places):
    tx, ty, tz = ((place >= TD // 2).astype(jnp.int32) for place in places)
    return (tx * 2 + ty) * 2 + tz


def bump(offset):
    return jnp.exp(-0.5 * offset * offset)


def spread_kernel(
    live_ref, pos_any, charge_any, tile_any, weights_any, blocks_any, top_any,
    grid_ref, coarse_ref, coord_ref, tiles_ref, drive_ref, frac_ref, corner_ref, weights_ref, blocks_ref, top_ref,
    pos_ref, charge_ref, tile_ref, wx_ref, wy_ref, wz_ref, cell_ref, sems,
):
    moves = [
        pltpu.make_async_copy(source, target, sems.at[at])
        for at, (source, target) in enumerate(
            (
                (pos_any, pos_ref), (charge_any, charge_ref), (tile_any, tile_ref),
                (weights_any, weights_ref), (blocks_any, blocks_ref), (top_any, top_ref),
            )
        )
    ]
    for move in moves:
        move.start()
    for move in moves[:3]:
        move.wait()
    cluster = 2 * iota((HALF, LANES), 0) + (iota((HALF, LANES), 1) >> 6)
    charge = charge_ref[...] * (cluster < live_ref[0, 0]).astype(jnp.float32)
    x, y = to_clusters(pos_ref[0], pos_ref[1])
    z, q = to_clusters(pos_ref[2], charge)
    coord_ref[0], coord_ref[1], coord_ref[2] = x, y, z
    for node in range(TL):
        wx_ref[node] = q * bump(x - node)
        wy_ref[node] = bump(y - node)
    nodes = iota((TL, LANES), 0).astype(jnp.float32)
    for atom in range(CS):
        wz_ref[atom] = bump(z[atom : atom + 1] - nodes)

    own = iota((LANES, LANES), 0)
    at = iota((LANES, LANES), 1)
    order = (own == jnp.where(at < HALF, 2 * at, 2 * at - 127)).astype(jnp.bfloat16)
    ids = jnp.broadcast_to(tile_ref[...].astype(jnp.float32), (8, LANES)).astype(jnp.bfloat16)
    tiles = jnp.dot(ids, order, preferred_element_type=jnp.float32)
    tiles_ref[...] = tiles
    tiles = tiles[:1].astype(jnp.int32)

    for half in range(2):

        def step(atom, total, half=half):
            row = pl.ds(atom, 1)
            wz = wz_ref[atom]
            line = [wy_ref[j, row, :] * wz for j in range(TL)]
            new = []
            for i in range(4):
                wx = jnp.broadcast_to(wx_ref[4 * half + i, row, :], (TL, LANES))
                new += [total[8 * i + j] + wx * line[j] for j in range(TL)]
            return tuple(new)

        start = tuple(jnp.zeros((TL, LANES), jnp.float32) for _ in range(32))
        total = lax.fori_loop(0, CS, step, start, unroll=4)
        for slot in range(32):
            cell_ref[pl.ds((32 * half + slot) * TL, TL), :] = total[slot]

    cell = cell_ref[...]
    high = cell.astype(jnp.bfloat16)
    low = (cell - high.astype(jnp.float32)).astype(jnp.bfloat16)
    hot = (iota((GRID_ROWS, LANES), 0) == tiles).astype(jnp.bfloat16)
    fine = lax.dot_general(
        jnp.concatenate([hot, hot], axis=1), jnp.concatenate([high, low], axis=1), (((1,), (1,)), ((), ())),
        preferred_element_type=jnp.float32,
    )
    grid_ref[...] = fine.astype(jnp.bfloat16)

    moves[3].wait()
    moments = jnp.sum(fine * weights_ref[...], axis=1, keepdims=True)
    tx, ty, tz = tile_coords(iota((GRID_ROWS, LANES), 0))
    mine = corner_of((tx, ty, tz)) == (iota((GRID_ROWS, LANES), 1) & 7)
    coarse = jnp.sum(jnp.where(mine, moments, 0.0), axis=0, keepdims=True)
    coarse = coarse * (1.0 / math.sqrt(TP * 27))
    for line in range(coarse_ref.shape[0]):
        coarse_ref[line] = coarse

    own_row = (iota((HALF, LANES), 1) >> 1) == iota((HALF, LANES), 0)
    rows = jnp.where(own_row, tile_ref[...].astype(jnp.float32), 0.0).astype(jnp.bfloat16)
    side = ((iota((LANES, LANES), 0) & 1) == (iota((LANES, LANES), 1) >> 6)).astype(jnp.bfloat16)
    tile = jnp.dot(rows, side, preferred_element_type=jnp.float32).astype(jnp.int32)
    places = tile_coords(tile)
    corner_ref[...] = corner_of(places)
    drive_ref[...] = -charge
    for axis in range(3):
        frac_ref[axis] = (places[axis].astype(jnp.float32) * TL + pos_ref[axis]) * (1.0 / (TL * TD))
    for move in moves[4:]:
        move.wait()


def odd(axis):
    return lax.axis_index("cx" if axis == "gx" else axis) & 1


def face_kernel(grid_ref, near_x_ref, far_x_ref, near_z_ref, far_z_ref, y_any, y_ref, sem):
    row = iota((FACE, GRID_ROWS), 0)
    line = (row * 10923) >> 16
    side_x, side_z = odd("gx"), odd("gz")
    low_y = line * 36 + (row - line * TD)
    def made(ids):
        count = len(ids)
        tile = jnp.where(jnp.concatenate([row] * count, axis=0) < TD * TD, jnp.concatenate(ids, axis=0), -1)
        hot = (iota((count * FACE, GRID_ROWS), 1) == tile).astype(jnp.bfloat16)
        faces = jnp.dot(hot, grid_ref[...], preferred_element_type=jnp.float32).astype(jnp.bfloat16)
        return [faces[at * FACE : (at + 1) * FACE] for at in range(count)]

    low, high = made([low_y, low_y + 30])
    me, count = lax.axis_index("gy"), lax.axis_size("gy")
    for step in range(count):
        y_ref[lax.rem(me + step, count)] = high if step == 1 else low
    move = pltpu.make_async_copy(y_ref, y_any, sem)
    move.start()
    ids = [row + 180 * (1 - side_x), row + 180 * side_x, row * TD + 5 * (1 - side_z), row * TD + 5 * side_z]
    for ref, face in zip((near_x_ref, far_x_ref, near_z_ref, far_z_ref), made(ids), strict=True):
        ref[...] = face
    move.wait()


def coarse_kernel(column_ref, top_ref, face_ref, own_ref, send_ref):
    lines = column_ref.shape[0]
    column = column_ref[...].reshape(lines, LANES)
    column = jnp.concatenate([column] * (lines * 8 // LANES), axis=1)
    shape = column.shape
    column = jnp.sum(jnp.where((iota(shape, 1) >> 3) == iota(shape, 0), column, 0.0), axis=0, keepdims=True)
    partial_value = jnp.sum(top_ref[...] * column, axis=1, keepdims=True)
    rows = partial_value.shape[0]
    lanes = jnp.where((iota((rows, LANES), 1) & 7) == (iota((rows, LANES), 0) & 7), partial_value, 0.0)
    lanes = jnp.sum(lanes.reshape(rows // 8, 8, LANES), axis=1)
    mine = iota((8, LANES), 1) >> 3 == iota((8, LANES), 0)
    lower, upper = (jnp.sum(jnp.where(mine, lanes[at : at + 8], 0.0), axis=0, keepdims=True) for at in (0, 8))
    half = jnp.broadcast_to(lax.axis_index("hx"), (1, LANES)) == 0
    own_ref[...] = jnp.where(half, lower, upper)
    rest = jnp.where(half, upper, lower)
    parts = []
    for _ in range(3):
        parts.append(rest.astype(jnp.bfloat16).astype(jnp.float32))
        rest = rest - parts[-1]
    sums = jnp.concatenate(parts + [jnp.zeros((1, LANES), jnp.float32)], axis=1)
    rows = face_ref[...].astype(jnp.float32)[:FAR_ROWS]
    send_ref[...] = jnp.where(iota((FAR_ROWS, TP), 0) == TD * TD, sums, rows).astype(jnp.bfloat16)


def gate_kernel(*refs):
    pass


def merge_kernel(own_ref, far_ref, field_any, out_ref):
    sums = far_ref[...].astype(jnp.float32)[TD * TD : TD * TD + 1]
    total = own_ref[...] + ((sums[:, :LANES] + sums[:, LANES : 2 * LANES]) + sums[:, 2 * LANES : 3 * LANES])
    for brick in range(8):
        out_ref[brick] = pltpu.roll(total, (LANES - 8 * brick) % LANES, 1) if brick else total


ATOM_ROWS = 16


def gradients(field_ref, wx, wy, wz, x, y, z):
    sums = [None] * 4
    for i in reversed(range(TL)):
        a = b = c = None
        for j in reversed(range(TL)):
            run = mean = None
            for k in reversed(range(TL)):
                term = wz[k] * field_ref[(i * TL + j) * TL + k : (i * TL + j) * TL + k + 1, :]
                run = term if run is None else run + term
                if k:
                    mean = run if mean is None else mean + run
            part = wy[j] * run
            cross = wy[j] * mean
            a = part if a is None else a + part
            c = cross if c is None else c + cross
            if j:
                b = a if b is None else b + a
        for at, value in enumerate((a, b, c)):
            term = wx[i] * value
            sums[at] = term if sums[at] is None else sums[at] + term
        if i:
            sums[3] = sums[0] if sums[3] is None else sums[3] + sums[0]
    total, with_y, with_z, with_x = sums
    return with_x - x * total, with_y - y * total, with_z - z * total


def tile_column(tiles_ref):
    return jnp.broadcast_to(tiles_ref[:1], (LANES, LANES)).T[:, :1].astype(jnp.int32)


def near_kernel(
    tiles_ref, grid_ref, near_x_ref, near_z_ref, far_z_ref, blocks_ref, coord_ref, weights_ref,
    field_ref, unit_ref,
    ext_ref, flat_ref, grad_ref,
):
    ext_ref[0:GRID_ROWS] = grid_ref[...]
    for at, ref in enumerate((near_x_ref, near_z_ref, far_z_ref)):
        ext_ref[GRID_ROWS + at * FACE : GRID_ROWS + (at + 1) * FACE] = ref[...]
    nothing = GRID_ROWS + 3 * FACE
    ext_ref[nothing:] = jnp.zeros((EXT_ROWS - nothing, TP), jnp.bfloat16)

    tile = tile_column(tiles_ref)
    tx, ty, tz = tile_coords(tile)
    row_x, row_z = ty * TD + tz, tx * TD + ty
    base = GRID_ROWS
    edges = (
        ("gx", tx, 36, base + row_x, nothing + 0 * row_x),
        ("gy", ty, TD, CUBES + 0 * row_x, CUBES + 0 * row_x),
        ("gz", tz, 1, base + FACE + row_z, base + 2 * FACE + row_z),
    )
    targets = [tile]
    for axis, place, stride, near, far in edges:
        side = jnp.broadcast_to(odd(axis), near.shape) == 1
        targets.append(jnp.where(place < TD - 1, tile + stride, jnp.where(side, far, near)))
        targets.append(jnp.where(place > 0, tile - stride, jnp.where(side, near, far)))
    field = None
    for at, target in enumerate(targets):
        reach = GRID_ROWS if at in (0, 3, 4) else EXT_ROWS
        hot = (iota((LANES, reach), 1) == target).astype(jnp.bfloat16)
        rows = jnp.dot(hot, ext_ref[:reach], preferred_element_type=jnp.float32).astype(jnp.bfloat16)
        flipped = at > 0 and at % 2 == 0
        term = lax.dot_general(
            rows, blocks_ref[(at + 1) // 2], (((1,), (0 if flipped else 1,)), ((), ())), preferred_element_type=jnp.float32
        )
        field = term if field is None else field + term
    field_ref[...] = field
    for part in range(TP // LANES):
        flat_ref[part * LANES : (part + 1) * LANES, :] = jnp.broadcast_to(
            weights_ref[:, part * LANES : (part + 1) * LANES], (LANES, LANES)
        ).T
    all_gradients(flat_ref, coord_ref, grad_ref)
    unit_ref[0], unit_ref[1] = to_atoms(grad_ref[0], grad_ref[1])
    unit_ref[2], _ = to_atoms(grad_ref[2], grad_ref[2])


def all_gradients(field_ref, coord_ref, grad_ref):
    @pl.loop(0, CS // ATOM_ROWS)
    def _(group):
        rows = pl.ds(pl.multiple_of(group * ATOM_ROWS, ATOM_ROWS), ATOM_ROWS)
        x, y, z = coord_ref[0, rows, :], coord_ref[1, rows, :], coord_ref[2, rows, :]
        wx, wy, wz = ([bump(u - node) for node in range(TL)] for u in (x, y, z))
        for axis, value in enumerate(gradients(field_ref, wx, wy, wz, x, y, z)):
            grad_ref[axis, rows, :] = value


def far_kernel(
    tiles_ref, part_ref, far_x_ref, y_ref, block_ref, coord_ref,
    near_ref,
    sum_ref, field_ref, grad_ref,
):
    tx, ty, tz = tile_coords(tile_column(tiles_ref))

    def picked(face, target):
        hot = (iota((LANES, FACE), 1) == target).astype(jnp.bfloat16)
        return jnp.dot(hot, face, preferred_element_type=jnp.float32).astype(jnp.bfloat16)

    def term(rows, block, up):
        return lax.dot_general(rows, block_ref[block], (((1,), (up,)), ((), ())), preferred_element_type=jnp.float32)

    me, count = lax.axis_index("gy"), lax.axis_size("gy")
    row = tx * TD + tz
    above = picked(y_ref[lax.rem(me + 1, count)], jnp.where(ty == TD - 1, row, -1))
    below = picked(y_ref[lax.rem(me + count - 1, count)], jnp.where(ty == 0, row, -1))
    field = part_ref[...] + term(above, 2, 1) + term(below, 2, 0)
    core = odd("gx")
    rest = jnp.zeros((FACE - FAR_ROWS, TP), jnp.float32)
    face = jnp.concatenate([far_x_ref[...].astype(jnp.float32), rest], axis=0).astype(jnp.bfloat16)
    rows = picked(face, jnp.where(tx == (TD - 1) * core, ty * TD + tz, -1))
    for side in range(2):

        @pl.when(core == side)
        def _(side=side):
            sum_ref[...] = field + term(rows, 1, side)

    for part in range(TP // LANES):
        field_ref[part * LANES : (part + 1) * LANES, :] = sum_ref[:, part * LANES : (part + 1) * LANES].T
    all_gradients(field_ref, coord_ref, grad_ref)
    near_ref[0], near_ref[1] = to_atoms(grad_ref[0], grad_ref[1])
    near_ref[2], _ = to_atoms(grad_ref[2], grad_ref[2])


def final_kernel(parts_ref, corner_ref, near_ref, unit_ref, frac_ref, drive_ref, force_ref, virial_ref):
    coarse = jnp.sum(parts_ref[...].reshape(parts_ref.shape[0], LANES), axis=0, keepdims=True)
    corner = corner_ref[...]
    pot = jnp.zeros((HALF, LANES), jnp.float32)
    for at in range(8):
        pot = jnp.where(corner == at, coarse[:, at : at + 1], pot)
    drive = drive_ref[...]
    forces = [drive * (near_ref[axis] + pot * unit_ref[axis]) for axis in range(3)]
    for axis in range(3):
        force_ref[axis] = forces[axis]
        virial_ref[axis] = frac_ref[axis] * forces[axis]
    virial_ref[3] = frac_ref[0] * forces[1]
    virial_ref[4] = frac_ref[0] * forces[2]
    virial_ref[5] = frac_ref[1] * forces[2]


VMEM = pl.BlockSpec(memory_space=pltpu.VMEM)
SMEM = pl.BlockSpec(memory_space=pltpu.SMEM)
ANY = pl.BlockSpec(memory_space=pl.ANY)
HBM = pl.BlockSpec(memory_space=pltpu.HBM)


def f32(*shape):
    return jax.ShapeDtypeStruct(shape, jnp.float32)


def bf16(*shape):
    return jax.ShapeDtypeStruct(shape, jnp.bfloat16)


def exchanged(value, axis, far):
    count = lax.axis_size(axis)
    return lax.ppermute(value, axis, [(i, (i + (1 if (i + far) % 2 == 0 else -1)) % count) for i in range(count)])


def shards(positions, charges, cluster_tile, live_clusters, kernel_blocks, restrict_weights, top_kernel):
    pos = positions.reshape(3, HALF, LANES)
    charge = charges.reshape(HALF, LANES)
    tile = cluster_tile.reshape(1, LANES)
    live = live_clusters.reshape(1, 1)
    weights = restrict_weights.reshape(1, TP)
    lines = lax.axis_size("gz")

    grid, coarse, coords, tiles, drive, frac, corner, weights, blocks, top = pl.pallas_call(
        spread_kernel,
        out_shape=(
            bf16(GRID_ROWS, TP), f32(lines, 1, LANES), f32(3, CS, LANES), f32(8, LANES), f32(HALF, LANES),
            f32(3, HALF, LANES), jax.ShapeDtypeStruct((HALF, LANES), jnp.int32), f32(1, TP),
            bf16(*kernel_blocks.shape), f32(*top_kernel.shape),
        ),
        in_specs=[SMEM] + [ANY] * 6,
        out_specs=[VMEM] * 10,
        scratch_shapes=[
            pltpu.VMEM((3, HALF, LANES), jnp.float32), pltpu.VMEM((HALF, LANES), jnp.float32),
            pltpu.VMEM((1, LANES), jnp.int32),
            pltpu.VMEM((TL, CS, LANES), jnp.float32), pltpu.VMEM((TL, CS, LANES), jnp.float32),
            pltpu.VMEM((CS, TL, LANES), jnp.float32), pltpu.VMEM((TP, LANES), jnp.float32),
            pltpu.SemaphoreType.DMA((6,)),
        ],
        compiler_params=pltpu.CompilerParams(vmem_limit_bytes=12 << 20),
        cost_estimate=pl.CostEstimate(flops=10_000_000, bytes_accessed=1_000_000, transcendentals=200_000),
        name="spread",
    )(live, *(pltpu.with_memory_space_constraint(a, pltpu.HBM) for a in (pos, charge, tile, weights, kernel_blocks, top_kernel)))
    column = lax.all_to_all(coarse, "gz", 0, 0, tiled=True)

    faces = pl.pallas_call(
        face_kernel,
        out_shape=(bf16(FACE, TP),) * 4 + (pltpu.HBM((lax.axis_size("gy"), FACE, TP), jnp.bfloat16),),
        in_specs=[VMEM],
        out_specs=[VMEM] * 4 + [HBM],
        scratch_shapes=[pltpu.VMEM((lax.axis_size("gy"), FACE, TP), jnp.bfloat16), pltpu.SemaphoreType.DMA],
        compiler_params=pltpu.CompilerParams(vmem_limit_bytes=8 << 20),
        cost_estimate=pl.CostEstimate(flops=80_000_000, bytes_accessed=600_000, transcendentals=0),
        name="faces",
    )(grid)
    near_x, far_x, near_z, far_z, face_y = faces
    far_z, near_z = exchanged(far_z, "gz", 1), exchanged(near_z, "gz", 0)
    near_x = exchanged(near_x, ("hx", "cx"), 0)

    own, far_x = pl.pallas_call(
        coarse_kernel,
        out_shape=(f32(1, LANES), bf16(FAR_ROWS, TP)),
        in_specs=[VMEM] * 3,
        out_specs=[VMEM] * 2,
        compiler_params=pltpu.CompilerParams(vmem_limit_bytes=8 << 20),
        cost_estimate=pl.CostEstimate(flops=70_000, bytes_accessed=200_000, transcendentals=0),
        name="coarse",
    )(column, top, far_x)
    far_x = exchanged(far_x, ("hx", "cx"), 1)
    face_y = pl.pallas_call(
        gate_kernel,
        out_shape=pltpu.HBM(face_y.shape, jnp.bfloat16),
        in_specs=[HBM] + [ANY] * 3,
        out_specs=HBM,
        input_output_aliases={0: 0},
        compiler_params=pltpu.CompilerParams(vmem_limit_bytes=4 << 20),
        cost_estimate=pl.CostEstimate(flops=1000, bytes_accessed=1000, transcendentals=0),
        name="gate",
    )(face_y, own, near_x, near_z)
    face_y = lax.all_to_all(face_y, "gy", 0, 0, tiled=True)

    field, unit = pl.pallas_call(
        near_kernel,
        out_shape=(f32(LANES, TP), f32(3, HALF, LANES)),
        in_specs=[VMEM] * 8,
        out_specs=[VMEM] * 2,
        scratch_shapes=[
            pltpu.VMEM((EXT_ROWS, TP), jnp.bfloat16), pltpu.VMEM((TP, LANES), jnp.float32),
            pltpu.VMEM((3, CS, LANES), jnp.float32),
        ],
        compiler_params=pltpu.CompilerParams(vmem_limit_bytes=16 << 20),
        cost_estimate=pl.CostEstimate(flops=20_000_000_000, bytes_accessed=1000, transcendentals=0),
        name="near",
    )(tiles, grid, near_x, near_z, far_z, blocks, coords, weights)

    parts = pl.pallas_call(
        merge_kernel,
        out_shape=f32(8, 1, LANES),
        in_specs=[VMEM] * 2 + [ANY],
        out_specs=VMEM,
        compiler_params=pltpu.CompilerParams(vmem_limit_bytes=4 << 20),
        cost_estimate=pl.CostEstimate(flops=10_000, bytes_accessed=60_000, transcendentals=0),
        name="merge",
    )(own, far_x, field)
    parts = lax.all_to_all(parts, ("cx", "gy"), 0, 0, tiled=True)

    near = pl.pallas_call(
        far_kernel,
        out_shape=f32(3, HALF, LANES),
        in_specs=[VMEM] * 6,
        out_specs=VMEM,
        scratch_shapes=[
            pltpu.VMEM((LANES, TP), jnp.float32), pltpu.VMEM((TP, LANES), jnp.float32),
            pltpu.VMEM((3, CS, LANES), jnp.float32),
        ],
        compiler_params=pltpu.CompilerParams(vmem_limit_bytes=16 << 20),
        cost_estimate=pl.CostEstimate(flops=1_000_000_000, bytes_accessed=4_000_000, transcendentals=200_000),
        name="far",
    )(tiles, field, far_x, face_y, blocks, coords)

    forces, virial = pl.pallas_call(
        final_kernel,
        out_shape=(f32(3, HALF, LANES), f32(6, HALF, LANES)),
        in_specs=[VMEM] * 6,
        out_specs=[VMEM] * 2,
        compiler_params=pltpu.CompilerParams(vmem_limit_bytes=8 << 20),
        cost_estimate=pl.CostEstimate(flops=500_000, bytes_accessed=600_000, transcendentals=0),
        name="final",
    )(parts, corner, near, unit, frac, drive)
    return forces.reshape(3, 1, 1, 1, -1), virial.reshape(6, 1, 1, 1, -1)


def solution(mesh):
    wide, high, deep = (mesh.shape[axis] for axis in ("gx", "gy", "gz"))
    split = jax.sharding.Mesh(mesh.devices.reshape(wide // 2, 2, high, deep), ("hx", "cx", "gy", "gz"))
    x = ("hx", "cx")
    placed = (
        P(None, x, "gy", "gz", None),
        P(x, "gy", "gz", None),
        P(x, "gy", "gz", None),
        P(x, "gy", "gz"),
        P(),
        P(),
        P("gz", ("hx", "cx", "gy")),
    )
    return jax.shard_map(
        shards,
        mesh=split,
        in_specs=placed,
        out_specs=(P(None, x, "gy", "gz", None), P(None, x, "gy", "gz", None)),
        check_vma=False,
    )
```

```python
import math

import jax
import jax.numpy as jnp
from jax import lax
from jax.experimental import pallas as pl
from jax.experimental.pallas import tpu as pltpu
from jax.sharding import PartitionSpec as P

TL = 8
TP = 512
CS = 64
TD = 6
CUBES = TD**3
FACE = 48
GRID_ROWS = 256
FAR_ROWS = 40
EXT_ROWS = 512
HALF = CS
LANES = 128


def iota(shape, axis):
    return lax.broadcasted_iota(jnp.int32, shape, axis)


def tile_coords(tile):
    plane = (tile * 10923) >> 16
    tx = (tile * 1821) >> 16
    return tx, plane - tx * TD, tile - plane * TD


def to_clusters(upper, lower):
    both = jnp.concatenate([upper, lower], axis=0).T
    even, odd = both[:HALF], both[HALF:]
    left = iota((HALF, LANES), 1) < HALF
    return (
        jnp.where(left, even, pltpu.roll(odd, HALF, 1)),
        jnp.where(left, pltpu.roll(even, HALF, 1), odd),
    )


def to_atoms(upper, lower):
    left = iota((HALF, LANES), 1) < HALF
    even = jnp.where(left, upper, pltpu.roll(lower, HALF, 1))
    odd = jnp.where(left, pltpu.roll(upper, HALF, 1), lower)
    both = jnp.concatenate([even, odd], axis=0).T
    return both[:HALF], both[HALF:]


def corner_of(places):
    tx, ty, tz = ((place >= TD // 2).astype(jnp.int32) for place in places)
    return (tx * 2 + ty) * 2 + tz


def bump(offset):
    return jnp.exp(-0.5 * offset * offset)


def spread_kernel(
    live_ref, pos_any, charge_any, tile_any, weights_any, blocks_any, top_any,
    grid_ref, coarse_ref, coord_ref, tiles_ref, drive_ref, frac_ref, corner_ref, weights_ref, blocks_ref, top_ref,
    pos_ref, charge_ref, tile_ref, wx_ref, wy_ref, wz_ref, cell_ref, sems,
):
    moves = [
        pltpu.make_async_copy(source, target, sems.at[at])
        for at, (source, target) in enumerate(
            (
                (pos_any, pos_ref), (charge_any, charge_ref), (tile_any, tile_ref),
                (weights_any, weights_ref), (blocks_any, blocks_ref), (top_any, top_ref),
            )
        )
    ]
    for move in moves:
        move.start()
    for move in moves[:3]:
        move.wait()
    cluster = 2 * iota((HALF, LANES), 0) + (iota((HALF, LANES), 1) >> 6)
    charge = charge_ref[...] * (cluster < live_ref[0, 0]).astype(jnp.float32)
    x, y = to_clusters(pos_ref[0], pos_ref[1])
    z, q = to_clusters(pos_ref[2], charge)
    coord_ref[0], coord_ref[1], coord_ref[2] = x, y, z
    for node in range(TL):
        wx_ref[node] = q * bump(x - node)
        wy_ref[node] = bump(y - node)
    nodes = iota((TL, LANES), 0).astype(jnp.float32)
    for atom in range(CS):
        wz_ref[atom] = bump(z[atom : atom + 1] - nodes)

    own = iota((LANES, LANES), 0)
    at = iota((LANES, LANES), 1)
    order = (own == jnp.where(at < HALF, 2 * at, 2 * at - 127)).astype(jnp.bfloat16)
    ids = jnp.broadcast_to(tile_ref[...].astype(jnp.float32), (8, LANES)).astype(jnp.bfloat16)
    tiles = jnp.dot(ids, order, preferred_element_type=jnp.float32)
    tiles_ref[...] = tiles
    tiles = tiles[:1].astype(jnp.int32)

    for half in range(2):

        def step(atom, total, half=half):
            row = pl.ds(atom, 1)
            wz = wz_ref[atom]
            line = [wy_ref[j, row, :] * wz for j in range(TL)]
            new = []
            for i in range(4):
                wx = jnp.broadcast_to(wx_ref[4 * half + i, row, :], (TL, LANES))
                new += [total[8 * i + j] + wx * line[j] for j in range(TL)]
            return tuple(new)

        start = tuple(jnp.zeros((TL, LANES), jnp.float32) for _ in range(32))
        total = lax.fori_loop(0, CS, step, start, unroll=8)
        for slot in range(32):
            cell_ref[pl.ds((32 * half + slot) * TL, TL), :] = total[slot]

    cell = cell_ref[...]
    high = cell.astype(jnp.bfloat16)
    low = (cell - high.astype(jnp.float32)).astype(jnp.bfloat16)
    hot = (iota((GRID_ROWS, LANES), 0) == tiles).astype(jnp.bfloat16)
    fine = lax.dot_general(
        jnp.concatenate([hot, hot], axis=1), jnp.concatenate([high, low], axis=1), (((1,), (1,)), ((), ())),
        preferred_element_type=jnp.float32,
    )
    grid_ref[...] = fine.astype(jnp.bfloat16)

    moves[3].wait()
    moments = jnp.sum(fine * weights_ref[...], axis=1, keepdims=True)
    tx, ty, tz = tile_coords(iota((GRID_ROWS, LANES), 0))
    mine = corner_of((tx, ty, tz)) == (iota((GRID_ROWS, LANES), 1) & 7)
    coarse = jnp.sum(jnp.where(mine, moments, 0.0), axis=0, keepdims=True)
    coarse = coarse * (1.0 / math.sqrt(TP * 27))
    for line in range(coarse_ref.shape[0]):
        coarse_ref[line] = coarse

    own_row = (iota((HALF, LANES), 1) >> 1) == iota((HALF, LANES), 0)
    rows = jnp.where(own_row, tile_ref[...].astype(jnp.float32), 0.0).astype(jnp.bfloat16)
    side = ((iota((LANES, LANES), 0) & 1) == (iota((LANES, LANES), 1) >> 6)).astype(jnp.bfloat16)
    tile = jnp.dot(rows, side, preferred_element_type=jnp.float32).astype(jnp.int32)
    places = tile_coords(tile)
    corner_ref[...] = corner_of(places)
    drive_ref[...] = -charge
    for axis in range(3):
        frac_ref[axis] = (places[axis].astype(jnp.float32) * TL + pos_ref[axis]) * (1.0 / (TL * TD))
    for move in moves[4:]:
        move.wait()


def odd(axis):
    return lax.axis_index("cx" if axis == "gx" else axis) & 1


def face_kernel(grid_ref, near_x_ref, far_x_ref, near_z_ref, far_z_ref, y_any, y_ref, sem):
    row = iota((FACE, GRID_ROWS), 0)
    line = (row * 10923) >> 16
    side_x, side_z = odd("gx"), odd("gz")
    low_y = line * 36 + (row - line * TD)
    def made(ids):
        count = len(ids)
        tile = jnp.where(jnp.concatenate([row] * count, axis=0) < TD * TD, jnp.concatenate(ids, axis=0), -1)
        hot = (iota((count * FACE, GRID_ROWS), 1) == tile).astype(jnp.bfloat16)
        faces = jnp.dot(hot, grid_ref[...], preferred_element_type=jnp.float32).astype(jnp.bfloat16)
        return [faces[at * FACE : (at + 1) * FACE] for at in range(count)]

    low, high = made([low_y, low_y + 30])
    me, count = lax.axis_index("gy"), lax.axis_size("gy")
    for step in range(count):
        y_ref[lax.rem(me + step, count)] = high if step == 1 else low
    move = pltpu.make_async_copy(y_ref, y_any, sem)
    move.start()
    ids = [row + 180 * (1 - side_x), row + 180 * side_x, row * TD + 5 * (1 - side_z), row * TD + 5 * side_z]
    for ref, face in zip((near_x_ref, far_x_ref, near_z_ref, far_z_ref), made(ids), strict=True):
        ref[...] = face
    move.wait()


def coarse_kernel(column_ref, top_ref, face_ref, own_ref, send_ref):
    lines = column_ref.shape[0]
    column = column_ref[...].reshape(lines, LANES)
    column = jnp.concatenate([column] * (lines * 8 // LANES), axis=1)
    shape = column.shape
    column = jnp.sum(jnp.where((iota(shape, 1) >> 3) == iota(shape, 0), column, 0.0), axis=0, keepdims=True)
    partial_value = jnp.sum(top_ref[...] * column, axis=1, keepdims=True)
    rows = partial_value.shape[0]
    lanes = jnp.where((iota((rows, LANES), 1) & 7) == (iota((rows, LANES), 0) & 7), partial_value, 0.0)
    lanes = jnp.sum(lanes.reshape(rows // 8, 8, LANES), axis=1)
    mine = iota((8, LANES), 1) >> 3 == iota((8, LANES), 0)
    lower, upper = (jnp.sum(jnp.where(mine, lanes[at : at + 8], 0.0), axis=0, keepdims=True) for at in (0, 8))
    half = jnp.broadcast_to(lax.axis_index("hx"), (1, LANES)) == 0
    own_ref[...] = jnp.where(half, lower, upper)
    rest = jnp.where(half, upper, lower)
    parts = []
    for _ in range(3):
        parts.append(rest.astype(jnp.bfloat16).astype(jnp.float32))
        rest = rest - parts[-1]
    sums = jnp.concatenate(parts + [jnp.zeros((1, LANES), jnp.float32)], axis=1)
    rows = face_ref[...].astype(jnp.float32)[:FAR_ROWS]
    send_ref[...] = jnp.where(iota((FAR_ROWS, TP), 0) == TD * TD, sums, rows).astype(jnp.bfloat16)


def gate_kernel(*refs):
    pass


def merge_kernel(own_ref, far_ref, field_any, out_ref):
    sums = far_ref[...].astype(jnp.float32)[TD * TD : TD * TD + 1]
    total = own_ref[...] + ((sums[:, :LANES] + sums[:, LANES : 2 * LANES]) + sums[:, 2 * LANES : 3 * LANES])
    for brick in range(8):
        out_ref[brick] = pltpu.roll(total, (LANES - 8 * brick) % LANES, 1) if brick else total


ATOM_ROWS = 16


def gradients(field_ref, wx, wy, wz, x, y, z):
    sums = [None] * 4
    for i in reversed(range(TL)):
        a = b = c = None
        for j in reversed(range(TL)):
            run = mean = None
            for k in reversed(range(TL)):
                term = wz[k] * field_ref[(i * TL + j) * TL + k : (i * TL + j) * TL + k + 1, :]
                run = term if run is None else run + term
                if k:
                    mean = run if mean is None else mean + run
            part = wy[j] * run
            cross = wy[j] * mean
            a = part if a is None else a + part
            c = cross if c is None else c + cross
            if j:
                b = a if b is None else b + a
        for at, value in enumerate((a, b, c)):
            term = wx[i] * value
            sums[at] = term if sums[at] is None else sums[at] + term
        if i:
            sums[3] = sums[0] if sums[3] is None else sums[3] + sums[0]
    total, with_y, with_z, with_x = sums
    return with_x - x * total, with_y - y * total, with_z - z * total


def tile_column(tiles_ref):
    return jnp.broadcast_to(tiles_ref[:1], (LANES, LANES)).T[:, :1].astype(jnp.int32)


def near_kernel(
    tiles_ref, grid_ref, near_x_ref, near_z_ref, far_z_ref, blocks_ref, coord_ref, weights_ref,
    field_ref, unit_ref,
    ext_ref, flat_ref, grad_ref,
):
    ext_ref[0:GRID_ROWS] = grid_ref[...]
    for at, ref in enumerate((near_x_ref, near_z_ref, far_z_ref)):
        ext_ref[GRID_ROWS + at * FACE : GRID_ROWS + (at + 1) * FACE] = ref[...]
    nothing = GRID_ROWS + 3 * FACE
    ext_ref[nothing:] = jnp.zeros((EXT_ROWS - nothing, TP), jnp.bfloat16)

    tile = tile_column(tiles_ref)
    tx, ty, tz = tile_coords(tile)
    row_x, row_z = ty * TD + tz, tx * TD + ty
    base = GRID_ROWS
    edges = (
        ("gx", tx, 36, base + row_x, nothing + 0 * row_x),
        ("gy", ty, TD, CUBES + 0 * row_x, CUBES + 0 * row_x),
        ("gz", tz, 1, base + FACE + row_z, base + 2 * FACE + row_z),
    )
    targets = [tile]
    for axis, place, stride, near, far in edges:
        side = jnp.broadcast_to(odd(axis), near.shape) == 1
        targets.append(jnp.where(place < TD - 1, tile + stride, jnp.where(side, far, near)))
        targets.append(jnp.where(place > 0, tile - stride, jnp.where(side, near, far)))
    field = None
    for at, target in enumerate(targets):
        reach = GRID_ROWS if at in (0, 3, 4) else EXT_ROWS
        hot = (iota((LANES, reach), 1) == target).astype(jnp.bfloat16)
        rows = jnp.dot(hot, ext_ref[:reach], preferred_element_type=jnp.float32).astype(jnp.bfloat16)
        flipped = at > 0 and at % 2 == 0
        term = lax.dot_general(
            rows, blocks_ref[(at + 1) // 2], (((1,), (0 if flipped else 1,)), ((), ())), preferred_element_type=jnp.float32
        )
        field = term if field is None else field + term
    field_ref[...] = field
    for part in range(TP // LANES):
        flat_ref[part * LANES : (part + 1) * LANES, :] = jnp.broadcast_to(
            weights_ref[:, part * LANES : (part + 1) * LANES], (LANES, LANES)
        ).T
    all_gradients(flat_ref, coord_ref, grad_ref)
    unit_ref[0], unit_ref[1] = to_atoms(grad_ref[0], grad_ref[1])
    unit_ref[2], _ = to_atoms(grad_ref[2], grad_ref[2])


def all_gradients(field_ref, coord_ref, grad_ref):
    @pl.loop(0, CS // ATOM_ROWS)
    def _(group):
        rows = pl.ds(pl.multiple_of(group * ATOM_ROWS, ATOM_ROWS), ATOM_ROWS)
        x, y, z = coord_ref[0, rows, :], coord_ref[1, rows, :], coord_ref[2, rows, :]
        wx, wy, wz = ([bump(u - node) for node in range(TL)] for u in (x, y, z))
        for axis, value in enumerate(gradients(field_ref, wx, wy, wz, x, y, z)):
            grad_ref[axis, rows, :] = value


def far_kernel(
    tiles_ref, part_ref, far_x_ref, y_ref, block_ref, coord_ref,
    near_ref,
    sum_ref, field_ref, grad_ref,
):
    tx, ty, tz = tile_coords(tile_column(tiles_ref))

    def picked(face, target):
        hot = (iota((LANES, FACE), 1) == target).astype(jnp.bfloat16)
        return jnp.dot(hot, face, preferred_element_type=jnp.float32).astype(jnp.bfloat16)

    def term(rows, block, up):
        return lax.dot_general(rows, block_ref[block], (((1,), (up,)), ((), ())), preferred_element_type=jnp.float32)

    me, count = lax.axis_index("gy"), lax.axis_size("gy")
    row = tx * TD + tz
    above = picked(y_ref[lax.rem(me + 1, count)], jnp.where(ty == TD - 1, row, -1))
    below = picked(y_ref[lax.rem(me + count - 1, count)], jnp.where(ty == 0, row, -1))
    field = part_ref[...] + term(above, 2, 1) + term(below, 2, 0)
    core = odd("gx")
    rest = jnp.zeros((FACE - FAR_ROWS, TP), jnp.float32)
    face = jnp.concatenate([far_x_ref[...].astype(jnp.float32), rest], axis=0).astype(jnp.bfloat16)
    rows = picked(face, jnp.where(tx == (TD - 1) * core, ty * TD + tz, -1))
    for side in range(2):

        @pl.when(core == side)
        def _(side=side):
            sum_ref[...] = field + term(rows, 1, side)

    for part in range(TP // LANES):
        field_ref[part * LANES : (part + 1) * LANES, :] = sum_ref[:, part * LANES : (part + 1) * LANES].T
    all_gradients(field_ref, coord_ref, grad_ref)
    near_ref[0], near_ref[1] = to_atoms(grad_ref[0], grad_ref[1])
    near_ref[2], _ = to_atoms(grad_ref[2], grad_ref[2])


def final_kernel(parts_ref, corner_ref, near_ref, unit_ref, frac_ref, drive_ref, force_ref, virial_ref):
    coarse = jnp.sum(parts_ref[...].reshape(parts_ref.shape[0], LANES), axis=0, keepdims=True)
    corner = corner_ref[...]
    pot = jnp.zeros((HALF, LANES), jnp.float32)
    for at in range(8):
        pot = jnp.where(corner == at, coarse[:, at : at + 1], pot)
    drive = drive_ref[...]
    forces = [drive * (near_ref[axis] + pot * unit_ref[axis]) for axis in range(3)]
    for axis in range(3):
        force_ref[axis] = forces[axis]
        virial_ref[axis] = frac_ref[axis] * forces[axis]
    virial_ref[3] = frac_ref[0] * forces[1]
    virial_ref[4] = frac_ref[0] * forces[2]
    virial_ref[5] = frac_ref[1] * forces[2]


VMEM = pl.BlockSpec(memory_space=pltpu.VMEM)
SMEM = pl.BlockSpec(memory_space=pltpu.SMEM)
ANY = pl.BlockSpec(memory_space=pl.ANY)
HBM = pl.BlockSpec(memory_space=pltpu.HBM)


def f32(*shape):
    return jax.ShapeDtypeStruct(shape, jnp.float32)


def bf16(*shape):
    return jax.ShapeDtypeStruct(shape, jnp.bfloat16)


def exchanged(value, axis, far):
    count = lax.axis_size(axis)
    return lax.ppermute(value, axis, [(i, (i + (1 if (i + far) % 2 == 0 else -1)) % count) for i in range(count)])


def shards(positions, charges, cluster_tile, live_clusters, kernel_blocks, restrict_weights, top_kernel):
    pos = positions.reshape(3, HALF, LANES)
    charge = charges.reshape(HALF, LANES)
    tile = cluster_tile.reshape(1, LANES)
    live = live_clusters.reshape(1, 1)
    weights = restrict_weights.reshape(1, TP)
    lines = lax.axis_size("gz")

    grid, coarse, coords, tiles, drive, frac, corner, weights, blocks, top = pl.pallas_call(
        spread_kernel,
        out_shape=(
            bf16(GRID_ROWS, TP), f32(lines, 1, LANES), f32(3, CS, LANES), f32(8, LANES), f32(HALF, LANES),
            f32(3, HALF, LANES), jax.ShapeDtypeStruct((HALF, LANES), jnp.int32), f32(1, TP),
            bf16(*kernel_blocks.shape), f32(*top_kernel.shape),
        ),
        in_specs=[SMEM] + [ANY] * 6,
        out_specs=[VMEM] * 10,
        scratch_shapes=[
            pltpu.VMEM((3, HALF, LANES), jnp.float32), pltpu.VMEM((HALF, LANES), jnp.float32),
            pltpu.VMEM((1, LANES), jnp.int32),
            pltpu.VMEM((TL, CS, LANES), jnp.float32), pltpu.VMEM((TL, CS, LANES), jnp.float32),
            pltpu.VMEM((CS, TL, LANES), jnp.float32), pltpu.VMEM((TP, LANES), jnp.float32),
            pltpu.SemaphoreType.DMA((6,)),
        ],
        compiler_params=pltpu.CompilerParams(vmem_limit_bytes=12 << 20),
        cost_estimate=pl.CostEstimate(flops=10_000_000, bytes_accessed=1_000_000, transcendentals=200_000),
        name="spread",
    )(live, *(pltpu.with_memory_space_constraint(a, pltpu.HBM) for a in (pos, charge, tile, weights, kernel_blocks, top_kernel)))
    column = lax.all_to_all(coarse, "gz", 0, 0, tiled=True)

    faces = pl.pallas_call(
        face_kernel,
        out_shape=(bf16(FACE, TP),) * 4 + (pltpu.HBM((lax.axis_size("gy"), FACE, TP), jnp.bfloat16),),
        in_specs=[VMEM],
        out_specs=[VMEM] * 4 + [HBM],
        scratch_shapes=[pltpu.VMEM((lax.axis_size("gy"), FACE, TP), jnp.bfloat16), pltpu.SemaphoreType.DMA],
        compiler_params=pltpu.CompilerParams(vmem_limit_bytes=8 << 20),
        cost_estimate=pl.CostEstimate(flops=80_000_000, bytes_accessed=600_000, transcendentals=0),
        name="faces",
    )(grid)
    near_x, far_x, near_z, far_z, face_y = faces
    far_z, near_z = exchanged(far_z, "gz", 1), exchanged(near_z, "gz", 0)
    near_x = exchanged(near_x, ("hx", "cx"), 0)

    own, far_x = pl.pallas_call(
        coarse_kernel,
        out_shape=(f32(1, LANES), bf16(FAR_ROWS, TP)),
        in_specs=[VMEM] * 3,
        out_specs=[VMEM] * 2,
        compiler_params=pltpu.CompilerParams(vmem_limit_bytes=8 << 20),
        cost_estimate=pl.CostEstimate(flops=70_000, bytes_accessed=200_000, transcendentals=0),
        name="coarse",
    )(column, top, far_x)
    far_x = exchanged(far_x, ("hx", "cx"), 1)
    face_y = pl.pallas_call(
        gate_kernel,
        out_shape=pltpu.HBM(face_y.shape, jnp.bfloat16),
        in_specs=[HBM] + [ANY] * 3,
        out_specs=HBM,
        input_output_aliases={0: 0},
        compiler_params=pltpu.CompilerParams(vmem_limit_bytes=4 << 20),
        cost_estimate=pl.CostEstimate(flops=1000, bytes_accessed=1000, transcendentals=0),
        name="gate",
    )(face_y, own, near_x, near_z)
    face_y = lax.all_to_all(face_y, "gy", 0, 0, tiled=True)

    field, unit = pl.pallas_call(
        near_kernel,
        out_shape=(f32(LANES, TP), f32(3, HALF, LANES)),
        in_specs=[VMEM] * 8,
        out_specs=[VMEM] * 2,
        scratch_shapes=[
            pltpu.VMEM((EXT_ROWS, TP), jnp.bfloat16), pltpu.VMEM((TP, LANES), jnp.float32),
            pltpu.VMEM((3, CS, LANES), jnp.float32),
        ],
        compiler_params=pltpu.CompilerParams(vmem_limit_bytes=16 << 20),
        cost_estimate=pl.CostEstimate(flops=20_000_000_000, bytes_accessed=1000, transcendentals=0),
        name="near",
    )(tiles, grid, near_x, near_z, far_z, blocks, coords, weights)

    parts = pl.pallas_call(
        merge_kernel,
        out_shape=f32(8, 1, LANES),
        in_specs=[VMEM] * 2 + [ANY],
        out_specs=VMEM,
        compiler_params=pltpu.CompilerParams(vmem_limit_bytes=4 << 20),
        cost_estimate=pl.CostEstimate(flops=10_000, bytes_accessed=60_000, transcendentals=0),
        name="merge",
    )(own, far_x, field)
    parts = lax.all_to_all(parts, ("cx", "gy"), 0, 0, tiled=True)

    near = pl.pallas_call(
        far_kernel,
        out_shape=f32(3, HALF, LANES),
        in_specs=[VMEM] * 6,
        out_specs=VMEM,
        scratch_shapes=[
            pltpu.VMEM((LANES, TP), jnp.float32), pltpu.VMEM((TP, LANES), jnp.float32),
            pltpu.VMEM((3, CS, LANES), jnp.float32),
        ],
        compiler_params=pltpu.CompilerParams(vmem_limit_bytes=16 << 20),
        cost_estimate=pl.CostEstimate(flops=1_000_000_000, bytes_accessed=4_000_000, transcendentals=200_000),
        name="far",
    )(tiles, field, far_x, face_y, blocks, coords)

    forces, virial = pl.pallas_call(
        final_kernel,
        out_shape=(f32(3, HALF, LANES), f32(6, HALF, LANES)),
        in_specs=[VMEM] * 6,
        out_specs=[VMEM] * 2,
        compiler_params=pltpu.CompilerParams(vmem_limit_bytes=8 << 20),
        cost_estimate=pl.CostEstimate(flops=500_000, bytes_accessed=600_000, transcendentals=0),
        name="final",
    )(parts, corner, near, unit, frac, drive)
    return forces.reshape(3, 1, 1, 1, -1), virial.reshape(6, 1, 1, 1, -1)


def solution(mesh):
    wide, high, deep = (mesh.shape[axis] for axis in ("gx", "gy", "gz"))
    split = jax.sharding.Mesh(mesh.devices.reshape(wide // 2, 2, high, deep), ("hx", "cx", "gy", "gz"))
    x = ("hx", "cx")
    placed = (
        P(None, x, "gy", "gz", None),
        P(x, "gy", "gz", None),
        P(x, "gy", "gz", None),
        P(x, "gy", "gz"),
        P(),
        P(),
        P("gz", ("hx", "cx", "gy")),
    )
    return jax.shard_map(
        shards,
        mesh=split,
        in_specs=placed,
        out_specs=(P(None, x, "gy", "gz", None), P(None, x, "gy", "gz", None)),
        check_vma=False,
    )
```
